128 devices in a mesh: dp: 16 (over z, y_hi, core), tensor: 8 (over y_lo, x).
Axes of the slice: x: 4, y: 4 (y_hi: 2, y_lo: 2; y = y_hi * 2 + y_lo), z: 4, core: 2. Of those that a mesh axis runs over, the one named last changes fastest.
Arguments:
- streams: bfloat16 [2048, 4, 2048], P('dp'), may hold values from -6 to 6
- placement: int32 [16], replicated, may hold values from 0 to 15, as said below
- w_query: bfloat16 [2048, 2048], P(None, 'tensor')
- w_key: bfloat16 [2048, 2048], P(None, 'tensor')
- w_value: bfloat16 [2048, 2048], P(None, 'tensor'), may hold values from -0.125 to 0.125
- w_output: bfloat16 [2048, 2048], P('tensor'), may hold values from -0.5 to 0.5
- w_gate: bfloat16 [2048, 8192], P(None, 'tensor'), may hold values from -0.125 to 0.125
- w_up: bfloat16 [2048, 8192], P(None, 'tensor'), may hold values from -0.125 to 0.125
- w_down: bfloat16 [8192, 2048], P('tensor'), may hold values from -0.0625 to 0.0625
- mix_dynamic: float32 [2, 2048, 6], replicated, may hold values from -0.125 to 0.125
- mix_static: float32 [2, 4, 6], replicated, may hold values from -0.3 to 1.5, as said below
- cotangent: bfloat16 [2048, 4, 2048], P('dp'), may hold values from -6 to 6
Outputs:
- streams_out: bfloat16 [2048, 4, 2048], P('dp')
- grad_streams: bfloat16 [2048, 4, 2048], P('dp')
- grad_w_query: float32 [2048, 2048], P('dp', 'tensor')
- grad_w_key: float32 [2048, 2048], P('dp', 'tensor')
- grad_w_value: float32 [2048, 2048], P('dp', 'tensor')
- grad_w_output: float32 [2048, 2048], P('tensor', 'dp')
- grad_w_gate: float32 [2048, 8192], P('dp', 'tensor')
- grad_w_up: float32 [2048, 8192], P('dp', 'tensor')
- grad_w_down: float32 [8192, 2048], P('tensor', 'dp')
- grad_mix_dynamic: float32 [2, 2048, 6], P(None, 'dp')
- grad_mix_static: float32 [2, 4, 6], replicated
The draws below stay inside these ranges and needn't reach their ends.
Inputs may be any that keep to these rules, and one draw needn't show every extreme that they name: placement is a permutation: placement[a] is the segment held by index a of dp; the first and the last index of dp always hold prompt spans. `mix_static`: columns 0 and 5 are positive; columns 1 to 4 form a matrix near the identity.
All inputs are finite; a program needn't handle non-finite values.
Results may differ from the reference program's by a relative error of at most 0.018.
Values may be sent and summed in bfloat16 or wider, within the bound.
No kernel may reach another device: no remote copies, remote signals or barrier semaphores. Data moves between devices by JAX's collectives and lax.ppermute only.
A program may use at most 192 MiB of HBM per device.

```python
from functools import partial
import jax
import jax.numpy as jnp
from jax import lax

D = 2048
HEADS = 16
HEAD = 128
FF = 8192
STREAMS = 4
SEG = 128
TOKENS = 2048
N_DP = 16


def draw_placement(key, part):
    key = jax.random.fold_in(key, 11)
    first_key, second_key = jax.random.split(key)
    prompts = N_DP // 2
    inner = (jax.random.permutation(first_key, N_DP - 2) + 1).astype(jnp.int32)
    prompt_devices = jnp.concatenate([jnp.array([0, N_DP - 1], jnp.int32), inner[:prompts - 2]])
    prompt_devices = prompt_devices[jax.random.permutation(second_key, prompts)]
    devices = jnp.concatenate([prompt_devices, inner[prompts - 2:]])
    return jnp.zeros((N_DP,), jnp.int32).at[devices].set(jnp.arange(N_DP, dtype=jnp.int32))


def draw_mix_static(key, part):
    key = jax.random.fold_in(key, 7)
    take_key, mix_key, give_key = jax.random.split(key, 3)
    taking = jax.random.uniform(take_key, (2, STREAMS, 1), jnp.float32, 0.1, 0.5)
    mixing = jnp.eye(STREAMS, dtype=jnp.float32)[None] + jax.random.uniform(mix_key, (2, STREAMS, STREAMS), jnp.float32, -0.3, 0.3)
    giving = jax.random.uniform(give_key, (2, STREAMS, 1), jnp.float32, 0.5, 1.5)
    return jnp.concatenate([taking, mixing, giving], -1)


def projection_entries(key):
    entries = jax.random.truncated_normal(key, -3.0, 3.0, (D, D), jnp.float32)
    return entries * float(D) ** (-0.5)


def draw_w_query(key, part):
    key = jax.random.fold_in(key, 23)
    return projection_entries(key).astype(jnp.bfloat16)


def draw_w_key(key, part):
    key = jax.random.fold_in(key, 29)
    return projection_entries(key).astype(jnp.bfloat16)


def steps_of(key, dims, cuts, least, high):
    gain, own = 1.0, jax.random.fold_in(key, 6)
    for dim, parts in cuts:
        heights = jnp.exp(jax.random.uniform(jax.random.fold_in(own, dim), (parts,), jnp.float32, least / len(cuts), high / len(cuts)))
        gain = gain * jnp.repeat(heights, dims[dim] // parts).reshape([-1 if axis == dim else 1 for axis in range(len(dims))])
    return gain


def noise(stream_key, extent, width, limit, shards=(), kind=jnp.bfloat16):
    values = width * jax.random.normal(stream_key, extent, jnp.float32)
    if shards:
        values = values * steps_of(stream_key, extent, shards, -0.22, 0.18)
    return jnp.clip(values, -limit, limit).astype(kind)


def setup_inputs(seed: int = 0) -> dict:
    streams_of = jax.random.split(jax.random.key(seed), 13)
    return {
        "streams": noise(streams_of[0], (TOKENS, STREAMS, D), 1.0, 6.0, ((0, 16),)),
        "placement": draw_placement(jax.random.fold_in(streams_of[12], 71), 0),
        "w_query": draw_w_query(jax.random.fold_in(streams_of[12], 71), 0),
        "w_key": draw_w_key(jax.random.fold_in(streams_of[12], 71), 0),
        "w_value": noise(streams_of[4], (D, D), D ** -0.5, 0.125, ((1, 8),)),
        "w_output": noise(streams_of[5], (D, D), (D // 16) ** -0.5, 0.5, ((0, 8),)),
        "w_gate": noise(streams_of[6], (D, FF), D ** -0.5, 0.125, ((1, 8),)),
        "w_up": noise(streams_of[7], (D, FF), D ** -0.5, 0.125, ((1, 8),)),
        "w_down": noise(streams_of[8], (FF, D), FF ** -0.5, 0.0625, ((0, 8),)),
        "mix_dynamic": noise(streams_of[9], (2, D, STREAMS + 2), D ** -0.5, 0.125, (), jnp.float32),
        "mix_static": draw_mix_static(jax.random.fold_in(streams_of[12], 71), 0),
        "cotangent": noise(streams_of[11], (TOKENS, STREAMS, D), 1.0, 6.0, ((0, 16),)),
    }


EPS = 1e-05
THETA = 10000.0
HIGH = lax.Precision.HIGHEST

@jax.custom_vjp
def low(v):
    return lax.optimization_barrier(v.astype(jnp.bfloat16)).astype(jnp.float32)

@jax.custom_vjp
def low_back(v):
    return v

def low_keep(v):
    return (low(v), None)

def low_pass(kept, grad):
    return (grad,)

def back_keep(v):
    return (v, None)

def back_low(kept, grad):
    return (low(grad),)
low.defvjp(low_keep, low_pass)
low_back.defvjp(back_keep, back_low)

def layer_norm(inputs):
    center = inputs - lax.optimization_barrier(jnp.mean(inputs, -1, keepdims=True))
    return center * lax.rsqrt(lax.optimization_barrier(jnp.mean(center * center, -1, keepdims=True)) + EPS)

def rotate(inputs, positions, direction):
    half_dim = inputs.shape[-1] // 2
    frequency = THETA ** (-jnp.arange(half_dim, dtype=jnp.float32) / half_dim)
    angles = positions.astype(jnp.float32)[:, None] * frequency[None, :]
    cosine = jnp.cos(angles)[:, None, :]
    sine_part = direction * jnp.sin(angles)[:, None, :]
    front_half = inputs[..., :half_dim]
    back_half = inputs[..., half_dim:]
    return jnp.concatenate([front_half * cosine - back_half * sine_part, front_half * sine_part + back_half * cosine], -1)

def visible(query_segment, query_row, key_segment, key_row, prompts, segment_rows):
    key_prompt = key_segment < prompts
    query_prompt = query_segment < prompts
    earlier = key_segment * segment_rows + key_row <= query_segment * segment_rows + query_row
    same_place = jnp.logical_and(key_segment == query_segment, key_row <= query_row)
    from_prompt = jnp.logical_or(jnp.logical_not(query_prompt), earlier)
    return jnp.where(key_prompt, from_prompt, same_place)

def pre_branch(streams, dynamic, static):
    normed = layer_norm(streams)
    mixing = static[None] + jnp.tanh(jnp.einsum('rkd,dc->rkc', normed, dynamic, precision=HIGH))
    taken = jnp.einsum('rk,rkd->rd', mixing[..., 0], streams, precision=HIGH)
    return (layer_norm(taken), mixing)

def mix_streams(mixing, streams, branch):
    count = streams.shape[1]
    mixed = jnp.einsum('rkj,rkd->rjd', mixing[..., 1:1 + count], streams, precision=HIGH)
    return mixed + mixing[..., 1 + count:2 + count] * branch[:, None, :]

def forward(streams, w_query, w_key, w_value, w_output, w_gate, w_up, w_down, mix_dynamic, mix_static, placement):
    groups = placement.shape[0]
    prompts = groups // 2
    count = streams.shape[0]
    row_ids = jnp.arange(SEG, dtype=jnp.int32)
    segment_of = jnp.repeat(placement, SEG)
    row_of = jnp.tile(row_ids, groups)
    positions = jnp.where(segment_of < prompts, segment_of * SEG + row_of, prompts * SEG + row_of)
    normed_one, mixing_one = pre_branch(streams, mix_dynamic[0], mix_static[0])
    normed_one = low(normed_one)
    queries = low(rotate(low_back(jnp.dot(normed_one, w_query, precision=HIGH)).reshape(count, HEADS, HEAD), positions, 1.0))
    keys_all = low(rotate(low_back(jnp.dot(normed_one, w_key, precision=HIGH)).reshape(count, HEADS, HEAD), positions, 1.0))
    values_all = low(low_back(jnp.dot(normed_one, w_value, precision=HIGH))).reshape(count, HEADS, HEAD)
    score_scale = HEAD ** (-0.5)

    def one_segment(inputs):
        block_queries, block_segment = inputs
        raw_scores = jnp.einsum('qhe,khe->hqk', block_queries, keys_all, precision=HIGH) * score_scale
        allowed = visible(block_segment, row_ids[:, None], segment_of[None, :], row_of[None, :], prompts, SEG)
        scores = jnp.where(allowed[None], low_back(raw_scores), -1e+30)
        row_max = lax.optimization_barrier(jnp.max(scores, -1, keepdims=True))
        exp_terms = jnp.exp(scores - row_max)
        softmax_w = low(exp_terms / lax.optimization_barrier(jnp.sum(exp_terms, -1, keepdims=True)))
        return jnp.einsum('hqk,khe->qhe', softmax_w, values_all, precision=HIGH)
    attended = lax.map(jax.checkpoint(one_segment), (queries.reshape(groups, SEG, HEADS, HEAD), placement))
    attended = low(low_back(attended.reshape(count, D)))
    branch_one = low_back(jnp.dot(attended, w_output, precision=HIGH))
    middle = mix_streams(mixing_one, streams, branch_one)
    normed_two, mixing_two = pre_branch(middle, mix_dynamic[1], mix_static[1])
    normed_two = low(normed_two)
    gate_act = low_back(jnp.dot(normed_two, w_gate, precision=HIGH))
    up_act = low_back(jnp.dot(normed_two, w_up, precision=HIGH))
    hidden = low(jax.nn.silu(gate_act) * up_act)
    branch_two = low_back(jnp.dot(hidden, w_down, precision=HIGH))
    return mix_streams(mixing_two, middle, branch_two)

def reference(streams, placement, w_query, w_key, w_value, w_output, w_gate, w_up, w_down, mix_dynamic, mix_static, cotangent):
    bound = partial(forward, placement=placement)
    result, pull_back = jax.vjp(bound, streams.astype(jnp.float32), w_query.astype(jnp.float32), w_key.astype(jnp.float32), w_value.astype(jnp.float32), w_output.astype(jnp.float32), w_gate.astype(jnp.float32), w_up.astype(jnp.float32), w_down.astype(jnp.float32), mix_dynamic.astype(jnp.float32), mix_static.astype(jnp.float32))
    grads = pull_back(cotangent.astype(jnp.float32))
    return (result.astype(jnp.bfloat16), grads[0].astype(jnp.bfloat16), grads[1], grads[2], grads[3], grads[4], grads[5], grads[6], grads[7], grads[8], grads[9])
```

```python
import functools

import jax
import jax.numpy as jnp
from jax import lax
from jax.experimental import pallas as pl
from jax.experimental.pallas import tpu as pltpu
from jax.sharding import Mesh
from jax.sharding import PartitionSpec as P

HEAD = 128
EPS = 1e-05
THETA = 10000.0
BF = jnp.bfloat16
F32 = jnp.float32
K = 4
DP = ("z", "yh", "core")
TP = ("yl", "x")
VMEM = pl.BlockSpec(memory_space=pltpu.VMEM)
SMEM = pl.BlockSpec(memory_space=pltpu.SMEM)
NT = (((1,), (1,)), ((), ()))
TN = (((0,), (0,)), ((), ()))
NN = (((1,), (0,)), ((), ()))


def dot(a, b, dims=NN):
    return lax.dot_general(a, b, dims, preferred_element_type=F32)


def lmean(v):
    return jnp.mean(v, -1, keepdims=True)


def lsum(v):
    return jnp.sum(v, -1, keepdims=True)


def norm_parts(v):
    ctr = v - lmean(v)
    rstd = lax.rsqrt(lmean(ctr * ctr) + EPS)
    return ctr * rstd, rstd


def norm_back(g, xhat, rstd):
    return rstd * (g - lmean(g) - xhat * lmean(g * xhat))


def three(v):
    hi = v.astype(BF)
    rest = v - hi.astype(F32)
    mid = rest.astype(BF)
    low = (rest - mid.astype(F32)).astype(BF)
    return hi, mid, low


def lanes(rows, pairs, start=None):
    lane = lax.broadcasted_iota(jnp.int32, (rows, 128), 1)
    out = jnp.zeros((rows, 128), F32) if start is None else start
    for at, v in pairs:
        out = jnp.where(lane == at, v, out)
    return out


def fold_parts(z):
    return z + pltpu.roll(z, 120, 1) + pltpu.roll(z, 112, 1)


def turn(v, cos, sin):
    return v * cos + pltpu.roll(v, 64, 1) * sin


def params(limit, **kw):
    return pltpu.CompilerParams(vmem_limit_bytes=limit * 2**20, **kw)


def first_kernel(s_ref, mp_ref, st_ref, cs_ref, cos_ref, sin_ref, wq_ref, wk_ref, wv_ref,
                 n_ref, c_ref, q_ref, kv_ref, z_ref):
    rows = s_ref.shape[1]
    width = s_ref.shape[2]
    z_ref[...] = dot(s_ref[...].reshape(K * rows, width), mp_ref[...], NT)

    def body(i, carry):
        r = pl.multiple_of(i * 16, 16)
        taken = None
        for k in range(K):
            z = z_ref[pl.ds(pl.multiple_of(k * rows + r, 16), 16), :]
            s = s_ref[k, pl.ds(r, 16), :].astype(F32)
            mean = z[:, 24:25] * (1.0 / width)
            ctr = s - mean
            rstd = lax.rsqrt(lmean(ctr * ctr) + EPS)
            c = st_ref[k : k + 1, :] + jnp.tanh(rstd * (fold_parts(z) - mean * cs_ref[...]))
            c_ref[k, pl.ds(r, 16), :] = lanes(16, ((8, mean), (9, rstd)), c)
            part = c[:, 0:1] * s
            taken = part if taken is None else taken + part
        n_ref[pl.ds(r, 16), :] = norm_parts(taken)[0].astype(BF)
        return carry

    lax.fori_loop(0, rows // 16, body, 0)
    normed = n_ref[...]
    cos, sin = cos_ref[...], sin_ref[...]
    q = dot(normed, wq_ref[...])
    k = dot(normed, wk_ref[...])
    heads = q.shape[1] // HEAD
    for h in range(heads):
        cut = slice(h * HEAD, (h + 1) * HEAD)
        q_ref[:, cut] = turn(q[:, cut], cos, sin).astype(BF)
        kv_ref[:, cut] = turn(k[:, cut], cos, sin).astype(BF)
    kv_ref[:, heads * HEAD :] = dot(normed, wv_ref[...]).astype(BF)


def first(s4, mp, st, cs, cos, sin, wq, wk, wv):
    _, rows, width = s4.shape
    cols = wq.shape[1]
    return pl.pallas_call(
        first_kernel,
        out_shape=(
            jax.ShapeDtypeStruct((rows, width), BF),
            jax.ShapeDtypeStruct((K, rows, 128), F32),
            jax.ShapeDtypeStruct((rows, cols), BF),
            jax.ShapeDtypeStruct((rows, 2 * cols), BF),
        ),
        in_specs=[VMEM] * 9,
        out_specs=[VMEM] * 4,
        scratch_shapes=[pltpu.VMEM((K * rows, 128), F32)],
        compiler_params=params(32),
        name="first",
    )(s4, mp, st, cs, cos, sin, wq, wk, wv)


def own_blocks(info_ref, place_ref, q_own_kv, same_ref, other_ref):
    me, core = info_ref[0], info_ref[1]
    own = place_ref[me]
    prompts = place_ref.shape[0] // 2
    is_cont = own >= prompts
    blocks = []
    for s in range(prompts):
        d = info_ref[4 + s]
        same = (d % 2) == core
        g = d // 2
        block = jnp.where(same, same_ref[g], other_ref[g])
        reach = jnp.where(is_cont | (s < own), 4096, jnp.where(s == own, 0, -4096))
        blocks.append((block, reach))
    blocks.append((q_own_kv[...], jnp.where(is_cont, 0, -4096)))
    return blocks


def key_after_query(keys, queries):
    return lax.broadcasted_iota(jnp.int32, (keys, queries), 0) - lax.broadcasted_iota(
        jnp.int32, (keys, queries), 1
    )


def attend_kernel(info_ref, place_ref, q_ref, kv_ref, same_ref, other_ref, wo_ref, scale,
                  at_ref, ql_ref, part_ref):
    rows, cols = q_ref.shape
    heads = cols // HEAD
    blocks = own_blocks(info_ref, place_ref, kv_ref, same_ref, other_ref)
    lag = key_after_query(rows, rows)
    logs = []
    for h in range(heads):
        cut = slice(h * HEAD, (h + 1) * HEAD)
        vcut = slice(cols + h * HEAD, cols + (h + 1) * HEAD)
        q = q_ref[:, cut]
        scores = [
            jnp.where(lag <= reach, dot(b[:, cut], q, NT) * scale, -1e30) for b, reach in blocks
        ]
        top = functools.reduce(jnp.maximum, [jnp.max(s, 0, keepdims=True) for s in scores])
        terms = [jnp.exp(s - top) for s in scores]
        total = functools.reduce(jnp.add, [jnp.sum(e, 0, keepdims=True) for e in terms])
        inv = 1.0 / total
        out = None
        for e, (b, _) in zip(terms, blocks):
            o = dot((e * inv).astype(BF), b[:, vcut], TN)
            out = o if out is None else out + o
        at_ref[:, cut] = out.astype(BF)
        logs.append(top + jnp.log(total))
    ql_ref[0:rows, :] = q_ref[...]
    ql_ref[rows:, :] = vector_rows(logs)
    part_ref[...] = dot(at_ref[...], wo_ref[...]).astype(BF)


def vector_rows(vectors):
    row = lax.broadcasted_iota(jnp.int32, (16, vectors[0].shape[1]), 0)
    out = []
    for v in vectors:
        a, b, c = three(v)
        a, b, c = a.astype(F32), b.astype(F32), c.astype(F32)
        out.append(jnp.where(row == 0, a, jnp.where(row == 1, b, jnp.where(row == 2, c, 0.0))))
    return jnp.concatenate(out, 1).astype(BF)


def vector_of(rows16):
    v = rows16.astype(F32)
    return v[0:1] + v[1:2] + v[2:3]


def attend(info, place, q, kv, same, other, wo, scale):
    rows, cols = q.shape
    width = wo.shape[1]

    def body(info_ref, place_ref, *refs):
        attend_kernel(info_ref, place_ref, *refs[:5], scale, *refs[5:])

    return pl.pallas_call(
        body,
        out_shape=(
            jax.ShapeDtypeStruct((rows, cols), BF),
            jax.ShapeDtypeStruct((rows + 16, cols), BF),
            jax.ShapeDtypeStruct((rows, width), BF),
        ),
        in_specs=[SMEM, SMEM] + [VMEM] * 5,
        out_specs=[VMEM] * 3,
        compiler_params=params(32),
        name="attend",
    )(info, place, q, kv, same, other, wo)


def middle_kernel(t_ref, parts_ref, s_ref, c_ref, mp_ref, st_ref, s1_ref, b1_ref, c2_ref, pay_ref,
                  split_ref):
    b1 = jnp.sum(parts_ref[...].astype(F32), 0)
    b1_ref[...] = b1
    rows, width = b1.shape
    s0 = [s_ref[k].astype(F32) for k in range(K)]
    c1 = [c_ref[k] for k in range(K)]
    stats = []
    for j in range(K):
        v = c1[j][:, 5:6] * b1
        for k in range(K):
            v = v + c1[k][:, 1 + j : 2 + j] * s0[k]
        s1_ref[j] = v
        mean = lmean(v)
        ctr = v - mean
        stats.append((mean, lax.rsqrt(lmean(ctr * ctr) + EPS)))
        hi = ctr.astype(BF)
        split_ref[j * rows : (j + 1) * rows, :] = hi
        split_ref[(K + j) * rows : (K + j + 1) * rows, :] = (ctr - hi.astype(F32)).astype(BF)
    z = dot(split_ref[...], mp_ref[...], NT)
    taken, gives = None, []
    for j in range(K):
        mean, rstd = stats[j]
        zj = z[j * rows : (j + 1) * rows] + z[(K + j) * rows : (K + j + 1) * rows]
        c = st_ref[j : j + 1, :] + jnp.tanh(rstd * fold_parts(zj))
        c2_ref[j] = lanes(rows, ((8, mean), (9, rstd)), c)
        part = c[:, 0:1] * s1_ref[j]
        taken = part if taken is None else taken + part
        a, b, d = three(c[:, 5:6])
        gives += [(j, a.astype(F32)), (4 + j, b.astype(F32)), (8 + j, d.astype(F32))]
    pay_ref[:, 0:width] = norm_parts(taken)[0].astype(BF)
    pay_ref[:, width:] = lanes(rows, gives).astype(BF)


def token_block(shape):
    n = len(shape)
    return pl.BlockSpec(shape, lambda i, t: (0,) * (n - 2) + (t[0], 0))


def whole_block(shape):
    n = len(shape)
    return pl.BlockSpec(shape, lambda i, t: (0,) * n)


def middle(t, parts, s4, c1, mp, st):
    _, rows, width = parts.shape
    return pl.pallas_call(
        middle_kernel,
        grid_spec=pltpu.PrefetchScalarGridSpec(
            num_scalar_prefetch=1,
            grid=(1,),
            in_specs=[
                whole_block(parts.shape),
                token_block((K, rows, width)),
                token_block((K, rows, 128)),
                whole_block(mp.shape),
                whole_block(st.shape),
            ],
            out_specs=[
                whole_block((K, rows, width)),
                whole_block((rows, width)),
                whole_block((K, rows, 128)),
                whole_block((rows, width + 128)),
            ],
            scratch_shapes=[pltpu.VMEM((2 * K * rows, width), BF)],
        ),
        out_shape=(
            jax.ShapeDtypeStruct((K, rows, width), F32),
            jax.ShapeDtypeStruct((rows, width), F32),
            jax.ShapeDtypeStruct((K, rows, 128), F32),
            jax.ShapeDtypeStruct((rows, width + 128), BF),
        ),
        compiler_params=params(32),
        name="middle",
    )(t, parts, s4, c1, mp, st)


def feed_kernel(pay_ref, cot_ref, wg_ref, wu_ref, wd_ref, gb_ref, acts_ref, out_ref, b_ref, l_ref):
    step, steps = pl.program_id(0), pl.num_programs(0)
    rows, width = gb_ref.shape

    @pl.when(step == 0)
    def _():
        def body(i, carry):
            r = pl.multiple_of(i * 16, 16)
            give = pay_ref[pl.ds(r, 16), width:].astype(F32)
            total = None
            for j in range(K):
                c = give[:, j : j + 1] + give[:, 4 + j : 5 + j] + give[:, 8 + j : 9 + j]
                part = c * cot_ref[j, pl.ds(r, 16), :].astype(F32)
                total = part if total is None else total + part
            gb_ref[pl.ds(r, 16), :] = total.astype(BF)
            return carry

        lax.fori_loop(0, rows // 16, body, 0)
        b_ref[...] = jnp.zeros_like(b_ref)
        l_ref[...] = jnp.zeros_like(l_ref)

    normed = pay_ref[:, 0:width]
    gate = dot(normed, wg_ref[...])
    up = dot(normed, wu_ref[...])
    sig = 1.0 / (1.0 + jnp.exp(-gate))
    silu = gate * sig
    hidden = (silu * up).astype(BF)
    grad = dot(gb_ref[...], wd_ref[...], NT)
    grad_gate = (grad * up * (sig * (1.0 + gate * (1.0 - sig)))).astype(BF)
    grad_up = (grad * silu).astype(BF)
    acts_ref[0] = grad_gate
    acts_ref[1] = grad_up
    acts_ref[2] = hidden
    b_ref[...] += dot(hidden, wd_ref[...])
    l_ref[...] += dot(grad_gate, wg_ref[...], NT) + dot(grad_up, wu_ref[...], NT)

    @pl.when(step == steps - 1)
    def _():
        out_ref[:, 0:width] = b_ref[...].astype(BF)
        out_ref[:, width:] = l_ref[...].astype(BF)


def feed(pay, cot4, wg, wu, wd):
    _, rows, width = cot4.shape
    hidden = wg.shape[1]
    tile = 256
    return pl.pallas_call(
        feed_kernel,
        grid=(hidden // tile,),
        in_specs=[
            pl.BlockSpec(pay.shape, lambda f: (0, 0)),
            pl.BlockSpec(cot4.shape, lambda f: (0, 0, 0)),
            pl.BlockSpec((width, tile), lambda f: (0, f)),
            pl.BlockSpec((width, tile), lambda f: (0, f)),
            pl.BlockSpec((tile, width), lambda f: (f, 0)),
        ],
        out_specs=[
            pl.BlockSpec((rows, width), lambda f: (0, 0)),
            pl.BlockSpec((3, rows, tile), lambda f: (0, 0, f)),
            pl.BlockSpec((rows, 2 * width), lambda f: (0, 0)),
        ],
        out_shape=(
            jax.ShapeDtypeStruct((rows, width), BF),
            jax.ShapeDtypeStruct((3, rows, hidden), BF),
            jax.ShapeDtypeStruct((rows, 2 * width), BF),
        ),
        scratch_shapes=[pltpu.VMEM((rows, width), F32), pltpu.VMEM((rows, width), F32)],
        compiler_params=params(40),
        name="feed",
    )(pay, cot4, wg, wu, wd)


def coef_back(grads, coefs, st_ref, m_ref, xhats, dm_ref, ds_ref, at, columns):
    rows = xhats[0].shape[0]
    dzs, statics = [], []
    for k in range(K):
        g = lanes(rows, grads[k].items())
        th = coefs[k] - st_ref[k : k + 1, :]
        dzs.append(g * (1.0 - th * th))
        statics.append(jnp.sum(g, 0, keepdims=True))
    ds_ref[at] = jnp.concatenate(statics + [jnp.zeros((8 - K, 128), F32)], 0)
    for c in range(8):
        if c in columns:
            v = None
            for k in range(K):
                part = dzs[k][:, c : c + 1] * xhats[k]
                v = part if v is None else v + part
            dm_ref[at, c : c + 1, :] = jnp.sum(v, 0, keepdims=True)
        else:
            dm_ref[at, c : c + 1, :] = jnp.zeros((1, xhats[0].shape[1]), F32)
    out = []
    for k in range(K):
        v = None
        for c in columns:
            part = dzs[k][:, c : c + 1] * m_ref[c : c + 1, :]
            v = part if v is None else v + part
        out.append(v)
    return out


def turn_kernel(t_ref, parts_ref, s1_ref, c2_ref, cot_ref, s_ref, c1_ref, b1_ref, m_ref, st1_ref,
                st2_ref, s2_ref, gb1_ref, base_ref, dm_ref, ds_ref):
    rows, width = b1_ref.shape
    both = jnp.sum(parts_ref[...].astype(F32), 0)
    b2, gn = both[:, 0:width], both[:, width:]
    s1 = [s1_ref[k] for k in range(K)]
    c2 = [c2_ref[k] for k in range(K)]
    g2 = [cot_ref[k].astype(F32) for k in range(K)]
    grads = [dict() for _ in range(K)]
    taken = None
    for j in range(K):
        v = c2[j][:, 5:6] * b2
        for k in range(K):
            v = v + c2[k][:, 1 + j : 2 + j] * s1[k]
        s2_ref[j] = v.astype(BF)
        grads[j][5] = lsum(g2[j] * b2)
        for k in range(K):
            grads[k][1 + j] = lsum(g2[j] * s1[k])
        part = c2[j][:, 0:1] * s1[j]
        taken = part if taken is None else taken + part
    normed, rstd = norm_parts(taken)
    gt = norm_back(gn, normed, rstd)
    for k in range(K):
        grads[k][0] = lsum(gt * s1[k])
    xhats = [(s1[k] - c2[k][:, 8:9]) * c2[k][:, 9:10] for k in range(K)]
    gx = coef_back(grads, c2, st2_ref, m_ref.at[1], xhats, dm_ref, ds_ref, 1, range(6))
    g1 = []
    for k in range(K):
        v = c2[k][:, 0:1] * gt + norm_back(gx[k], xhats[k], c2[k][:, 9:10])
        for j in range(K):
            v = v + c2[k][:, 1 + j : 2 + j] * g2[j]
        g1.append(v)
    c1 = [c1_ref[k] for k in range(K)]
    b1 = b1_ref[...]
    s0 = [s_ref[k].astype(F32) for k in range(K)]
    gb1 = None
    grads = [dict() for _ in range(K)]
    for j in range(K):
        part = c1[j][:, 5:6] * g1[j]
        gb1 = part if gb1 is None else gb1 + part
        grads[j][5] = lsum(g1[j] * b1)
        for k in range(K):
            grads[k][1 + j] = lsum(g1[j] * s0[k])
    gb1_ref[...] = gb1.astype(BF)
    xhats = [(s0[k] - c1[k][:, 8:9]) * c1[k][:, 9:10] for k in range(K)]
    gx = coef_back(grads, c1, st1_ref, m_ref.at[0], xhats, dm_ref, ds_ref, 0, range(1, 6))
    for k in range(K):
        v = norm_back(gx[k], xhats[k], c1[k][:, 9:10])
        for j in range(K):
            v = v + c1[k][:, 1 + j : 2 + j] * g1[j]
        base_ref[k] = v


def turn_back(t, parts, s1, c2, cot4, s4, c1, b1, mt, st1, st2):
    rows, width = b1.shape
    tok = token_block((K, rows, width))
    return pl.pallas_call(
        turn_kernel,
        grid_spec=pltpu.PrefetchScalarGridSpec(
            num_scalar_prefetch=1,
            grid=(1,),
            in_specs=[
                whole_block(parts.shape),
                whole_block(s1.shape),
                whole_block(c2.shape),
                tok,
                tok,
                token_block((K, rows, 128)),
                whole_block(b1.shape),
                whole_block(mt.shape),
                whole_block(st1.shape),
                whole_block(st2.shape),
            ],
            out_specs=[
                whole_block((K, rows, width)),
                whole_block((rows, width)),
                whole_block((K, rows, width)),
                whole_block((2, 8, width)),
                whole_block((2, 8, 128)),
            ],
        ),
        out_shape=(
            jax.ShapeDtypeStruct((K, rows, width), BF),
            jax.ShapeDtypeStruct((rows, width), BF),
            jax.ShapeDtypeStruct((K, rows, width), F32),
            jax.ShapeDtypeStruct((2, 8, width), F32),
            jax.ShapeDtypeStruct((2, 8, 128), F32),
        ),
        compiler_params=params(32),
        name="turn",
    )(t, parts, s1, c2, cot4, s4, c1, b1, mt, st1, st2)


def query_kernel(info_ref, place_ref, gb_ref, wo_ref, q_ref, kv_ref, ql_ref, same_ref, other_ref,
                 cos_ref, sin_ref, scale, do_ref, gq_ref):
    rows, cols = q_ref.shape
    heads = cols // HEAD
    grad = dot(gb_ref[...], wo_ref[...], NT).astype(BF)
    do_ref[0:rows, :] = grad
    blocks = own_blocks(info_ref, place_ref, kv_ref, same_ref, other_ref)
    lag = key_after_query(rows, rows)
    inners = []
    for h in range(heads):
        cut = slice(h * HEAD, (h + 1) * HEAD)
        vcut = slice(cols + h * HEAD, cols + (h + 1) * HEAD)
        q, do = q_ref[:, cut], grad[:, cut]
        log = vector_of(ql_ref[rows:, cut])
        probs, gps, inner = [], [], None
        for b, reach in blocks:
            s = jnp.where(lag <= reach, dot(b[:, cut], q, NT) * scale, -1e30)
            p = jnp.exp(s - log)
            gp = dot(b[:, vcut], do, NT)
            part = jnp.sum(p * gp, 0, keepdims=True)
            inner = part if inner is None else inner + part
            probs.append(p)
            gps.append(gp)
        gq = None
        for p, gp, (b, _) in zip(probs, gps, blocks):
            part = dot((p * (gp - inner)).astype(BF), b[:, cut], TN)
            gq = part if gq is None else gq + part
        gq_ref[:, cut] = turn(gq * scale, cos_ref[...], -sin_ref[...]).astype(BF)
        inners.append(inner)
    do_ref[rows:, :] = vector_rows(inners)


def query_back(info, place, gb1, wo, q, kv, ql, same, other, cos, sin, scale):
    rows, cols = q.shape

    def body(info_ref, place_ref, *refs):
        query_kernel(info_ref, place_ref, *refs[:9], scale, *refs[9:])

    return pl.pallas_call(
        body,
        out_shape=(
            jax.ShapeDtypeStruct((rows + 16, cols), BF),
            jax.ShapeDtypeStruct((rows, cols), BF),
        ),
        in_specs=[SMEM, SMEM] + [VMEM] * 9,
        out_specs=[VMEM] * 2,
        compiler_params=params(32),
        name="query_back",
    )(info, place, gb1, wo, q, kv, ql, same, other, cos, sin)


def key_kernel(info_ref, place_ref, kv_ref, qall_ref, same_ref, other_ref, gq_ref, cos_ref, sin_ref,
               wq_ref, wk_ref, wv_ref, scale, gkv_ref, part_ref):
    rows, cols = gq_ref.shape
    heads = cols // HEAD
    me, core = info_ref[0], info_ref[1]
    own = place_ref[me]
    count = place_ref.shape[0]
    prompts = count // 2
    groups = [(g, rel) for g in range(count // 2) for rel in range(2)]
    reach = []
    for g, rel in groups:
        seg = place_ref[2 * g + (core + rel) % 2]
        full = (own < prompts) & (seg > own)
        value = jnp.where(full, 4096, jnp.where(seg == own, 0, -4096))
        reach.append(jnp.zeros((1, rows), jnp.int32) + value)
    reach = jnp.concatenate(reach, 1)
    lag = key_after_query(rows, rows)
    seen = jnp.concatenate([lag] * count, 1) <= reach
    for h in range(heads):
        cut = slice(h * HEAD, (h + 1) * HEAD)
        vcut = slice(cols + h * HEAD, cols + (h + 1) * HEAD)
        k, v = kv_ref[:, cut], kv_ref[:, vcut]
        qs, dos, logs, inners = [], [], [], []
        for g, rel in groups:
            d = 2 * g + (core + rel) % 2
            qs.append(qall_ref[d, 0:rows, cut])
            logs.append(vector_of(qall_ref[d, rows:, cut]))
            src = same_ref if rel == 0 else other_ref
            dos.append(src[g, 0:rows, cut])
            inners.append(vector_of(src[g, rows:, cut]))
        qs, dos = jnp.concatenate(qs, 0), jnp.concatenate(dos, 0)
        logs, inners = jnp.concatenate(logs, 1), jnp.concatenate(inners, 1)
        s = jnp.where(seen, dot(k, qs, NT) * scale, -1e30)
        p = jnp.exp(s - logs)
        gp = dot(v, dos, NT)
        ds = (p * (gp - inners)).astype(BF)
        gv = dot(p.astype(BF), dos)
        gk = dot(ds, qs) * scale
        gkv_ref[:, cut] = turn(gk, cos_ref[...], -sin_ref[...]).astype(BF)
        gkv_ref[:, vcut] = gv.astype(BF)
    part = dot(gq_ref[...], wq_ref[...], NT)
    part += dot(gkv_ref[:, 0:cols], wk_ref[...], NT)
    part += dot(gkv_ref[:, cols:], wv_ref[...], NT)
    part_ref[...] = part.astype(BF)


def key_back(info, place, kv, qall, same, other, gq, cos, sin, wq, wk, wv, scale):
    rows, cols = gq.shape
    width = wq.shape[0]

    def body(info_ref, place_ref, *refs):
        key_kernel(info_ref, place_ref, *refs[:10], scale, *refs[10:])

    return pl.pallas_call(
        body,
        out_shape=(
            jax.ShapeDtypeStruct((rows, 2 * cols), BF),
            jax.ShapeDtypeStruct((rows, width), BF),
        ),
        in_specs=[SMEM, SMEM] + [VMEM] * 10,
        out_specs=[VMEM] * 2,
        compiler_params=params(40),
        name="key_back",
    )(info, place, kv, qall, same, other, gq, cos, sin, wq, wk, wv)


def last_kernel(t_ref, parts_ref, base_ref, s_ref, c_ref, m_ref, st_ref, dmin_ref, dsin_ref,
                out_ref, dm_ref, ds_ref):
    gn = jnp.sum(parts_ref[...].astype(F32), 0)
    rows, width = gn.shape
    s0 = [s_ref[k].astype(F32) for k in range(K)]
    c1 = [c_ref[k] for k in range(K)]
    taken = None
    for k in range(K):
        part = c1[k][:, 0:1] * s0[k]
        taken = part if taken is None else taken + part
    normed, rstd = norm_parts(taken)
    gt = norm_back(gn, normed, rstd)
    dm_ref[...] = dmin_ref[...]
    ds_ref[...] = dsin_ref[...]
    total = None
    for k in range(K):
        g = lsum(gt * s0[k])
        th = c1[k][:, 0:1] - st_ref[k : k + 1, 0:1]
        dz = g * (1.0 - th * th)
        xhat = (s0[k] - c1[k][:, 8:9]) * c1[k][:, 9:10]
        part = dz * xhat
        total = part if total is None else total + part
        lane = lax.broadcasted_iota(jnp.int32, (1, 128), 1)
        ds_ref[0, k : k + 1, :] += jnp.where(lane == 0, jnp.sum(g, 0, keepdims=True), 0.0)
        v = base_ref[k] + c1[k][:, 0:1] * gt
        out_ref[k] = (v + norm_back(dz * m_ref[0, 0:1, :], xhat, c1[k][:, 9:10])).astype(BF)
    dm_ref[0, 0:1, :] = jnp.sum(total, 0, keepdims=True)


def last(t, parts, base, s4, c1, mt, st, dm, ds):
    _, rows, width = parts.shape
    return pl.pallas_call(
        last_kernel,
        grid_spec=pltpu.PrefetchScalarGridSpec(
            num_scalar_prefetch=1,
            grid=(1,),
            in_specs=[
                whole_block(parts.shape),
                whole_block(base.shape),
                token_block((K, rows, width)),
                token_block((K, rows, 128)),
                whole_block(mt.shape),
                whole_block(st.shape),
                whole_block(dm.shape),
                whole_block(ds.shape),
            ],
            out_specs=[
                whole_block((K, rows, width)),
                whole_block(dm.shape),
                whole_block(ds.shape),
            ],
        ),
        out_shape=(
            jax.ShapeDtypeStruct((K, rows, width), BF),
            jax.ShapeDtypeStruct(dm.shape, F32),
            jax.ShapeDtypeStruct(ds.shape, F32),
        ),
        compiler_params=params(32),
        name="last",
    )(t, parts, base, s4, c1, mt, st, dm, ds)


def to_all(shard, axes):
    copies = jnp.broadcast_to(shard, (lax.axis_size(axes), *shard.shape))
    return lax.all_to_all(copies, axes, 0, 0, tiled=True)


def scatter_parts(partial, axes):
    n = lax.axis_size(axes)
    blocks = partial.reshape(n, partial.shape[0] // n, partial.shape[1])
    return lax.all_to_all(blocks, axes, 0, 0, tiled=True)


def swap(v, axis):
    return lax.ppermute(v, axis, [(0, 1), (1, 0)])


def over_chips(shard):
    same = to_all(shard, ("z", "yh"))
    return same, swap(same, "core")


def column_blocks(v):
    n = lax.axis_size("z")
    me = lax.axis_index("z")
    rows, width = v.shape
    cols = width // n
    out = jnp.zeros((n, rows, cols), v.dtype)
    for s in range(n):
        piece = lax.dynamic_slice(v, (0, lax.rem(me + s, n) * cols), (rows, cols))
        if s:
            piece = lax.ppermute(piece, "z", [(i, (i + s) % n) for i in range(n)])
        out = lax.dynamic_update_slice(out, piece[None], (lax.rem(me - s + n, n), 0, 0))
    return out


def sum_rows(partial):
    core, yh = lax.axis_index("core"), lax.axis_index("yh")
    rows = partial.shape[0] // 4
    v = partial.reshape(2, 2, rows, partial.shape[1])
    keep = lax.dynamic_index_in_dim(v, core, 1, keepdims=False)
    give = lax.dynamic_index_in_dim(v, 1 - core, 1, keepdims=False)
    v = keep + swap(give.astype(BF), "core").astype(F32)
    keep = lax.dynamic_index_in_dim(v, yh, 0, keepdims=False)
    give = lax.dynamic_index_in_dim(v, 1 - yh, 0, keepdims=False)
    return keep + swap(give.astype(BF), "yh").astype(F32)


def grad_product(left, right):
    return jnp.einsum("ztd,ztf->df", left, right, preferred_element_type=F32)


def per_device(streams, placement, w_query, w_key, w_value, w_output, w_gate, w_up, w_down,
               mix_dynamic, mix_static, cotangent):
    rows = streams.shape[0]
    width = streams.shape[2]
    groups = placement.shape[0]
    prompts = groups // 2
    cols = w_query.shape[1]
    scale = HEAD ** (-0.5)
    me = lax.axis_index(DP)
    core = lax.axis_index("core")
    t = lax.axis_index(TP).astype(jnp.int32)[None]
    own = placement[me]
    holders = jnp.sum(
        jnp.where(
            placement[None, :] == jnp.arange(prompts, dtype=jnp.int32)[:, None],
            jnp.arange(groups, dtype=jnp.int32)[None, :],
            0,
        ),
        1,
    )
    info = jnp.concatenate(
        [jnp.stack([me, core, me, me]).astype(jnp.int32), holders.astype(jnp.int32)]
    )
    half = HEAD // 2
    frequency = THETA ** (-jnp.arange(half, dtype=F32) / half)
    start = jnp.minimum(own, prompts) * rows
    angles = (start + jnp.arange(rows, dtype=jnp.int32)).astype(F32)[:, None] * frequency[None, :]
    cos, sin = jnp.cos(angles), jnp.sin(angles)
    cos = jnp.concatenate([cos, cos], 1)
    sin = jnp.concatenate([-sin, sin], 1)

    s4 = jnp.transpose(streams, (1, 0, 2))
    cot4 = jnp.transpose(cotangent, (1, 0, 2))
    mt = jnp.transpose(mix_dynamic, (0, 2, 1))
    zero2 = jnp.zeros((2, 2, width), F32)
    hi = lax.reduce_precision(mt, 8, 7)
    mid = lax.reduce_precision(mt - hi, 8, 7)
    low = mt - hi - mid
    ones = jnp.ones((2, 1, width), F32)
    mparts = jnp.concatenate(
        [hi, zero2, mid, zero2, low, zero2, ones, jnp.zeros((2, 103, width), F32)], 1
    ).astype(BF)
    mt8 = jnp.concatenate([mt, zero2], 1)
    csum = jnp.pad(jnp.sum(mt, 2), ((0, 0), (0, 122)))[:, None, :]
    st = jnp.pad(mix_static, ((0, 0), (0, 4), (0, 122)))

    normed_one, c1, q, kv = first(
        s4, mparts[0], st[0], csum[0], cos, sin, w_query, w_key, w_value
    )
    kv_same, kv_other = over_chips(kv)
    attended, ql, part_one = attend(info, placement, q, kv, kv_same, kv_other, w_output, scale)
    qall = lax.all_gather(ql, DP, axis=0)
    s1, b1, c2, pay = middle(t, scatter_parts(part_one, TP), s4, c1, mparts[1], st[1])
    pay = to_all(pay, TP).reshape(rows, width + 128)
    gb2, acts, part_two = feed(pay, cot4, w_gate, w_up, w_down)
    acts_z = lax.all_gather(acts, "z", axis=0)
    s2, gb1, base, dm, ds = turn_back(
        t, scatter_parts(part_two, TP), s1, c2, cot4, s4, c1, b1, mt8, st[0], st[1]
    )
    streams_out = lax.all_gather(jnp.transpose(s2, (1, 0, 2)), TP, axis=0, tiled=True)
    gb1 = to_all(gb1, TP).reshape(rows, width)
    do, gq = query_back(
        info, placement, gb1, w_output, q, kv, ql, kv_same, kv_other, cos, sin, scale
    )
    do_same, do_other = over_chips(do)
    gkv, part_three = key_back(
        info, placement, kv, qall, do_same, do_other, gq, cos, sin, w_query, w_key, w_value, scale
    )
    small = jnp.concatenate([gq, gkv], 1)
    small_z = lax.all_gather(small, "z", axis=0)
    grad4, dm, ds = last(t, scatter_parts(part_three, TP), base, s4, c1, mt8, st[0], dm, ds)
    grad_streams = to_all(jnp.transpose(grad4, (1, 0, 2)), TP).reshape(streams.shape)

    x_two = column_blocks(pay[:, 0:width])
    y_two = column_blocks(gb2)
    x_one = column_blocks(normed_one)
    y_one = column_blocks(gb1)
    hidden = w_gate.shape[1]
    part = jnp.concatenate(
        [
            grad_product(x_two, acts_z[:, 0]),
            grad_product(x_two, acts_z[:, 1]),
            grad_product(y_two, acts_z[:, 2]),
        ],
        1,
    )
    ff = sum_rows(part)
    att_z = lax.all_gather(attended, "z", axis=0)
    out = sum_rows(grad_product(y_one, att_z))
    qkv = sum_rows(grad_product(x_one, small_z))

    spread = jnp.transpose(dm.reshape(16, groups, width // groups), (1, 0, 2))
    statics = jnp.broadcast_to(ds.reshape(1, 16, 128), (groups, 16, 128))
    packed = jnp.concatenate([spread, statics], 1)
    packed = jnp.sum(lax.all_to_all(packed, DP, 0, 0, tiled=True), 0)
    packed = jnp.sum(to_all(packed, TP), 0)
    grad_dynamic = jnp.transpose(packed[:16].reshape(2, 8, -1)[:, :6], (0, 2, 1))
    grad_static = packed[16:].reshape(2, 8, 128)[:, :4, :6]
    return (
        streams_out,
        grad_streams,
        qkv[:, 0:cols],
        qkv[:, cols : 2 * cols],
        qkv[:, 2 * cols :],
        jnp.transpose(out),
        ff[:, 0:hidden],
        ff[:, hidden : 2 * hidden],
        jnp.transpose(ff[:, 2 * hidden :]),
        grad_dynamic,
        grad_static,
    )


def solution(mesh):
    fine = Mesh(mesh.devices.reshape(4, 2, 2, 2, 4), ("z", "yh", "core", "yl", "x"))
    placed = (
        P(DP, None, None),
        P(),
        P(None, TP),
        P(None, TP),
        P(None, TP),
        P(TP, None),
        P(None, TP),
        P(None, TP),
        P(TP, None),
        P(),
        P(),
        P(DP, None, None),
    )
    return jax.shard_map(
        per_device,
        mesh=fine,
        in_specs=placed,
        out_specs=(
            P(DP, None, None),
            P(DP, None, None),
            P(DP, TP),
            P(DP, TP),
            P(DP, TP),
            P(TP, DP),
            P(DP, TP),
            P(DP, TP),
            P(TP, DP),
            P(None, DP, None),
            P(),
        ),
        check_vma=False,
    )
```

```python
import functools

import jax
import jax.numpy as jnp
import numpy as np
from jax import lax
from jax.experimental import pallas as pl
from jax.experimental.pallas import tpu as pltpu
from jax.sharding import Mesh
from jax.sharding import PartitionSpec as P

HEAD = 128
EPS = 1e-05
THETA = 10000.0
BF = jnp.bfloat16
F32 = jnp.float32
K = 4
DP = ("z", "yh", "core")
TP = ("yl", "x")
SMEM = pl.BlockSpec(memory_space=pltpu.SMEM)
NT = (((1,), (1,)), ((), ()))
TN = (((0,), (0,)), ((), ()))
NN = (((1,), (0,)), ((), ()))


def dot(a, b, dims=NN):
    return lax.dot_general(a, b, dims, preferred_element_type=F32)


def lmean(v):
    return jnp.mean(v, -1, keepdims=True)


def lsum(v):
    return jnp.sum(v, -1, keepdims=True)


def norm_parts(v):
    ctr = v - lmean(v)
    rstd = lax.rsqrt(lmean(ctr * ctr) + EPS)
    return ctr * rstd, rstd


def norm_back(g, xhat, rstd):
    return rstd * (g - lmean(g) - xhat * lmean(g * xhat))


def three(v):
    hi = v.astype(BF)
    rest = v - hi.astype(F32)
    mid = rest.astype(BF)
    low = (rest - mid.astype(F32)).astype(BF)
    return hi, mid, low


def lanes(rows, pairs, start=None):
    lane = lax.broadcasted_iota(jnp.int32, (rows, 128), 1)
    out = jnp.zeros((rows, 128), F32) if start is None else start
    for at, v in pairs:
        out = jnp.where(lane == at, v, out)
    return out


def fold_parts(z):
    return z + pltpu.roll(z, 120, 1) + pltpu.roll(z, 112, 1)


def turn(v, cos, sin):
    return v * cos + pltpu.roll(v, 64, 1) * sin


def params(limit, **kw):
    return pltpu.CompilerParams(vmem_limit_bytes=60 * 2**20, **kw)


def whole(shape):
    n = len(shape)
    return pl.BlockSpec(shape, lambda *_: (0,) * n)


def like(*shapes):
    return tuple(jax.ShapeDtypeStruct(s, d) for s, d in shapes)


def iota(shape, dim):
    return lax.broadcasted_iota(jnp.int32, shape, dim)


def order(rows, to_planes):
    count = rows // K
    a, b = iota((rows, rows), 0), iota((rows, rows), 1)
    if not to_planes:
        a, b = b, a
    return (a == (b % K) * count + b // K).astype(BF)


def planes(block):
    rows, _, width = block.shape
    v = dot(order(K * rows, True), block.reshape(K * rows, width))
    return [v[k * rows : (k + 1) * rows] for k in range(K)]


def unplanes(parts):
    rows, width = parts[0].shape
    v = dot(order(K * rows, False), jnp.concatenate(parts, 0))
    return v.reshape(rows, K, width).astype(BF)


def stream_coefs(ref, rows):
    return [ref[pl.ds(k, rows, stride=K), :] for k in range(K)]


def static_rows(st_ref, layer, rows):
    row, lane = iota((rows, 128), 0) % K, iota((rows, 128), 1)
    out = jnp.zeros((rows, 128), F32)
    for k in range(K):
        for c in range(K + 2):
            out = jnp.where((row == k) & (lane == c), st_ref[layer, k, c], out)
    return out


def static_row(st_ref, layer, k):
    lane = iota((1, 128), 1)
    out = jnp.zeros((1, 128), F32)
    for c in range(K + 2):
        out = jnp.where(lane == c, st_ref[layer, k, c], out)
    return out


def fill_parts(m, wide_ref, mp_ref):
    cols = m.shape[0]
    wide_ref[...] = jnp.zeros_like(wide_ref)
    for i, v in enumerate(three(m)):
        wide_ref[8 * i : 8 * i + cols, :] = v.astype(F32)
    wide_ref[24:25, :] = jnp.ones((1, m.shape[1]), F32)
    mp_ref[...] = jnp.zeros_like(mp_ref)
    mp_ref[0:32, :] = wide_ref[...].astype(BF)


def device_index():
    core = lax.axis_index("core")
    return (lax.axis_index("z") * 2 + lax.axis_index("yh")) * 2 + core, core


def first_kernel(place_ref, st_ref, freq_ref, s_ref, m_ref, wq_ref, wk_ref, wv_ref,
                 n_ref, c_ref, qkv_ref, trig_ref, wide_ref, mp_ref):
    rows, _, width = s_ref.shape
    fill_parts(m_ref[0], wide_ref, mp_ref)
    sums = fold_parts(dot(jnp.ones((16, width), BF), mp_ref[...], NT))[0:1]
    step = 32
    part = K * step
    static = static_rows(st_ref, 0, part)
    row, lane = iota((part, 128), 0), iota((part, 128), 1)
    mine = (lane % step) == row // K

    def body(i, carry):
        r = pl.multiple_of(i * step, step)
        low = s_ref[pl.ds(r, step)].reshape(part, width)
        z = dot(low, mp_ref[...], NT)
        s = low.astype(F32)
        mean = z[:, 24:25] * (1.0 / width)
        ctr = s - mean
        rstd = lax.rsqrt(lmean(ctr * ctr) + EPS)
        c = static + jnp.tanh(rstd * (fold_parts(z) - mean * sums))
        c_ref[pl.ds(pl.multiple_of(i * part, part), part), :] = lanes(part, ((8, mean), (9, rstd)), c)
        a, b, d = (v.astype(F32) for v in three(c[:, 0:1]))
        take = jnp.where(lane < step, a, jnp.where(lane < 2 * step, b, d))
        take = jnp.where(mine & (lane < 3 * step), take, 0.0).astype(BF)
        w = dot(take, low, TN)
        taken = w[0:step] + w[step : 2 * step] + w[2 * step : 3 * step]
        n_ref[pl.ds(r, step), :] = norm_parts(taken)[0].astype(BF)
        return carry

    lax.fori_loop(0, rows // step, body, 0)
    me, _ = device_index()
    prompts = place_ref.shape[0] // 2
    start = jnp.minimum(place_ref[me], prompts) * rows
    angle = (start + iota((rows, HEAD), 0)).astype(F32) * freq_ref[...]
    cos = jnp.cos(angle)
    sin = jnp.where(iota((rows, HEAD), 1) < HEAD // 2, -1.0, 1.0) * jnp.sin(angle)
    trig_ref[0] = cos
    trig_ref[1] = sin
    normed = n_ref[...]
    q = dot(normed, wq_ref[...])
    k = dot(normed, wk_ref[...])
    heads = q.shape[1] // HEAD
    for h in range(heads):
        cut = slice(h * HEAD, (h + 1) * HEAD)
        qkv_ref[:, cut] = turn(q[:, cut], cos, sin).astype(BF)
        kcut = slice((heads + h) * HEAD, (heads + h + 1) * HEAD)
        qkv_ref[:, kcut] = turn(k[:, cut], cos, sin).astype(BF)
    qkv_ref[:, 2 * heads * HEAD :] = dot(normed, wv_ref[...]).astype(BF)


def first(place, st, streams, mt, wq, wk, wv):
    rows, _, width = streams.shape
    cols = wq.shape[1]
    half = HEAD // 2
    freq = np.float32(THETA) ** (-np.arange(half, dtype=np.float32) / np.float32(half))
    freq = jnp.asarray(np.concatenate([freq, freq])[None].astype(np.float32))
    outs = (
        ((rows, width), BF),
        ((K * rows, 128), F32),
        ((rows, 3 * cols), BF),
        ((2, rows, HEAD), F32),
    )
    return pl.pallas_call(
        first_kernel,
        grid=(1,),
        out_shape=like(*outs),
        in_specs=[SMEM, SMEM, whole(freq.shape), whole(streams.shape),
                  pl.BlockSpec((1, *mt.shape[1:]), lambda i: (0, 0, 0)),
                  whole(wq.shape), whole(wk.shape), whole(wv.shape)],
        out_specs=[whole(s) for s, _ in outs],
        scratch_shapes=[pltpu.VMEM((32, width), F32), pltpu.VMEM((128, width), BF)],
        compiler_params=params(26),
        name="first",
    )(place, st, freq, streams, mt, wq, wk, wv)


def own_blocks(place_ref, own_ref, same_ref, other_ref):
    me, core = device_index()
    own = place_ref[me]
    count = place_ref.shape[0]
    prompts = count // 2
    is_cont = own >= prompts
    blocks = []
    for s in range(prompts):
        d = jnp.int32(0)
        for a in range(count):
            d = jnp.where(place_ref[a] == s, a, d)
        block = jnp.where((d % 2) == core, same_ref[d // 2], other_ref[d // 2])
        reach = jnp.where(is_cont | (s < own), 4096, jnp.where(s == own, 0, -4096))
        blocks.append((block, reach))
    blocks.append((own_ref[...], jnp.where(is_cont, 0, -4096)))
    return blocks


def key_after_query(keys, queries):
    return iota((keys, queries), 0) - iota((keys, queries), 1)


def vector_rows(*vectors):
    row = iota((16, vectors[0].shape[1]), 0)
    out = jnp.zeros(row.shape, F32)
    for i, v in enumerate(vectors):
        for n, p in enumerate(three(v)):
            out = jnp.where(row == 3 * i + n, p.astype(F32), out)
    return out


def vector_of(rows16, i):
    v = rows16.astype(F32)
    return v[3 * i : 3 * i + 1] + v[3 * i + 1 : 3 * i + 2] + v[3 * i + 2 : 3 * i + 3]


def head_cuts(cols, h):
    return [slice(i * cols + h * HEAD, i * cols + (h + 1) * HEAD) for i in range(3)]


def attend_kernel(place_ref, own_ref, same_ref, other_ref, wo_ref, at_ref, log_ref, part_ref):
    rows, cols = at_ref.shape
    heads = cols // HEAD
    scale = HEAD ** (-0.5)
    blocks = own_blocks(place_ref, own_ref, same_ref, other_ref)
    lag = key_after_query(rows, rows)
    logs = []
    for h in range(heads):
        cut, kcut, vcut = head_cuts(cols, h)
        q = own_ref[:, cut]
        scores = [
            jnp.where(lag <= reach, dot(b[:, kcut], q, NT) * scale, -1e30) for b, reach in blocks
        ]
        top = functools.reduce(jnp.maximum, [jnp.max(s, 0, keepdims=True) for s in scores])
        terms = [jnp.exp(s - top) for s in scores]
        total = functools.reduce(jnp.add, [jnp.sum(e, 0, keepdims=True) for e in terms])
        inv = 1.0 / total
        out = None
        for e, (b, _) in zip(terms, blocks):
            o = dot((e * inv).astype(BF), b[:, vcut], TN)
            out = o if out is None else out + o
        at_ref[:, cut] = out.astype(BF)
        logs.append(top + jnp.log(total))
    log_ref[...] = jnp.concatenate(logs, 1)
    part_ref[...] = dot(at_ref[...], wo_ref[...]).astype(BF)


def attend(place, own, same, other, wo):
    rows = own.shape[0]
    cols = wo.shape[0]
    args = (own, same, other, wo)
    outs = (((rows, cols), BF), ((1, cols), F32), ((rows, wo.shape[1]), BF))
    return pl.pallas_call(
        attend_kernel,
        grid=(1,),
        out_shape=like(*outs),
        in_specs=[SMEM] + [whole(v.shape) for v in args],
        out_specs=[whole(s) for s, _ in outs],
        compiler_params=params(16),
        name="attend",
    )(place, *args)


def middle_kernel(t_ref, st_ref, parts_ref, s_ref, c_ref, m_ref, s1_ref, b1_ref, c2_ref, pay_ref,
                  wide_ref, mp_ref, split_ref):
    fill_parts(m_ref[0], wide_ref, mp_ref)
    b1 = jnp.sum(parts_ref[...].astype(F32), 0)
    b1_ref[...] = b1
    rows, width = b1.shape
    s0 = planes(s_ref[...])
    c1 = stream_coefs(c_ref, rows)
    stats = []
    for j in range(K):
        v = c1[j][:, 5:6] * b1
        for k in range(K):
            v = v + c1[k][:, 1 + j : 2 + j] * s0[k]
        s1_ref[j] = v
        mean = lmean(v)
        ctr = v - mean
        stats.append((mean, lax.rsqrt(lmean(ctr * ctr) + EPS)))
        hi = ctr.astype(BF)
        split_ref[j * rows : (j + 1) * rows, :] = hi
        split_ref[(K + j) * rows : (K + j + 1) * rows, :] = (ctr - hi.astype(F32)).astype(BF)
    z = dot(split_ref[...], mp_ref[...], NT)
    taken, gives = None, []
    for j in range(K):
        mean, rstd = stats[j]
        zj = z[j * rows : (j + 1) * rows] + z[(K + j) * rows : (K + j + 1) * rows]
        c = static_row(st_ref, 1, j) + jnp.tanh(rstd * fold_parts(zj))
        c2_ref[j] = lanes(rows, ((8, mean), (9, rstd)), c)
        part = c[:, 0:1] * s1_ref[j]
        taken = part if taken is None else taken + part
        gives += [(4 * i + j, v.astype(F32)) for i, v in enumerate(three(c[:, 5:6]))]
    pay_ref[:, 0:width] = norm_parts(taken)[0].astype(BF)
    pay_ref[:, width:] = lanes(rows, gives).astype(BF)


def token_call(kernel, name, t, tables, args, outs, scratch, limit):
    in_specs = [SMEM] * len(tables)
    for v, block in args:
        if block is None:
            in_specs.append(pl.BlockSpec(v.shape, lambda i, t, n=v.ndim: (0,) * n))
        else:
            in_specs.append(pl.BlockSpec(block, lambda i, t, n=v.ndim: (t[0],) + (0,) * (n - 1)))
    return pl.pallas_call(
        kernel,
        grid_spec=pltpu.PrefetchScalarGridSpec(
            num_scalar_prefetch=1,
            grid=(1,),
            in_specs=in_specs,
            out_specs=[pl.BlockSpec(s, lambda i, t, n=len(s): (0,) * n) for s, _ in outs],
            scratch_shapes=scratch,
        ),
        out_shape=like(*outs),
        compiler_params=params(limit),
        name=name,
    )(t, *tables, *[v for v, _ in args])


def middle(t, st, parts, streams, c1, mt_two):
    _, rows, width = parts.shape
    return token_call(
        middle_kernel,
        "middle",
        t,
        (st,),
        (
            (parts, None),
            (streams, (rows, K, width)),
            (c1, (K * rows, 128)),
            (mt_two, None),
        ),
        (
            ((K, rows, width), F32),
            ((rows, width), F32),
            ((K, rows, 128), F32),
            ((rows, width + 128), BF),
        ),
        [
            pltpu.VMEM((32, width), F32),
            pltpu.VMEM((128, width), BF),
            pltpu.VMEM((2 * K * rows, width), BF),
        ],
        12,
    )


def columns_for(step, count, piece):
    at = lax.rem(lax.axis_index("z") + step, count) * piece
    return pl.ds(pl.multiple_of(at, piece), piece)


def feed_kernel(pay_ref, cot_ref, wg_ref, wu_ref, wd_ref, *refs):
    *xy_refs, acts_ref, out_ref, gb_ref, b_ref, l_ref = refs
    step, steps = pl.program_id(0), pl.num_programs(0)
    rows, width = gb_ref.shape
    piece = width // len(xy_refs)

    @pl.when(step == 0)
    def _():
        chunk = 32
        row, lane = iota((chunk, K * chunk), 0), iota((chunk, K * chunk), 1)

        def body(i, carry):
            r = pl.multiple_of(i * chunk, chunk)
            give = pay_ref[pl.ds(r, chunk), width:].astype(F32)
            block = cot_ref[pl.ds(r, chunk)].reshape(K * chunk, width)
            total = None
            for n in range(3):
                w = jnp.zeros((chunk, K * chunk), F32)
                for j in range(K):
                    w = jnp.where(lane == K * row + j, give[:, K * n + j : K * n + j + 1], w)
                part = dot(w.astype(BF), block)
                total = part if total is None else total + part
            gb_ref[pl.ds(r, chunk), :] = total.astype(BF)
            return carry

        lax.fori_loop(0, rows // chunk, body, 0)
        for i, ref in enumerate(xy_refs):
            at = columns_for(i, len(xy_refs), piece)
            ref[:, 0:piece] = pay_ref[:, at]
            ref[:, piece:] = gb_ref[:, at]
        b_ref[...] = jnp.zeros_like(b_ref)
        l_ref[...] = jnp.zeros_like(l_ref)

    normed = pay_ref[:, 0:width]
    gate = dot(normed, wg_ref[...])
    up = dot(normed, wu_ref[...])
    sig = 1.0 / (1.0 + jnp.exp(-gate))
    silu = gate * sig
    hidden = (silu * up).astype(BF)
    grad = dot(gb_ref[...], wd_ref[...], NT)
    grad_gate = (grad * up * (sig * (1.0 + gate * (1.0 - sig)))).astype(BF)
    grad_up = (grad * silu).astype(BF)
    tile = hidden.shape[1]
    acts_ref[:, 0:tile] = grad_gate
    acts_ref[:, tile : 2 * tile] = grad_up
    acts_ref[:, 2 * tile :] = hidden
    b_ref[...] += dot(hidden, wd_ref[...])
    l_ref[...] += dot(grad_gate, wg_ref[...], NT) + dot(grad_up, wu_ref[...], NT)

    @pl.when(step == steps - 1)
    def _():
        out_ref[:, 0:width] = b_ref[...].astype(BF)
        out_ref[:, width:] = l_ref[...].astype(BF)


FEED_TILE = 256


def feed(pay, cotangent, wg, wu, wd, count):
    rows, _, width = cotangent.shape
    hidden = wg.shape[1]
    tile = FEED_TILE
    xy = (rows, 2 * width // count)
    return pl.pallas_call(
        feed_kernel,
        grid=(hidden // tile,),
        in_specs=[
            whole(pay.shape),
            whole(cotangent.shape),
            pl.BlockSpec((width, tile), lambda f: (0, f)),
            pl.BlockSpec((width, tile), lambda f: (0, f)),
            pl.BlockSpec((tile, width), lambda f: (f, 0)),
        ],
        out_specs=[
            *[whole(xy)] * count,
            pl.BlockSpec((rows, 3 * tile), lambda f: (0, f)),
            whole((rows, 2 * width)),
        ],
        out_shape=like(
            *[(xy, BF)] * count,
            ((rows, 3 * hidden), BF),
            ((rows, 2 * width), BF),
        ),
        scratch_shapes=[
            pltpu.VMEM((rows, width), BF),
            pltpu.VMEM((rows, width), F32),
            pltpu.VMEM((rows, width), F32),
        ],
        compiler_params=params(30),
        name="feed",
    )(pay, cotangent, wg, wu, wd)


def coef_back(grads, coefs, st_ref, layer, m, xhats, dm_ref, ds_ref, columns):
    rows = xhats[0].shape[0]
    dzs, statics = [], []
    for k in range(K):
        g = lanes(rows, grads[k].items())
        th = coefs[k] - static_row(st_ref, layer, k)
        dzs.append(g * (1.0 - th * th))
        statics.append(jnp.sum(g, 0, keepdims=True))
    ds_ref[layer] = jnp.concatenate(statics + [jnp.zeros((8 - K, 128), F32)], 0)
    for c in range(8):
        if c in columns:
            v = None
            for k in range(K):
                part = dzs[k][:, c : c + 1] * xhats[k]
                v = part if v is None else v + part
            dm_ref[layer, c : c + 1, :] = jnp.sum(v, 0, keepdims=True)
        else:
            dm_ref[layer, c : c + 1, :] = jnp.zeros((1, xhats[0].shape[1]), F32)
    out = []
    for k in range(K):
        v = None
        for c in columns:
            part = dzs[k][:, c : c + 1] * m[c : c + 1, :]
            v = part if v is None else v + part
        out.append(v)
    return out


def turn_kernel(t_ref, st_ref, parts_ref, s1_ref, c2_ref, cot_ref, s_ref, c1_ref, b1_ref, m_ref,
                s2_ref, gb1_ref, base_ref, dm_ref, ds_ref):
    rows, width = b1_ref.shape
    both = jnp.sum(parts_ref[...].astype(F32), 0)
    b2, gn = both[:, 0:width], both[:, width:]
    s1 = [s1_ref[k] for k in range(K)]
    c2 = [c2_ref[k] for k in range(K)]
    g2 = planes(cot_ref[...])
    grads = [dict() for _ in range(K)]
    taken, s2 = None, []
    for j in range(K):
        v = c2[j][:, 5:6] * b2
        for k in range(K):
            v = v + c2[k][:, 1 + j : 2 + j] * s1[k]
        s2.append(v.astype(BF))
        grads[j][5] = lsum(g2[j] * b2)
        for k in range(K):
            grads[k][1 + j] = lsum(g2[j] * s1[k])
        part = c2[j][:, 0:1] * s1[j]
        taken = part if taken is None else taken + part
    s2_ref[...] = unplanes(s2)
    normed, rstd = norm_parts(taken)
    gt = norm_back(gn, normed, rstd)
    for k in range(K):
        grads[k][0] = lsum(gt * s1[k])
    xhats = [(s1[k] - c2[k][:, 8:9]) * c2[k][:, 9:10] for k in range(K)]
    gx = coef_back(grads, c2, st_ref, 1, m_ref[1], xhats, dm_ref, ds_ref, range(6))
    g1 = []
    for k in range(K):
        v = c2[k][:, 0:1] * gt + norm_back(gx[k], xhats[k], c2[k][:, 9:10])
        for j in range(K):
            v = v + c2[k][:, 1 + j : 2 + j] * g2[j]
        g1.append(v)
    c1 = stream_coefs(c1_ref, rows)
    b1 = b1_ref[...]
    s0 = planes(s_ref[...])
    gb1 = None
    grads = [dict() for _ in range(K)]
    for j in range(K):
        part = c1[j][:, 5:6] * g1[j]
        gb1 = part if gb1 is None else gb1 + part
        grads[j][5] = lsum(g1[j] * b1)
        for k in range(K):
            grads[k][1 + j] = lsum(g1[j] * s0[k])
    gb1_ref[...] = gb1.astype(BF)
    xhats = [(s0[k] - c1[k][:, 8:9]) * c1[k][:, 9:10] for k in range(K)]
    gx = coef_back(grads, c1, st_ref, 0, m_ref[0], xhats, dm_ref, ds_ref, range(1, 6))
    base = []
    for k in range(K):
        v = norm_back(gx[k], xhats[k], c1[k][:, 9:10])
        for j in range(K):
            v = v + c1[k][:, 1 + j : 2 + j] * g1[j]
        base.append(v.astype(BF))
    base_ref[...] = unplanes(base)


def turn_back(t, st, parts, s1, c2, cotangent, streams, c1, b1, mt):
    rows, width = b1.shape
    block = (rows, K, width)
    return token_call(
        turn_kernel,
        "turn",
        t,
        (st,),
        (
            (parts, None),
            (s1, None),
            (c2, None),
            (cotangent, block),
            (streams, block),
            (c1, (K * rows, 128)),
            (b1, None),
            (mt, None),
        ),
        (
            (block, BF),
            ((rows, width), BF),
            (block, BF),
            ((2, 8, width), F32),
            ((2, 8, 128), F32),
        ),
        [],
        20,
    )


def query_kernel(place_ref, gb_ref, wo_ref, own_ref, log_ref, same_ref, other_ref, trig_ref,
                 at_ref, n_ref, do_ref, gq_ref, *ship_refs):
    rows, cols = gq_ref.shape
    heads = cols // HEAD
    scale = HEAD ** (-0.5)
    piece = gb_ref.shape[1] // len(ship_refs)
    grad = dot(gb_ref[...], wo_ref[...], NT).astype(BF)
    do_ref[0:rows, :] = grad
    blocks = own_blocks(place_ref, own_ref, same_ref, other_ref)
    lag = key_after_query(rows, rows)
    inners, logs = [], []
    for h in range(heads):
        cut, kcut, vcut = head_cuts(cols, h)
        q, do = own_ref[:, cut], grad[:, cut]
        log = log_ref[:, cut]
        logs.append(log)
        probs, gps, inner = [], [], None
        for b, reach in blocks:
            s = jnp.where(lag <= reach, dot(b[:, kcut], q, NT) * scale, -1e30)
            p = jnp.exp(s - log)
            gp = dot(b[:, vcut], do, NT)
            part = jnp.sum(p * gp, 0, keepdims=True)
            inner = part if inner is None else inner + part
            probs.append(p)
            gps.append(gp)
        gq = None
        for p, gp, (b, _) in zip(probs, gps, blocks):
            part = dot((p * (gp - inner)).astype(BF), b[:, kcut], TN)
            gq = part if gq is None else gq + part
        gq_ref[:, cut] = turn(gq * scale, trig_ref[0], -trig_ref[1]).astype(BF)
        inners.append(inner)
    do_ref[rows:, :] = jnp.concatenate(
        [vector_rows(i, log) for i, log in zip(inners, logs)], 1
    ).astype(BF)
    for i, ref in enumerate(ship_refs):
        at = columns_for(i, len(ship_refs), piece)
        ref[:, 0:piece] = gb_ref[:, at]
        ref[:, piece : 2 * piece] = n_ref[:, at]
        ref[:, 2 * piece :] = at_ref[...]


def query_back(place, gb1, wo, own, log, same, other, trig, attended, normed, count):
    rows, cols = attended.shape
    ship = ((rows, 2 * normed.shape[1] // count + cols), BF)
    args = (gb1, wo, own, log, same, other, trig, attended, normed)
    outs = (((rows + 16, cols), BF), ((rows, cols), BF), *[ship] * count)
    return pl.pallas_call(
        query_kernel,
        grid=(1,),
        out_shape=like(*outs),
        in_specs=[SMEM] + [whole(v.shape) for v in args],
        out_specs=[whole(s) for s, _ in outs],
        compiler_params=params(24),
        name="query_back",
    )(place, *args)


def key_kernel(place_ref, own_ref, qsame_ref, qother_ref, same_ref, other_ref, gq_ref, trig_ref,
               wq_ref, wk_ref, wv_ref, small_ref, part_ref):
    rows, cols = gq_ref.shape
    heads = cols // HEAD
    scale = HEAD ** (-0.5)
    me, core = device_index()
    own = place_ref[me]
    count = place_ref.shape[0]
    prompts = count // 2
    groups = [(g, rel) for g in range(count // 2) for rel in range(2)]
    reach = []
    for g, rel in groups:
        seg = place_ref[2 * g + (core + rel) % 2]
        full = (own < prompts) & (seg > own)
        value = jnp.where(full, 4096, jnp.where(seg == own, 0, -4096))
        reach.append(jnp.zeros((1, rows), jnp.int32) + value)
    reach = jnp.concatenate(reach, 1)
    lag = key_after_query(rows, rows)
    seen = jnp.concatenate([lag] * count, 1) <= reach
    for h in range(heads):
        cut, kcut, vcut = head_cuts(cols, h)
        k, v = own_ref[:, kcut], own_ref[:, vcut]
        qs, dos, logs, inners = [], [], [], []
        for g, rel in groups:
            src = same_ref if rel == 0 else other_ref
            qs.append((qsame_ref if rel == 0 else qother_ref)[g, :, cut])
            dos.append(src[g, 0:rows, cut])
            inners.append(vector_of(src[g, rows:, cut], 0))
            logs.append(vector_of(src[g, rows:, cut], 1))
        qs, dos = jnp.concatenate(qs, 0), jnp.concatenate(dos, 0)
        logs, inners = jnp.concatenate(logs, 1), jnp.concatenate(inners, 1)
        s = jnp.where(seen, dot(k, qs, NT) * scale, -1e30)
        p = jnp.exp(s - logs)
        gp = dot(v, dos, NT)
        ds = (p * (gp - inners)).astype(BF)
        gv = dot(p.astype(BF), dos)
        gk = dot(ds, qs) * scale
        small_ref[:, kcut] = turn(gk, trig_ref[0], -trig_ref[1]).astype(BF)
        small_ref[:, vcut] = gv.astype(BF)
    small_ref[:, 0:cols] = gq_ref[...]
    part = dot(gq_ref[...], wq_ref[...], NT)
    part += dot(small_ref[:, cols : 2 * cols], wk_ref[...], NT)
    part += dot(small_ref[:, 2 * cols :], wv_ref[...], NT)
    part_ref[...] = part.astype(BF)


def key_back(place, own, qsame, qother, same, other, gq, trig, wq, wk, wv):
    rows, cols = gq.shape
    args = (own, qsame, qother, same, other, gq, trig, wq, wk, wv)
    queries = pl.BlockSpec((*qsame.shape[:2], cols), lambda i: (0, 0, 0))
    specs = [whole(v.shape) for v in args]
    specs[1] = specs[2] = queries
    outs = (((rows, 3 * cols), BF), ((rows, wq.shape[0]), BF))
    return pl.pallas_call(
        key_kernel,
        grid=(1,),
        out_shape=like(*outs),
        in_specs=[SMEM] + specs,
        out_specs=[whole(s) for s, _ in outs],
        compiler_params=params(32),
        name="key_back",
    )(place, *args)


def last_kernel(t_ref, st_ref, parts_ref, s_ref, c_ref, dmin_ref, dsin_ref, gt_ref, dm_ref, ds_ref):
    gn = jnp.sum(parts_ref[...].astype(F32), 0)
    rows, width = gn.shape
    s0 = planes(s_ref[...])
    c1 = stream_coefs(c_ref, rows)
    taken = None
    for k in range(K):
        part = c1[k][:, 0:1] * s0[k]
        taken = part if taken is None else taken + part
    normed, rstd = norm_parts(taken)
    gt = norm_back(gn, normed, rstd)
    gt_ref[...] = gt.astype(BF)
    dm_ref[...] = dmin_ref[...]
    ds_ref[...] = dsin_ref[...]
    total = None
    lane = iota((1, 128), 1)
    for k in range(K):
        g = lsum(gt * s0[k])
        th = c1[k][:, 0:1] - st_ref[0, k, 0]
        part = g * (1.0 - th * th) * ((s0[k] - c1[k][:, 8:9]) * c1[k][:, 9:10])
        total = part if total is None else total + part
        ds_ref[0, k : k + 1, :] += jnp.where(lane == 0, jnp.sum(g, 0, keepdims=True), 0.0)
    dm_ref[0, 0:1, :] = jnp.sum(total, 0, keepdims=True)


def last(t, st, parts, streams, c1, dm, ds):
    _, rows, width = parts.shape
    return token_call(
        last_kernel,
        "last",
        t,
        (st,),
        (
            (parts, None),
            (streams, (rows, K, width)),
            (c1, (K * rows, 128)),
            (dm, None),
            (ds, None),
        ),
        (((rows, width), BF), (dm.shape, F32), (ds.shape, F32)),
        [],
        12,
    )


def final_kernel(st_ref, gt_ref, base_ref, s_ref, c_ref, m_ref, out_ref):
    rows, _, width = s_ref.shape
    part = K * rows
    spread = (iota((part, rows), 0) // K == iota((part, rows), 1)).astype(BF)
    gt = dot(spread, gt_ref[...])
    s0 = s_ref[...].reshape(part, width).astype(F32)
    c = c_ref[...]
    g = lsum(gt * s0)
    th = (c - static_rows(st_ref, 0, part))[:, 0:1]
    rstd = c[:, 9:10]
    xhat = (s0 - c[:, 8:9]) * rstd
    m = m_ref[0, 0:1, :]
    back = (m - lmean(m)) - xhat * lmean(m * xhat)
    v = base_ref[...].reshape(part, width).astype(F32) + c[:, 0:1] * gt
    v = v + (rstd * g * (1.0 - th * th)) * back
    out_ref[...] = v.astype(BF).reshape(rows, K, width)


def final(st, gt, base, streams, c1, mt):
    rows, _, width = streams.shape
    step = 32
    block = pl.BlockSpec((step, K, width), lambda i: (i, 0, 0))
    return pl.pallas_call(
        final_kernel,
        grid=(rows // step,),
        out_shape=jax.ShapeDtypeStruct(streams.shape, BF),
        in_specs=[
            SMEM,
            pl.BlockSpec((step, width), lambda i: (i, 0)),
            block,
            block,
            pl.BlockSpec((K * step, 128), lambda i: (i, 0)),
            whole(mt.shape),
        ],
        out_specs=block,
        compiler_params=params(20),
        name="final",
    )(st, gt, base, streams, c1, mt)


def weight_kernel(picks, tile, count, gathered, *refs):
    *lefts, keep_ref, give_ref, hold_ref = refs
    rights = lefts[-1:] if gathered else lefts[-count:]
    lefts = lefts[: -len(rights)]
    core, z = lax.axis_index("core"), lax.axis_index("z")
    mats = [
        jnp.concatenate([r[...] for r in lefts[i : i + count]], 0)
        for i in range(0, len(lefts), count)
    ]
    part = mats[0].shape[1] // 2
    for u, pick in enumerate(picks):
        cut = slice(u * tile, (u + 1) * tile)
        if gathered:
            right = [rights[0][lax.rem(z - i + count, count), :, cut] for i in range(count)]
        else:
            right = [r[:, cut] for r in rights]
        hold_ref[...] = dot(mats[pick], jnp.concatenate(right, 0), TN)
        keep_ref[0, u] = hold_ref[pl.ds(pl.multiple_of(core * part, part), part), :]
        give_ref[0, u] = hold_ref[pl.ds(pl.multiple_of((1 - core) * part, part), part), :].astype(BF)


def weight_part(left, offsets, right, right_at, tiles, picks, tile, name):
    count = len(left)
    rows = left[0].shape[0]
    units = len(picks)
    gathered = not isinstance(right, (list, tuple))
    shape = (2, units, 128, tiles * tile)
    out = pl.BlockSpec((1, units, 128, tile), lambda f, y: (y, 0, 0, f))
    specs = [
        pl.BlockSpec((rows, 256), lambda f, y, o=o: (0, o + y)) for o in offsets for _ in left
    ]
    if gathered:
        specs.append(pl.BlockSpec((count, rows, units * tile), lambda f, y: (0, 0, right_at + f)))
        right = [right]
    else:
        specs += [pl.BlockSpec((rows, units * tile), lambda f, y: (0, right_at + f))] * count
    return pl.pallas_call(
        functools.partial(weight_kernel, picks, tile, count, gathered),
        grid=(tiles, 2),
        in_specs=specs,
        out_specs=[out, out],
        out_shape=like((shape, F32), (shape, BF)),
        scratch_shapes=[pltpu.VMEM((256, tile), F32)],
        compiler_params=params(16),
        name=name,
    )(*[v for _ in offsets for v in left], *right)


def to_all(shard, axes):
    copies = jnp.broadcast_to(shard, (lax.axis_size(axes), *shard.shape))
    return lax.all_to_all(copies, axes, 0, 0, tiled=True)


def exchange(blocks, axes):
    return lax.all_to_all(blocks, axes, 0, 0, tiled=True)


def scatter_parts(partial, axes):
    n = lax.axis_size(axes)
    return exchange(partial.reshape(n, partial.shape[0] // n, partial.shape[1]), axes)


def swap(v, axis):
    return lax.ppermute(v, axis, [(0, 1), (1, 0)])


def over_chips(shard):
    same = to_all(shard, ("z", "yh"))
    return same, swap(same, "core")


def along_z(pieces):
    n = lax.axis_size("z")
    return [pieces[0]] + [
        lax.ppermute(pieces[i], "z", [(a, (a + i) % n) for a in range(n)]) for i in range(1, n)
    ]


def pick(v, at):
    return lax.dynamic_index_in_dim(v, at, 0, keepdims=False)


def over_yh(kept, got):
    yh = lax.axis_index("yh")
    give = pick(kept, 1 - yh) + pick(got, 1 - yh).astype(F32)
    return pick(kept, yh) + pick(got, yh).astype(F32) + swap(give.astype(BF), "yh").astype(F32)


def per_device(streams, placement, w_query, w_key, w_value, w_output, w_gate, w_up, w_down,
               mix_dynamic, mix_static, cotangent):
    rows, _, width = streams.shape
    groups = placement.shape[0]
    t = lax.axis_index(TP).astype(jnp.int32)[None]
    nz = lax.axis_size("z")
    mt = jnp.transpose(mix_dynamic, (0, 2, 1))

    normed_one, c1, own, trig = first(placement, mix_static, streams, mt, w_query, w_key, w_value)
    same, other = over_chips(own)
    attended, log, part_one = attend(placement, own, same, other, w_output)
    s1, b1, c2, pay = middle(t, mix_static, scatter_parts(part_one, TP), streams, c1, mt[1:2])
    pay = to_all(pay, TP).reshape(rows, width + 128)
    *xy, acts, part_two = feed(pay, cotangent, w_gate, w_up, w_down, nz)
    acts = lax.all_gather(acts, "z", axis=0)
    xy = along_z(xy)
    parts = scatter_parts(part_two, TP)
    s2, gb1, base, dm, ds = turn_back(t, mix_static, parts, s1, c2, cotangent, streams, c1, b1, mt)
    gb1 = to_all(gb1, TP).reshape(rows, width)
    base = lax.all_gather(base, TP, axis=0, tiled=True)
    streams_out = lax.all_gather(s2, TP, axis=0, tiled=True)
    do, gq, *ship = query_back(
        placement, gb1, w_output, own, log, same, other, trig, attended, normed_one, nz
    )
    ship = along_z(ship)
    do_same, do_other = over_chips(do)
    small, part_three = key_back(
        placement, own, same, other, do_same, do_other, gq, trig, w_query, w_key, w_value
    )
    small = along_z([small] * nz)
    parts = scatter_parts(part_three, TP)
    gt, dm, ds = last(t, mix_static, parts, streams, c1, dm, ds)
    gt = to_all(gt, TP).reshape(rows, width)
    grad_streams = final(mix_static, gt, base, streams, c1, mt)

    tiles = w_gate.shape[1] // FEED_TILE
    keep, give = weight_part(xy, (0, 2), acts, 0, tiles, (0, 0, 1), FEED_TILE, "feed_weights")
    ff = over_yh(keep, swap(give, "core"))
    keep, give = weight_part(ship, (0,), ship, 4, 1, (0,), 256, "output_weights")
    out = over_yh(keep, swap(give, "core"))
    keep, give = weight_part(ship, (2,), small, 0, 1, (0, 0, 0), 256, "qkv_weights")
    qkv = over_yh(keep, swap(give, "core"))

    spread = jnp.transpose(dm.reshape(16, groups, width // groups), (1, 0, 2))
    statics = jnp.broadcast_to(ds.reshape(1, 16, 128), (groups, 16, 128))
    packed = jnp.concatenate([spread, statics], 1)
    packed = jnp.sum(exchange(packed, DP), 0)
    packed = jnp.sum(to_all(packed, TP), 0)
    grad_dynamic = jnp.transpose(packed[:16].reshape(2, 8, -1)[:, :6], (0, 2, 1))
    grad_static = packed[16:].reshape(2, 8, 128)[:, :4, :6]
    return (
        streams_out,
        grad_streams,
        qkv[0],
        qkv[1],
        qkv[2],
        jnp.transpose(out[0]),
        ff[0],
        ff[1],
        jnp.transpose(ff[2]),
        grad_dynamic,
        grad_static,
    )


def solution(mesh):
    fine = Mesh(mesh.devices.reshape(4, 2, 2, 2, 4), ("z", "yh", "core", "yl", "x"))
    placed = (
        P(DP, None, None),
        P(),
        P(None, TP),
        P(None, TP),
        P(None, TP),
        P(TP, None),
        P(None, TP),
        P(None, TP),
        P(TP, None),
        P(),
        P(),
        P(DP, None, None),
    )
    return jax.shard_map(
        per_device,
        mesh=fine,
        in_specs=placed,
        out_specs=(
            P(DP, None, None),
            P(DP, None, None),
            P(DP, TP),
            P(DP, TP),
            P(DP, TP),
            P(TP, DP),
            P(DP, TP),
            P(DP, TP),
            P(TP, DP),
            P(None, DP, None),
            P(),
        ),
        check_vma=False,
    )
```

```python
import functools

import jax
import jax.numpy as jnp
import numpy as np
from jax import lax
from jax.experimental import pallas as pl
from jax.experimental.pallas import tpu as pltpu
from jax.sharding import Mesh
from jax.sharding import PartitionSpec as P

HEAD = 128
EPS = 1e-05
THETA = 10000.0
BF = jnp.bfloat16
F32 = jnp.float32
K = 4
DP = ("z", "yh", "core")
TP = ("yl", "x")
SMEM = pl.BlockSpec(memory_space=pltpu.SMEM)
ANY = pl.BlockSpec(memory_space=pl.ANY)
NT = (((1,), (1,)), ((), ()))
TN = (((0,), (0,)), ((), ()))
NN = (((1,), (0,)), ((), ()))


def dot(a, b, dims=NN):
    return lax.dot_general(a, b, dims, preferred_element_type=F32)


def lmean(v):
    return jnp.mean(v, -1, keepdims=True)


def lsum(v):
    return jnp.sum(v, -1, keepdims=True)


def norm_parts(v):
    ctr = v - lmean(v)
    rstd = lax.rsqrt(lmean(ctr * ctr) + EPS)
    return ctr * rstd, rstd


def norm_back(g, xhat, rstd):
    return rstd * (g - lmean(g) - xhat * lmean(g * xhat))


def three(v):
    hi = v.astype(BF)
    rest = v - hi.astype(F32)
    mid = rest.astype(BF)
    low = (rest - mid.astype(F32)).astype(BF)
    return hi, mid, low


def lanes(rows, pairs, start=None):
    lane = lax.broadcasted_iota(jnp.int32, (rows, 128), 1)
    out = jnp.zeros((rows, 128), F32) if start is None else start
    for at, v in pairs:
        out = jnp.where(lane == at, v, out)
    return out


def fold_parts(z):
    return z + pltpu.roll(z, 120, 1) + pltpu.roll(z, 112, 1)


def turn(v, cos, sin):
    return v * cos + pltpu.roll(v, 64, 1) * sin


def cost(us):
    return pl.CostEstimate(flops=0, bytes_accessed=int(us * 3.69e6), transcendentals=0)


def params():
    return pltpu.CompilerParams(vmem_limit_bytes=60 * 2**20)


def whole(shape):
    n = len(shape)
    return pl.BlockSpec(shape, lambda *_: (0,) * n)


def like(*shapes):
    return tuple(jax.ShapeDtypeStruct(s, d) for s, d in shapes)


def iota(shape, dim):
    return lax.broadcasted_iota(jnp.int32, shape, dim)


def order(rows, to_planes):
    count = rows // K
    a, b = iota((rows, rows), 0), iota((rows, rows), 1)
    if not to_planes:
        a, b = b, a
    return (a == (b % K) * count + b // K).astype(BF)


def planes(block):
    rows, _, width = block.shape
    v = dot(order(K * rows, True), block.reshape(K * rows, width))
    return [v[k * rows : (k + 1) * rows] for k in range(K)]


def unplanes(parts):
    rows = parts[0].shape[0]
    return dot(order(K * rows, False), jnp.concatenate(parts, 0)).astype(BF)


def stream_coefs(ref, rows):
    return [ref[pl.ds(k, rows, stride=K), :] for k in range(K)]


def static_rows(st_ref, layer, rows):
    row, lane = iota((rows, 128), 0) % K, iota((rows, 128), 1)
    out = jnp.zeros((rows, 128), F32)
    for k in range(K):
        for c in range(K + 2):
            out = jnp.where((row == k) & (lane == c), st_ref[layer, k, c], out)
    return out


def static_row(st_ref, layer, k):
    lane = iota((1, 128), 1)
    out = jnp.zeros((1, 128), F32)
    for c in range(K + 2):
        out = jnp.where(lane == c, st_ref[layer, k, c], out)
    return out


def fill_parts(m, wide_ref, mp_ref):
    cols = m.shape[0]
    wide_ref[...] = jnp.zeros_like(wide_ref)
    for i, v in enumerate(three(m)):
        wide_ref[8 * i : 8 * i + cols, :] = v.astype(F32)
    wide_ref[24:25, :] = jnp.ones((1, m.shape[1]), F32)
    mp_ref[...] = jnp.zeros_like(mp_ref)
    mp_ref[0:32, :] = wide_ref[...].astype(BF)


def columns_for(step, count, piece):
    at = lax.rem(lax.axis_index("z") + step, count) * piece
    return pl.ds(pl.multiple_of(at, piece), piece)


def copies(ref):
    for i in range(1, ref.shape[0]):
        ref[i] = ref[0]


def device_index():
    core = lax.axis_index("core")
    return (lax.axis_index("z") * 2 + lax.axis_index("yh")) * 2 + core, core


def first_kernel(place_ref, st_ref, freq_ref, s_ref, m_ref, wq_ref, wk_ref, wv_ref,
                 c_ref, q_ref, kv_ref, trig_ref, *refs):
    *x_refs, n_ref, wide_ref, mp_ref = refs
    rows, _, width = s_ref.shape
    fill_parts(m_ref[:, 0, :], wide_ref, mp_ref)
    sums = fold_parts(dot(jnp.ones((16, width), BF), mp_ref[...], NT))[0:1]
    step = 32
    part = K * step
    static = static_rows(st_ref, 0, part)
    row, lane = iota((part, 128), 0), iota((part, 128), 1)
    mine = (lane % step) == row // K

    def body(i, carry):
        r = pl.multiple_of(i * step, step)
        low = s_ref[pl.ds(r, step)].reshape(part, width)
        z = dot(low, mp_ref[...], NT)
        s = low.astype(F32)
        mean = z[:, 24:25] * (1.0 / width)
        ctr = s - mean
        rstd = lax.rsqrt(lmean(ctr * ctr) + EPS)
        c = static + jnp.tanh(rstd * (fold_parts(z) - mean * sums))
        c_ref[pl.ds(pl.multiple_of(i * part, part), part), :] = lanes(part, ((8, mean), (9, rstd)), c)
        a, b, d = (v.astype(F32) for v in three(c[:, 0:1]))
        take = jnp.where(lane < step, a, jnp.where(lane < 2 * step, b, d))
        take = jnp.where(mine & (lane < 3 * step), take, 0.0).astype(BF)
        w = dot(take, low, TN)
        taken = w[0:step] + w[step : 2 * step] + w[2 * step : 3 * step]
        n_ref[pl.ds(r, step), :] = norm_parts(taken)[0].astype(BF)
        return carry

    lax.fori_loop(0, rows // step, body, 0)
    piece = width // len(x_refs)
    for i, ref in enumerate(x_refs):
        ref[...] = n_ref[:, columns_for(i, len(x_refs), piece)]
    me, _ = device_index()
    prompts = place_ref.shape[0] // 2
    start = jnp.minimum(place_ref[me], prompts) * rows
    angle = (start + iota((rows, HEAD), 0)).astype(F32) * freq_ref[...]
    cos = jnp.cos(angle)
    sin = jnp.where(iota((rows, HEAD), 1) < HEAD // 2, -1.0, 1.0) * jnp.sin(angle)
    trig_ref[0] = cos
    trig_ref[1] = sin
    normed = n_ref[...]
    q = dot(normed, wq_ref[...])
    k = dot(normed, wk_ref[...])
    heads = q.shape[1] // HEAD
    for h in range(heads):
        cut = slice(h * HEAD, (h + 1) * HEAD)
        q_ref[:, cut] = turn(q[:, cut], cos, sin).astype(BF)
        kv_ref[0, :, cut] = turn(k[:, cut], cos, sin).astype(BF)
    kv_ref[0, :, heads * HEAD :] = dot(normed, wv_ref[...]).astype(BF)
    copies(kv_ref)


def first(place, st, streams, mt, wq, wk, wv, chips, count):
    rows, _, width = streams.shape
    cols = wq.shape[1]
    half = HEAD // 2
    freq = np.float32(THETA) ** (-np.arange(half, dtype=np.float32) / np.float32(half))
    freq = jnp.asarray(np.concatenate([freq, freq])[None].astype(np.float32))
    outs = (
        ((K * rows, 128), F32),
        ((rows, cols), BF),
        ((chips, rows, 2 * cols), BF),
        ((2, rows, HEAD), F32),
        *[((rows, width // count), BF)] * count,
    )
    return pl.pallas_call(
        first_kernel,
        grid=(1,),
        out_shape=like(*outs),
        in_specs=[SMEM, SMEM, whole(freq.shape), whole(streams.shape),
                  whole(mt.shape),
                  whole(wq.shape), whole(wk.shape), whole(wv.shape)],
        out_specs=[whole(s) for s, _ in outs],
        scratch_shapes=[
            pltpu.VMEM((rows, width), BF),
            pltpu.VMEM((32, width), F32),
            pltpu.VMEM((128, width), BF),
        ],
        compiler_params=params(),
        cost_estimate=cost(10),
        name="first",
    )(place, st, freq, streams, mt, wq, wk, wv)


def own_blocks(place_ref, own_ref, same_ref, other_ref):
    me, core = device_index()
    own = place_ref[me]
    count = place_ref.shape[0]
    prompts = count // 2
    is_cont = own >= prompts
    blocks = []
    for s in range(prompts):
        d = jnp.int32(0)
        for a in range(count):
            d = jnp.where(place_ref[a] == s, a, d)
        block = jnp.where((d % 2) == core, same_ref[d // 2], other_ref[d // 2])
        reach = jnp.where(is_cont | (s < own), 4096, jnp.where(s == own, 0, -4096))
        blocks.append((block, reach))
    blocks.append((own_ref[0], jnp.where(is_cont, 0, -4096)))
    return blocks


def key_after_query(keys, queries):
    return iota((keys, queries), 0) - iota((keys, queries), 1)


def vector_rows(*vectors):
    row = iota((16, vectors[0].shape[1]), 0)
    out = jnp.zeros(row.shape, F32)
    for i, v in enumerate(vectors):
        for n, p in enumerate(three(v)):
            out = jnp.where(row == 3 * i + n, p.astype(F32), out)
    return out


def vector_of(rows16, i):
    v = rows16.astype(F32)
    return v[3 * i : 3 * i + 1] + v[3 * i + 1 : 3 * i + 2] + v[3 * i + 2 : 3 * i + 3]


def head_cuts(cols, h):
    return [slice(i * cols + h * HEAD, i * cols + (h + 1) * HEAD) for i in (0, 1)]


def attend_kernel(place_ref, q_ref, own_ref, same_ref, other_ref, wo_ref, at_ref, log_ref, part_ref, qcopy_ref):
    rows, cols = at_ref.shape
    heads = cols // HEAD
    scale = HEAD ** (-0.5)
    blocks = own_blocks(place_ref, own_ref, same_ref, other_ref)
    lag = key_after_query(rows, rows)
    logs = []
    for h in range(heads):
        cut, vcut = head_cuts(cols, h)
        q = q_ref[:, cut]
        scores = [
            jnp.where(lag <= reach, dot(b[:, cut], q, NT) * scale, -1e30) for b, reach in blocks
        ]
        top = functools.reduce(jnp.maximum, [jnp.max(s, 0, keepdims=True) for s in scores])
        terms = [jnp.exp(s - top) for s in scores]
        total = functools.reduce(jnp.add, [jnp.sum(e, 0, keepdims=True) for e in terms])
        inv = 1.0 / total
        out = None
        for e, (b, _) in zip(terms, blocks):
            o = dot((e * inv).astype(BF), b[:, vcut], TN)
            out = o if out is None else out + o
        at_ref[:, cut] = out.astype(BF)
        logs.append(top + jnp.log(total))
    log_ref[...] = jnp.concatenate(logs, 1)
    qcopy_ref[...] = q_ref[...]
    part_ref[...] = dot(at_ref[...], wo_ref[...]).astype(BF)


def own_block(kv):
    return pl.BlockSpec((1, *kv.shape[1:]), lambda i: (0, 0, 0))


def attend(place, q, kv, same, other, wo):
    rows, cols = q.shape
    args = (q, kv, same, other, wo)
    outs = (((rows, cols), BF), ((1, cols), F32), ((rows, wo.shape[1]), BF), ((rows, cols), BF))
    return pl.pallas_call(
        attend_kernel,
        grid=(1,),
        out_shape=like(*outs),
        in_specs=[SMEM, whole(q.shape), own_block(kv)] + [whole(v.shape) for v in args[2:]],
        out_specs=[whole(s) for s, _ in outs],
        compiler_params=params(),
        cost_estimate=cost(4.5),
        name="attend",
    )(place, *args)


def middle_kernel(t_ref, st_ref, parts_ref, s_ref, c_ref, m_ref, s1_ref, b1_ref, c2_ref, pay_ref,
                  wide_ref, mp_ref, split_ref):
    fill_parts(m_ref[:, 1, :], wide_ref, mp_ref)
    b1 = jnp.sum(parts_ref[...].astype(F32), 0)
    b1_ref[...] = b1
    rows, width = b1.shape
    s0 = planes(s_ref[...])
    c1 = stream_coefs(c_ref, rows)
    stats = []
    for j in range(K):
        v = c1[j][:, 5:6] * b1
        for k in range(K):
            v = v + c1[k][:, 1 + j : 2 + j] * s0[k]
        s1_ref[j] = v
        mean = lmean(v)
        ctr = v - mean
        stats.append((mean, lax.rsqrt(lmean(ctr * ctr) + EPS)))
        hi = ctr.astype(BF)
        split_ref[j * rows : (j + 1) * rows, :] = hi
        split_ref[(K + j) * rows : (K + j + 1) * rows, :] = (ctr - hi.astype(F32)).astype(BF)
    z = dot(split_ref[...], mp_ref[...], NT)
    taken, gives = None, []
    for j in range(K):
        mean, rstd = stats[j]
        zj = z[j * rows : (j + 1) * rows] + z[(K + j) * rows : (K + j + 1) * rows]
        c = static_row(st_ref, 1, j) + jnp.tanh(rstd * fold_parts(zj))
        c2_ref[j] = lanes(rows, ((8, mean), (9, rstd)), c)
        part = c[:, 0:1] * s1_ref[j]
        taken = part if taken is None else taken + part
        gives += [(4 * i + j, v.astype(F32)) for i, v in enumerate(three(c[:, 5:6]))]
    pay_ref[0, :, 0:width] = norm_parts(taken)[0].astype(BF)
    pay_ref[0, :, width:] = lanes(rows, gives).astype(BF)
    copies(pay_ref)


def token_call(kernel, name, t, tables, args, outs, scratch, waits=()):
    count = 1 + len(tables) + len(args)

    def body(*refs):
        kernel(*refs[:count], *refs[count + len(waits) :])

    in_specs = [SMEM] * len(tables)
    for v, block in args:
        if block is None:
            in_specs.append(pl.BlockSpec(v.shape, lambda i, t, n=v.ndim: (0,) * n))
        else:
            in_specs.append(pl.BlockSpec(block, lambda i, t, n=v.ndim: (t[0],) + (0,) * (n - 1)))
    return pl.pallas_call(
        body,
        grid_spec=pltpu.PrefetchScalarGridSpec(
            num_scalar_prefetch=1,
            grid=(1,),
            in_specs=in_specs + [ANY] * len(waits),
            out_specs=[pl.BlockSpec(s, lambda i, t, n=len(s): (0,) * n) for s, _ in outs],
            scratch_shapes=scratch,
        ),
        out_shape=like(*outs),
        compiler_params=params(),
        cost_estimate=cost(4),
        name=name,
    )(t, *tables, *[v for v, _ in args], *waits)


def middle(t, st, parts, streams, c1, mt, waits):
    peers, rows, width = parts.shape
    return token_call(
        middle_kernel,
        "middle",
        t,
        (st,),
        (
            (parts, None),
            (streams, (rows, K, width)),
            (c1, (K * rows, 128)),
            (mt, None),
        ),
        (
            ((K, rows, width), F32),
            ((rows, width), F32),
            ((K, rows, 128), F32),
            ((peers, rows, width + 128), BF),
        ),
        [
            pltpu.VMEM((32, width), F32),
            pltpu.VMEM((128, width), BF),
            pltpu.VMEM((2 * K * rows, width), BF),
        ],
        waits,
    )


def feed_kernel(pay_ref, cot_ref, wg_ref, wu_ref, wd_ref, *refs):
    *xy_refs, acts_ref, out_ref, gb_ref, b_ref, l_ref = refs
    step, steps = pl.program_id(0), pl.num_programs(0)
    rows, width = gb_ref.shape
    piece = width // len(xy_refs)

    @pl.when(step == 0)
    def _():
        chunk = 32
        row, lane = iota((chunk, K * chunk), 0), iota((chunk, K * chunk), 1)

        def body(i, carry):
            r = pl.multiple_of(i * chunk, chunk)
            give = pay_ref[pl.ds(r, chunk), width:].astype(F32)
            block = cot_ref[pl.ds(r, chunk)].reshape(K * chunk, width)
            total = None
            for n in range(3):
                w = jnp.zeros((chunk, K * chunk), F32)
                for j in range(K):
                    w = jnp.where(lane == K * row + j, give[:, K * n + j : K * n + j + 1], w)
                part = dot(w.astype(BF), block)
                total = part if total is None else total + part
            gb_ref[pl.ds(r, chunk), :] = total.astype(BF)
            return carry

        lax.fori_loop(0, rows // chunk, body, 0)
        for i, ref in enumerate(xy_refs):
            at = columns_for(i, len(xy_refs), piece)
            ref[:, 0:piece] = pay_ref[:, at]
            ref[:, piece:] = gb_ref[:, at]
        b_ref[...] = jnp.zeros_like(b_ref)
        l_ref[...] = jnp.zeros_like(l_ref)

    normed = pay_ref[:, 0:width]
    gate = dot(normed, wg_ref[...])
    up = dot(normed, wu_ref[...])
    sig = 1.0 / (1.0 + jnp.exp(-gate))
    silu = gate * sig
    hidden = (silu * up).astype(BF)
    grad = dot(gb_ref[...], wd_ref[...], NT)
    grad_gate = (grad * up * (sig * (1.0 + gate * (1.0 - sig)))).astype(BF)
    grad_up = (grad * silu).astype(BF)
    tile = hidden.shape[1]
    acts_ref[:, 0:tile] = grad_gate
    acts_ref[:, tile : 2 * tile] = grad_up
    acts_ref[:, 2 * tile :] = hidden
    b_ref[...] += dot(hidden, wd_ref[...])
    l_ref[...] += dot(grad_gate, wg_ref[...], NT) + dot(grad_up, wu_ref[...], NT)

    @pl.when(step == steps - 1)
    def _():
        out_ref[:, 0:width] = b_ref[...].astype(BF)
        out_ref[:, width:] = l_ref[...].astype(BF)


FEED_TILE = 256


def feed(pay, cotangent, wg, wu, wd, count):
    rows, _, width = cotangent.shape
    hidden = wg.shape[1]
    tile = FEED_TILE
    xy = (rows, 2 * width // count)
    return pl.pallas_call(
        feed_kernel,
        grid=(hidden // tile,),
        in_specs=[
            whole(pay.shape),
            whole(cotangent.shape),
            pl.BlockSpec((width, tile), lambda f: (0, f)),
            pl.BlockSpec((width, tile), lambda f: (0, f)),
            pl.BlockSpec((tile, width), lambda f: (f, 0)),
        ],
        out_specs=[
            *[whole(xy)] * count,
            pl.BlockSpec((rows, 3 * tile), lambda f: (0, f)),
            whole((rows, 2 * width)),
        ],
        out_shape=like(
            *[(xy, BF)] * count,
            ((rows, 3 * hidden), BF),
            ((rows, 2 * width), BF),
        ),
        scratch_shapes=[
            pltpu.VMEM((rows, width), BF),
            pltpu.VMEM((rows, width), F32),
            pltpu.VMEM((rows, width), F32),
        ],
        compiler_params=params(),
        cost_estimate=cost(14),
        name="feed",
    )(pay, cotangent, wg, wu, wd)


def coef_back(grads, coefs, st_ref, layer, m, xhats, dm_ref, ds_ref, columns):
    rows = xhats[0].shape[0]
    dzs, statics = [], []
    for k in range(K):
        g = lanes(rows, grads[k].items())
        th = coefs[k] - static_row(st_ref, layer, k)
        dzs.append(g * (1.0 - th * th))
        statics.append(jnp.sum(g, 0, keepdims=True))
    ds_ref[layer] = jnp.concatenate(statics + [jnp.zeros((8 - K, 128), F32)], 0)
    for c in range(8):
        if c in columns:
            v = None
            for k in range(K):
                part = dzs[k][:, c : c + 1] * xhats[k]
                v = part if v is None else v + part
            dm_ref[layer, c : c + 1, :] = jnp.sum(v, 0, keepdims=True)
        else:
            dm_ref[layer, c : c + 1, :] = jnp.zeros((1, xhats[0].shape[1]), F32)
    out = []
    for k in range(K):
        v = None
        for c in columns:
            part = dzs[k][:, c : c + 1] * m[c : c + 1, :]
            v = part if v is None else v + part
        out.append(v)
    return out


def turn_kernel(t_ref, st_ref, parts_ref, s1_ref, c2_ref, cot_ref, s_ref, c1_ref, b1_ref, m_ref,
                own_ref, pair_ref, base_ref, gb1_ref, dm_ref, ds_ref):
    rows, width = b1_ref.shape
    both = jnp.sum(parts_ref[...].astype(F32), 0)
    b2, gn = both[:, 0:width], both[:, width:]
    s1 = [s1_ref[k] for k in range(K)]
    c2 = [c2_ref[k] for k in range(K)]
    g2 = planes(cot_ref[...])
    grads = [dict() for _ in range(K)]
    taken, s2 = None, []
    for j in range(K):
        v = c2[j][:, 5:6] * b2
        for k in range(K):
            v = v + c2[k][:, 1 + j : 2 + j] * s1[k]
        s2.append(v.astype(BF))
        grads[j][5] = lsum(g2[j] * b2)
        for k in range(K):
            grads[k][1 + j] = lsum(g2[j] * s1[k])
        part = c2[j][:, 0:1] * s1[j]
        taken = part if taken is None else taken + part
    s2 = unplanes(s2)
    own_ref[...] = s2
    pair_ref[0] = s2
    normed, rstd = norm_parts(taken)
    gt = norm_back(gn, normed, rstd)
    for k in range(K):
        grads[k][0] = lsum(gt * s1[k])
    xhats = [(s1[k] - c2[k][:, 8:9]) * c2[k][:, 9:10] for k in range(K)]
    gx = coef_back(grads, c2, st_ref, 1, m_ref[:, 1, :], xhats, dm_ref, ds_ref, range(6))
    g1 = []
    for k in range(K):
        v = c2[k][:, 0:1] * gt + norm_back(gx[k], xhats[k], c2[k][:, 9:10])
        for j in range(K):
            v = v + c2[k][:, 1 + j : 2 + j] * g2[j]
        g1.append(v)
    c1 = stream_coefs(c1_ref, rows)
    b1 = b1_ref[...]
    s0 = planes(s_ref[...])
    gb1 = None
    grads = [dict() for _ in range(K)]
    for j in range(K):
        part = c1[j][:, 5:6] * g1[j]
        gb1 = part if gb1 is None else gb1 + part
        grads[j][5] = lsum(g1[j] * b1)
        for k in range(K):
            grads[k][1 + j] = lsum(g1[j] * s0[k])
    gb1_ref[0] = gb1.astype(BF)
    copies(gb1_ref)
    xhats = [(s0[k] - c1[k][:, 8:9]) * c1[k][:, 9:10] for k in range(K)]
    gx = coef_back(grads, c1, st_ref, 0, m_ref[:, 0, :], xhats, dm_ref, ds_ref, range(1, 6))
    for k in range(K):
        v = norm_back(gx[k], xhats[k], c1[k][:, 9:10])
        for j in range(K):
            v = v + c1[k][:, 1 + j : 2 + j] * g1[j]
        base_ref[k] = v


def turn_back(t, st, parts, s1, c2, cotangent, streams, c1, b1, mt, waits):
    rows, width = b1.shape
    block = (rows, K, width)
    return token_call(
        turn_kernel,
        "turn",
        t,
        (st,),
        (
            (parts, None),
            (s1, None),
            (c2, None),
            (cotangent, block),
            (streams, block),
            (c1, (K * rows, 128)),
            (b1, None),
            (mt, None),
        ),
        (
            ((K * rows, width), BF),
            ((2, K * rows, width), BF),
            ((K, rows, width), F32),
            ((parts.shape[0], rows, width), BF),
            ((2, 8, width), F32),
            ((2, 8, 128), F32),
        ),
        [],
        waits,
    )


def query_kernel(waits, place_ref, gb_ref, wo_ref, q_ref, own_ref, log_ref, same_ref, other_ref, trig_ref,
                 *refs):
    do_ref, gq_ref = refs[waits:]
    rows, cols = gq_ref.shape
    heads = cols // HEAD
    scale = HEAD ** (-0.5)
    grad = dot(gb_ref[...], wo_ref[...], NT).astype(BF)
    do_ref[0, 0:rows, :] = grad
    blocks = own_blocks(place_ref, own_ref, same_ref, other_ref)
    lag = key_after_query(rows, rows)
    inners, logs = [], []
    for h in range(heads):
        cut, vcut = head_cuts(cols, h)
        q, do = q_ref[:, cut], grad[:, cut]
        log = log_ref[:, cut]
        logs.append(log)
        probs, gps, inner = [], [], None
        for b, reach in blocks:
            s = jnp.where(lag <= reach, dot(b[:, cut], q, NT) * scale, -1e30)
            p = jnp.exp(s - log)
            gp = dot(b[:, vcut], do, NT)
            part = jnp.sum(p * gp, 0, keepdims=True)
            inner = part if inner is None else inner + part
            probs.append(p)
            gps.append(gp)
        gq = None
        for p, gp, (b, _) in zip(probs, gps, blocks):
            part = dot((p * (gp - inner)).astype(BF), b[:, cut], TN)
            gq = part if gq is None else gq + part
        gq_ref[:, cut] = turn(gq * scale, trig_ref[0], -trig_ref[1]).astype(BF)
        inners.append(inner)
    do_ref[0, rows:, :] = jnp.concatenate(
        [vector_rows(i, log) for i, log in zip(inners, logs)], 1
    ).astype(BF)
    copies(do_ref)


def query_back(place, gb1, wo, q, kv, log, same, other, trig, waits):
    rows, cols = q.shape
    args = (gb1, wo, q, kv, log, same, other, trig)
    outs = (((same.shape[0], rows + 16, cols), BF), ((rows, cols), BF))
    specs = [whole(v.shape) for v in args]
    specs[3] = own_block(kv)
    return pl.pallas_call(
        functools.partial(query_kernel, len(waits)),
        grid=(1,),
        out_shape=like(*outs),
        in_specs=[SMEM] + specs + [ANY] * len(waits),
        out_specs=[whole(s) for s, _ in outs],
        compiler_params=params(),
        cost_estimate=cost(5.5),
        name="query_back",
    )(place, *args, *waits)


def key_kernel(waits, place_ref, own_ref, qall_ref, same_ref, other_ref, gq_ref, trig_ref,
               wq_ref, wk_ref, wv_ref, gb_ref, at_ref, *refs):
    part_ref, *ship_refs = refs[waits:]
    rows, cols = gq_ref.shape
    small_ref = ship_refs[0].at[:, cols : 4 * cols]
    ship_refs[0][:, 0:cols] = at_ref[...]
    heads = cols // HEAD
    scale = HEAD ** (-0.5)
    me, core = device_index()
    own = place_ref[me]
    count = place_ref.shape[0]
    prompts = count // 2
    groups = [(g, rel) for g in range(count // 2) for rel in range(2)]
    reach = []
    for g, rel in groups:
        seg = place_ref[2 * g + (core + rel) % 2]
        full = (own < prompts) & (seg > own)
        value = jnp.where(full, 4096, jnp.where(seg == own, 0, -4096))
        reach.append(jnp.zeros((1, rows), jnp.int32) + value)
    reach = jnp.concatenate(reach, 1)
    lag = key_after_query(rows, rows)
    seen = jnp.concatenate([lag] * count, 1) <= reach
    for h in range(heads):
        cut, vcut = head_cuts(cols, h)
        k, v = own_ref[0, :, cut], own_ref[0, :, vcut]
        qs, dos, logs, inners = [], [], [], []
        for g, rel in groups:
            src = same_ref if rel == 0 else other_ref
            qs.append(qall_ref[2 * g + (core + rel) % 2, :, cut])
            dos.append(src[g, 0:rows, cut])
            inners.append(vector_of(src[g, rows:, cut], 0))
            logs.append(vector_of(src[g, rows:, cut], 1))
        qs, dos = jnp.concatenate(qs, 0), jnp.concatenate(dos, 0)
        logs, inners = jnp.concatenate(logs, 1), jnp.concatenate(inners, 1)
        s = jnp.where(seen, dot(k, qs, NT) * scale, -1e30)
        p = jnp.exp(s - logs)
        gp = dot(v, dos, NT)
        ds = (p * (gp - inners)).astype(BF)
        gv = dot(p.astype(BF), dos)
        gk = dot(ds, qs) * scale
        small_ref[:, vcut] = turn(gk, trig_ref[0], -trig_ref[1]).astype(BF)
        small_ref[:, 2 * cols + h * HEAD : 2 * cols + (h + 1) * HEAD] = gv.astype(BF)
    small_ref[:, 0:cols] = gq_ref[...]
    part = dot(gq_ref[...], wq_ref[...], NT)
    part += dot(small_ref[:, cols : 2 * cols], wk_ref[...], NT)
    part += dot(small_ref[:, 2 * cols :], wv_ref[...], NT)
    part_ref[...] = part.astype(BF)
    count = len(ship_refs)
    piece = gb_ref.shape[1] // count
    for i, ref in enumerate(ship_refs):
        if i:
            ref[:, 0 : 4 * cols] = ship_refs[0][:, 0 : 4 * cols]
        ref[:, 4 * cols :] = gb_ref[:, columns_for(i, count, piece)]


def key_back(place, kv, qall, same, other, gq, trig, wq, wk, wv, gb1, attended, count, waits):
    rows, cols = gq.shape
    width = wq.shape[0]
    args = (kv, qall, same, other, gq, trig, wq, wk, wv, gb1, attended)
    specs = [whole(v.shape) for v in args]
    specs[0] = own_block(kv)
    outs = (((rows, width), BF), *[((rows, 4 * cols + width // count), BF)] * count)
    return pl.pallas_call(
        functools.partial(key_kernel, len(waits)),
        grid=(1,),
        out_shape=like(*outs),
        in_specs=[SMEM] + specs + [ANY] * len(waits),
        out_specs=[whole(s) for s, _ in outs],
        compiler_params=params(),
        cost_estimate=cost(6.5),
        name="key_back",
    )(place, *args, *waits)


def last_kernel(t_ref, st_ref, parts_ref, base_ref, s_ref, c_ref, m_ref, dm_ref, ds_ref, out_ref, keep_ref, give_ref):
    gn = jnp.sum(parts_ref[...].astype(F32), 0)
    rows, width = gn.shape
    s0 = planes(s_ref[...])
    c1 = stream_coefs(c_ref, rows)
    taken = None
    for k in range(K):
        part = c1[k][:, 0:1] * s0[k]
        taken = part if taken is None else taken + part
    normed, rstd = norm_parts(taken)
    gt = norm_back(gn, normed, rstd)
    total, statics, out = None, [], []
    lane = iota((1, 128), 1)
    m = m_ref[0:1, 0, :]
    ctr = m - lmean(m)
    for k in range(K):
        g = lsum(gt * s0[k])
        th = c1[k][:, 0:1] - st_ref[0, k, 0]
        dz = g * (1.0 - th * th)
        xhat = (s0[k] - c1[k][:, 8:9]) * c1[k][:, 9:10]
        part = dz * xhat
        total = part if total is None else total + part
        v = base_ref[k] + c1[k][:, 0:1] * gt
        out.append((v + c1[k][:, 9:10] * dz * (ctr - xhat * lmean(m * xhat))).astype(BF))
        statics.append(jnp.where(lane == 0, jnp.sum(g, 0, keepdims=True), 0.0))
    out_ref[0] = unplanes(out)
    copies(out_ref)
    top = dm_ref[0] + jnp.concatenate(
        [jnp.sum(total, 0, keepdims=True), jnp.zeros((7, width), F32)], 0
    )
    statics = ds_ref[0] + jnp.concatenate(statics + [jnp.zeros((8 - K, 128), F32)], 0)
    bottom = dm_ref[1]
    core = lax.axis_index("core")
    blocks = keep_ref.shape[0] - 1
    nz = blocks // 2
    for yh in range(2):
        for z in range(nz):
            pair = []
            for i in range(2):
                at = ((z * 2 + yh) * 2 + i) * 128
                pair.append(jnp.concatenate([top[:, at : at + 128], bottom[:, at : at + 128]], 0))
            keep_ref[yh * nz + z] = jnp.where(core == 0, pair[0], pair[1])
            give_ref[yh * nz + z] = jnp.where(core == 0, pair[1], pair[0])
    both = jnp.concatenate([statics, ds_ref[1]], 0)
    keep_ref[blocks] = both
    give_ref[blocks] = both


def last(t, st, parts, base, streams, c1, mt, dm, ds, waits):
    peers, rows, width = parts.shape
    blocks = ((width // 256 + 1, 16, 128), F32)
    return token_call(
        last_kernel,
        "last",
        t,
        (st,),
        (
            (parts, None),
            (base, None),
            (streams, (rows, K, width)),
            (c1, (K * rows, 128)),
            (mt, None),
            (dm, None),
            (ds, None),
        ),
        (((peers, K * rows, width), BF), blocks, blocks),
        [],
        waits,
    )


def weight_kernel(picks, tile, count, gathered, waits, whole_sums, *refs):
    if whole_sums:
        *lefts, sum_ref = refs
        span = sum_ref.shape[3]
    else:
        *lefts, keep_ref, give_ref, hold_ref = refs
        span = keep_ref.shape[3]
    lefts = lefts[: len(lefts) - waits]
    rights = lefts[-1:] if gathered else lefts[-count:]
    lefts = lefts[: -len(rights)]
    units = len(picks)
    core, z = lax.axis_index("core"), lax.axis_index("z")
    mats = [
        jnp.concatenate([r[...] for r in lefts[i : i + count]], 0).T
        for i in range(0, len(lefts), count)
    ]
    part = 128
    kept = pl.ds(pl.multiple_of(core * part, part), part)
    given = pl.ds(pl.multiple_of((1 - core) * part, part), part)
    for f in range(span // tile):
        for u, pick in enumerate(picks):
            cut = slice((f * units + u) * tile, (f * units + u + 1) * tile)
            if gathered:
                right = [rights[0][lax.rem(z - i + count, count), :, cut] for i in range(count)]
            else:
                right = [r[:, cut] for r in rights]
            v = dot(mats[pick], jnp.concatenate(right, 0))
            to = slice(f * tile, (f + 1) * tile)
            if whole_sums:
                sum_ref[0, u, :, to] = v[0:part].astype(BF)
                sum_ref[1, u, :, to] = v[part:].astype(BF)
            else:
                hold_ref[f % 2] = v
                keep_ref[0, u, :, to] = hold_ref[f % 2, kept, :]
                give_ref[0, u, :, to] = hold_ref[f % 2, given, :].astype(BF)


def weight_part(lefts, right, tiles, picks, tile, name, us, waits=(), whole_sums=False):
    count = len(lefts[0][0])
    rows = lefts[0][0][0].shape[0]
    units = len(picks)
    gathered = not isinstance(right, (list, tuple))
    shape = (2, units, 128, tiles * tile)
    out = pl.BlockSpec((1, *shape[1:]), lambda y: (y, 0, 0, 0))
    outs, shapes = [out, out], like((shape, F32), (shape, BF))
    scratch = [pltpu.VMEM((2, 256, tile), F32)]
    if whole_sums:
        outs = pl.BlockSpec(shape, lambda y: (y, 0, 0, 0))
        shapes = jax.ShapeDtypeStruct((4, *shape[1:]), BF)
        scratch = []
    specs = [
        pl.BlockSpec((rows, 256), lambda y, o=o: (0, o + y)) for pieces, o in lefts for _ in pieces
    ]
    if gathered:
        specs.append(pl.BlockSpec((count, rows, units * tile * tiles), lambda y: (0, 0, 0)))
        right = [right]
    else:
        specs += [pl.BlockSpec((rows, units * tile * tiles), lambda y: (0, 0))] * count
    return pl.pallas_call(
        functools.partial(weight_kernel, picks, tile, count, gathered, len(waits), whole_sums),
        grid=(2,),
        in_specs=specs + [ANY] * len(waits),
        out_specs=outs,
        out_shape=shapes,
        scratch_shapes=scratch,
        compiler_params=params(),
        cost_estimate=cost(us),
        name=name,
    )(*[v for pieces, _ in lefts for v in pieces], *right, *waits)


def exchange(blocks, axes):
    return lax.all_to_all(blocks, axes, 0, 0, tiled=True)


def scatter_parts(partial, axes):
    n = lax.axis_size(axes)
    return exchange(partial.reshape(n, partial.shape[0] // n, partial.shape[1]), axes)


def swap(v, axis):
    return lax.ppermute(v, axis, [(0, 1), (1, 0)])


def along_z(pieces):
    n = lax.axis_size("z")
    return [pieces[0]] + [
        lax.ppermute(pieces[i], "z", [(a, (a + i) % n) for a in range(n)]) for i in range(1, n)
    ]


def pin(v, *waits):
    def body(*refs):
        pass

    return pl.pallas_call(
        body,
        out_shape=jax.ShapeDtypeStruct(v.shape, v.dtype),
        in_specs=[ANY] * (1 + len(waits)),
        out_specs=ANY,
        input_output_aliases={0: 0},
        name="pin",
    )(v, *waits)


def over_tensor(pair):
    half, _, rows, width = pair.shape
    return pl.BlockSpec(
        (half, 1, rows, width), lambda i, t: (0, jnp.abs(i - t[0] // half), 0, 0)
    )


def gathered_rows(blocks, t, wait):
    rows, width = blocks.shape[-2:]
    half = int(np.prod(blocks.shape[:-2])) // 2
    out = (half * rows // K, K, width)
    spec = pl.BlockSpec((half, rows, width), lambda i, t: (i, 0, 0))
    if blocks.ndim == 4:
        spec = over_tensor(blocks)

    def body(t_ref, in_ref, _, out_ref):
        out_ref[...] = in_ref[...].reshape(out)

    return pl.pallas_call(
        body,
        grid_spec=pltpu.PrefetchScalarGridSpec(
            num_scalar_prefetch=1,
            grid=(2,),
            in_specs=[spec, ANY],
            out_specs=pl.BlockSpec(out, lambda i, t: (i, 0, 0)),
        ),
        out_shape=jax.ShapeDtypeStruct((2 * out[0], *out[1:]), blocks.dtype),
        compiler_params=params(),
        cost_estimate=cost(2.6),
        name="rows",
    )(t, blocks, wait)


def to_each(v, axis):
    n = lax.axis_size(axis)
    return v + sum(lax.ppermute(v, axis, [(a, (a + i) % n) for a in range(n)]) for i in range(1, n))


def pick(v, at):
    return lax.dynamic_index_in_dim(v, at, 0, keepdims=False)


def over_core(kept, got):
    yh = lax.axis_index("yh")
    give = pick(kept, 1 - yh) + pick(got, 1 - yh).astype(F32)
    return pick(kept, yh) + pick(got, yh).astype(F32), give.astype(BF)


def per_device(streams, placement, w_query, w_key, w_value, w_output, w_gate, w_up, w_down,
               mix_dynamic, mix_static, cotangent):
    rows, _, width = streams.shape
    groups = placement.shape[0]
    t = lax.axis_index(TP).astype(jnp.int32)[None]
    nz = lax.axis_size("z")
    mt = jnp.transpose(mix_dynamic, (2, 0, 1))

    c1, q, kv, trig, *x_one = first(
        placement, mix_static, streams, mt, w_query, w_key, w_value, groups // 2, nz
    )
    same = exchange(kv, ("z", "yh"))
    other = swap(same, "core")
    attended, log, part_one, q = attend(placement, q, kv, same, other, w_output)
    qall = lax.all_gather(q, DP, axis=0)
    x_one = along_z(x_one)
    s1, b1, c2, pay = middle(
        t, mix_static, scatter_parts(part_one, TP), streams, c1, mt, x_one[1:]
    )
    pay = exchange(pay, TP).reshape(rows, width + 128)
    *xy, acts, part_two = feed(pay, cotangent, w_gate, w_up, w_down, nz)
    acts = lax.all_gather(acts, "z", axis=0)
    turned, pair, base, gb1, dm, ds = turn_back(
        t, mix_static, scatter_parts(part_two, TP), s1, c2, cotangent, streams, c1, b1, mt, (qall,)
    )
    turned = swap(turned, "yl")
    pair = lax.dynamic_update_slice(pair, turned[None], (1, 0, 0))
    gb1 = exchange(gb1, TP).reshape(rows, width)
    do, gq = query_back(placement, gb1, w_output, q, kv, log, same, other, trig, (pair,))
    pair = lax.all_gather(pin(pair, gb1), "x", axis=0)
    tiles = w_gate.shape[1] // FEED_TILE
    xy = along_z([pin(v, gq) for v in xy])
    do_same = exchange(do, ("z", "yh"))
    do_same = pin(do_same, *xy[1:])
    do_other = swap(do_same, "core")
    part_three, *ship = key_back(
        placement, kv, qall, do_same, do_other, gq, trig, w_query, w_key, w_value, gb1, attended, nz,
        (),
    )
    ff_keep, ff_give = weight_part(
        ((xy, 0), (xy, 2)), acts, tiles, (0, 0, 1), FEED_TILE, "feed_weights", 8, (part_three,)
    )
    ship = along_z(ship)
    gt, mix_keep, mix_give = last(
        t, mix_static, scatter_parts(part_three, TP), base, streams, c1, mt, dm, ds, (ff_keep,)
    )
    streams_out = gathered_rows(pair, t, mix_keep)
    gt = exchange(gt, TP)
    grad_streams = gathered_rows(gt, t, streams_out)
    ff_keep, ff_give = over_core(ff_keep, swap(ff_give, "core"))
    ff = ff_keep + swap(ff_give, "yh").astype(F32)
    v = mix_keep + swap(mix_give, "core")
    yh, z = lax.axis_index("yh"), lax.axis_index("z")

    def half(at):
        return jnp.concatenate([lax.dynamic_slice_in_dim(v, at * nz, nz, 0), v[2 * nz :]], 0)

    v = half(yh) + swap(half(1 - yh), "yh")
    mix_mid = v

    def mine(at):
        return jnp.stack([pick(v, lax.rem(at, nz)), v[nz]])

    v = sum(along_z([mine(z + i) for i in range(nz)]))
    v = to_each(to_each(v, "yl"), "x")
    grad_dynamic = jnp.transpose(v[0].reshape(2, 8, -1)[:, :6], (0, 2, 1))
    grad_static = v[1].reshape(2, 8, 128)[:, :4, :6]
    keep, give = weight_part(
        ((ship, 4), (x_one, 0)), ship, 1, (0, 1, 1, 1), 256, "tail_weights", 4, (mix_mid,)
    )
    keep, give = over_core(keep, swap(give, "core"))
    tail = keep + swap(give, "yh").astype(F32)

    return (
        streams_out,
        grad_streams,
        tail[1],
        tail[2],
        tail[3],
        jnp.transpose(tail[0]),
        ff[0],
        ff[1],
        jnp.transpose(ff[2]),
        grad_dynamic,
        grad_static,
    )


def solution(mesh):
    fine = Mesh(mesh.devices.reshape(4, 2, 2, 2, 4), ("z", "yh", "core", "yl", "x"))
    placed = (
        P(DP, None, None),
        P(),
        P(None, TP),
        P(None, TP),
        P(None, TP),
        P(TP, None),
        P(None, TP),
        P(None, TP),
        P(TP, None),
        P(),
        P(),
        P(DP, None, None),
    )
    return jax.shard_map(
        per_device,
        mesh=fine,
        in_specs=placed,
        out_specs=(
            P(DP, None, None),
            P(DP, None, None),
            P(DP, TP),
            P(DP, TP),
            P(DP, TP),
            P(TP, DP),
            P(DP, TP),
            P(DP, TP),
            P(TP, DP),
            P(None, DP, None),
            P(),
        ),
        check_vma=False,
    )
```

```python
import functools

import jax
import jax.numpy as jnp
import numpy as np
from jax import lax
from jax.experimental import pallas as pl
from jax.experimental.pallas import tpu as pltpu
from jax.sharding import Mesh
from jax.sharding import PartitionSpec as P

HEAD = 128
EPS = 1e-05
THETA = 10000.0
BF = jnp.bfloat16
F32 = jnp.float32
K = 4
DP = ("z", "yh", "core")
TP = ("yl", "x")
SMEM = pl.BlockSpec(memory_space=pltpu.SMEM)
ANY = pl.BlockSpec(memory_space=pl.ANY)
NT = (((1,), (1,)), ((), ()))
TN = (((0,), (0,)), ((), ()))
NN = (((1,), (0,)), ((), ()))


def dot(a, b, dims=NN):
    return lax.dot_general(a, b, dims, preferred_element_type=F32)


def lmean(v):
    return jnp.mean(v, -1, keepdims=True)


def lsum(v):
    return jnp.sum(v, -1, keepdims=True)


def norm_parts(v):
    ctr = v - lmean(v)
    rstd = lax.rsqrt(lmean(ctr * ctr) + EPS)
    return ctr * rstd, rstd


def norm_back(g, xhat, rstd):
    return rstd * (g - lmean(g) - xhat * lmean(g * xhat))


def three(v):
    hi = v.astype(BF)
    rest = v - hi.astype(F32)
    mid = rest.astype(BF)
    low = (rest - mid.astype(F32)).astype(BF)
    return hi, mid, low


def lanes(rows, pairs, start=None):
    lane = lax.broadcasted_iota(jnp.int32, (rows, 128), 1)
    out = jnp.zeros((rows, 128), F32) if start is None else start
    for at, v in pairs:
        out = jnp.where(lane == at, v, out)
    return out


def fold_parts(z):
    return z + pltpu.roll(z, 120, 1) + pltpu.roll(z, 112, 1)


def turn(v, cos, sin):
    return v * cos + pltpu.roll(v, 64, 1) * sin


def cost(us):
    return pl.CostEstimate(flops=0, bytes_accessed=int(us * 3.69e6), transcendentals=0)


def params():
    return pltpu.CompilerParams(vmem_limit_bytes=60 * 2**20)


def whole(shape):
    n = len(shape)
    return pl.BlockSpec(shape, lambda *_: (0,) * n)


def like(*shapes):
    return tuple(jax.ShapeDtypeStruct(s, d) for s, d in shapes)


def iota(shape, dim):
    return lax.broadcasted_iota(jnp.int32, shape, dim)


def order(rows, to_planes):
    count = rows // K
    a, b = iota((rows, rows), 0), iota((rows, rows), 1)
    if not to_planes:
        a, b = b, a
    return (a == (b % K) * count + b // K).astype(BF)


def planes(block):
    rows, _, width = block.shape
    v = dot(order(K * rows, True), block.reshape(K * rows, width))
    return [v[k * rows : (k + 1) * rows] for k in range(K)]


def unplanes(parts):
    rows = parts[0].shape[0]
    return dot(order(K * rows, False), jnp.concatenate(parts, 0)).astype(BF)


def stream_coefs(ref, rows):
    return [ref[pl.ds(k, rows, stride=K), :] for k in range(K)]


def static_rows(st_ref, layer, rows):
    row, lane = iota((rows, 128), 0) % K, iota((rows, 128), 1)
    out = jnp.zeros((rows, 128), F32)
    for k in range(K):
        for c in range(K + 2):
            out = jnp.where((row == k) & (lane == c), st_ref[layer, k, c], out)
    return out


def static_row(st_ref, layer, k):
    lane = iota((1, 128), 1)
    out = jnp.zeros((1, 128), F32)
    for c in range(K + 2):
        out = jnp.where(lane == c, st_ref[layer, k, c], out)
    return out


def fill_parts(m, wide_ref, mp_ref):
    cols = m.shape[0]
    wide_ref[...] = jnp.zeros_like(wide_ref)
    for i, v in enumerate(three(m)):
        wide_ref[8 * i : 8 * i + cols, :] = v.astype(F32)
    wide_ref[24:25, :] = jnp.ones((1, m.shape[1]), F32)
    mp_ref[...] = jnp.zeros_like(mp_ref)
    mp_ref[0:32, :] = wide_ref[...].astype(BF)


def columns_for(step, count, piece):
    at = lax.rem(lax.axis_index("z") + step, count) * piece
    return pl.ds(pl.multiple_of(at, piece), piece)


def copies(ref):
    for i in range(1, ref.shape[0]):
        ref[i] = ref[0]


def device_index():
    core = lax.axis_index("core")
    return (lax.axis_index("z") * 2 + lax.axis_index("yh")) * 2 + core, core


def first_kernel(place_ref, st_ref, freq_ref, s_ref, m_ref, wq_ref, wk_ref, wv_ref,
                 c_ref, q_ref, kv_ref, trig_ref, *refs):
    *x_refs, n_ref, wide_ref, mp_ref = refs
    rows, _, width = s_ref.shape
    fill_parts(m_ref[:, 0, :], wide_ref, mp_ref)
    sums = fold_parts(dot(jnp.ones((16, width), BF), mp_ref[...], NT))[0:1]
    step = 32
    part = K * step
    static = static_rows(st_ref, 0, part)
    row, lane = iota((part, 128), 0), iota((part, 128), 1)
    mine = (lane % step) == row // K

    def body(i, carry):
        r = pl.multiple_of(i * step, step)
        low = s_ref[pl.ds(r, step)].reshape(part, width)
        z = dot(low, mp_ref[...], NT)
        s = low.astype(F32)
        mean = z[:, 24:25] * (1.0 / width)
        ctr = s - mean
        rstd = lax.rsqrt(lmean(ctr * ctr) + EPS)
        c = static + jnp.tanh(rstd * (fold_parts(z) - mean * sums))
        c_ref[pl.ds(pl.multiple_of(i * part, part), part), :] = lanes(part, ((8, mean), (9, rstd)), c)
        a, b, d = (v.astype(F32) for v in three(c[:, 0:1]))
        take = jnp.where(lane < step, a, jnp.where(lane < 2 * step, b, d))
        take = jnp.where(mine & (lane < 3 * step), take, 0.0).astype(BF)
        w = dot(take, low, TN)
        taken = w[0:step] + w[step : 2 * step] + w[2 * step : 3 * step]
        n_ref[pl.ds(r, step), :] = norm_parts(taken)[0].astype(BF)
        return carry

    lax.fori_loop(0, rows // step, body, 0, unroll=True)
    piece = width // len(x_refs)
    for i, ref in enumerate(x_refs):
        ref[...] = n_ref[:, columns_for(i, len(x_refs), piece)]
    me, _ = device_index()
    prompts = place_ref.shape[0] // 2
    start = jnp.minimum(place_ref[me], prompts) * rows
    angle = (start + iota((rows, HEAD), 0)).astype(F32) * freq_ref[...]
    cos = jnp.cos(angle)
    sin = jnp.where(iota((rows, HEAD), 1) < HEAD // 2, -1.0, 1.0) * jnp.sin(angle)
    trig_ref[0] = cos
    trig_ref[1] = sin
    normed = n_ref[...]
    q = dot(normed, wq_ref[...])
    k = dot(normed, wk_ref[...])
    heads = q.shape[1] // HEAD
    for h in range(heads):
        cut = slice(h * HEAD, (h + 1) * HEAD)
        q_ref[:, cut] = turn(q[:, cut], cos, sin).astype(BF)
        kv_ref[0, :, cut] = turn(k[:, cut], cos, sin).astype(BF)
    kv_ref[0, :, heads * HEAD :] = dot(normed, wv_ref[...]).astype(BF)
    copies(kv_ref)


def first(place, st, streams, mt, wq, wk, wv, chips, count):
    rows, _, width = streams.shape
    cols = wq.shape[1]
    half = HEAD // 2
    freq = np.float32(THETA) ** (-np.arange(half, dtype=np.float32) / np.float32(half))
    freq = jnp.asarray(np.concatenate([freq, freq])[None].astype(np.float32))
    outs = (
        ((K * rows, 128), F32),
        ((rows, cols), BF),
        ((chips, rows, 2 * cols), BF),
        ((2, rows, HEAD), F32),
        *[((rows, width // count), BF)] * count,
    )
    return pl.pallas_call(
        first_kernel,
        grid=(1,),
        out_shape=like(*outs),
        in_specs=[SMEM, SMEM, whole(freq.shape), whole(streams.shape),
                  whole(mt.shape),
                  whole(wq.shape), whole(wk.shape), whole(wv.shape)],
        out_specs=[whole(s) for s, _ in outs],
        scratch_shapes=[
            pltpu.VMEM((rows, width), BF),
            pltpu.VMEM((32, width), F32),
            pltpu.VMEM((128, width), BF),
        ],
        compiler_params=params(),
        cost_estimate=cost(10),
        name="first",
    )(place, st, freq, streams, mt, wq, wk, wv)


def own_blocks(place_ref, own_ref, same_ref, other_ref):
    me, core = device_index()
    own = place_ref[me]
    count = place_ref.shape[0]
    prompts = count // 2
    is_cont = own >= prompts
    blocks = []
    for s in range(prompts):
        d = jnp.int32(0)
        for a in range(count):
            d = jnp.where(place_ref[a] == s, a, d)
        block = jnp.where((d % 2) == core, same_ref[d // 2], other_ref[d // 2])
        reach = jnp.where(is_cont | (s < own), 4096, jnp.where(s == own, 0, -4096))
        blocks.append((block, reach))
    blocks.append((own_ref[0], jnp.where(is_cont, 0, -4096)))
    return blocks


def key_after_query(keys, queries):
    return iota((keys, queries), 0) - iota((keys, queries), 1)


def vector_rows(*vectors):
    row = iota((16, vectors[0].shape[1]), 0)
    out = jnp.zeros(row.shape, F32)
    for i, v in enumerate(vectors):
        for n, p in enumerate(three(v)):
            out = jnp.where(row == 3 * i + n, p.astype(F32), out)
    return out


def vector_of(rows16, i):
    v = rows16.astype(F32)
    return v[3 * i : 3 * i + 1] + v[3 * i + 1 : 3 * i + 2] + v[3 * i + 2 : 3 * i + 3]


def head_cuts(cols, h):
    return [slice(i * cols + h * HEAD, i * cols + (h + 1) * HEAD) for i in (0, 1)]


def attend_kernel(place_ref, q_ref, own_ref, same_ref, other_ref, wo_ref, at_ref, log_ref, part_ref, qcopy_ref):
    rows, cols = at_ref.shape
    heads = cols // HEAD
    scale = HEAD ** (-0.5)
    blocks = own_blocks(place_ref, own_ref, same_ref, other_ref)
    lag = key_after_query(rows, rows)
    logs = []
    for h in range(heads):
        cut, vcut = head_cuts(cols, h)
        q = q_ref[:, cut]
        scores = [
            jnp.where(lag <= reach, dot(b[:, cut], q, NT) * scale, -1e30) for b, reach in blocks
        ]
        top = functools.reduce(jnp.maximum, [jnp.max(s, 0, keepdims=True) for s in scores])
        terms = [jnp.exp(s - top) for s in scores]
        total = functools.reduce(jnp.add, [jnp.sum(e, 0, keepdims=True) for e in terms])
        inv = 1.0 / total
        out = None
        for e, (b, _) in zip(terms, blocks):
            o = dot((e * inv).astype(BF), b[:, vcut], TN)
            out = o if out is None else out + o
        at_ref[:, cut] = out.astype(BF)
        logs.append(top + jnp.log(total))
    log_ref[...] = jnp.concatenate(logs, 1)
    qcopy_ref[...] = q_ref[...]
    part_ref[...] = dot(at_ref[...], wo_ref[...]).astype(BF)


def own_block(kv):
    return pl.BlockSpec((1, *kv.shape[1:]), lambda i: (0, 0, 0))


def attend(place, q, kv, same, other, wo):
    rows, cols = q.shape
    args = (q, kv, same, other, wo)
    outs = (((rows, cols), BF), ((1, cols), F32), ((rows, wo.shape[1]), BF), ((rows, cols), BF))
    return pl.pallas_call(
        attend_kernel,
        grid=(1,),
        out_shape=like(*outs),
        in_specs=[SMEM, whole(q.shape), own_block(kv)] + [whole(v.shape) for v in args[2:]],
        out_specs=[whole(s) for s, _ in outs],
        compiler_params=params(),
        cost_estimate=cost(4.5),
        name="attend",
    )(place, *args)


def middle_kernel(t_ref, st_ref, parts_ref, s_ref, c_ref, m_ref, s1_ref, b1_ref, c2_ref, pay_ref,
                  wide_ref, mp_ref, split_ref):
    fill_parts(m_ref[:, 1, :], wide_ref, mp_ref)
    b1 = jnp.sum(parts_ref[...].astype(F32), 0)
    b1_ref[...] = b1
    rows, width = b1.shape
    s0 = planes(s_ref[...])
    c1 = stream_coefs(c_ref, rows)
    stats = []
    for j in range(K):
        v = c1[j][:, 5:6] * b1
        for k in range(K):
            v = v + c1[k][:, 1 + j : 2 + j] * s0[k]
        s1_ref[j] = v
        mean = lmean(v)
        ctr = v - mean
        stats.append((mean, lax.rsqrt(lmean(ctr * ctr) + EPS)))
        hi = ctr.astype(BF)
        split_ref[j * rows : (j + 1) * rows, :] = hi
        split_ref[(K + j) * rows : (K + j + 1) * rows, :] = (ctr - hi.astype(F32)).astype(BF)
    z = dot(split_ref[...], mp_ref[...], NT)
    taken, gives = None, []
    for j in range(K):
        mean, rstd = stats[j]
        zj = z[j * rows : (j + 1) * rows] + z[(K + j) * rows : (K + j + 1) * rows]
        c = static_row(st_ref, 1, j) + jnp.tanh(rstd * fold_parts(zj))
        c2_ref[j] = lanes(rows, ((8, mean), (9, rstd)), c)
        part = c[:, 0:1] * s1_ref[j]
        taken = part if taken is None else taken + part
        gives += [(4 * i + j, v.astype(F32)) for i, v in enumerate(three(c[:, 5:6]))]
    pay_ref[0, :, 0:width] = norm_parts(taken)[0].astype(BF)
    pay_ref[0, :, width:] = lanes(rows, gives).astype(BF)
    copies(pay_ref)


def token_call(kernel, name, t, tables, args, outs, scratch, waits=()):
    count = 1 + len(tables) + len(args)

    def body(*refs):
        kernel(*refs[:count], *refs[count + len(waits) :])

    in_specs = [SMEM] * len(tables)
    for v, block in args:
        if block is None:
            in_specs.append(pl.BlockSpec(v.shape, lambda i, t, n=v.ndim: (0,) * n))
        else:
            in_specs.append(pl.BlockSpec(block, lambda i, t, n=v.ndim: (t[0],) + (0,) * (n - 1)))
    return pl.pallas_call(
        body,
        grid_spec=pltpu.PrefetchScalarGridSpec(
            num_scalar_prefetch=1,
            grid=(1,),
            in_specs=in_specs + [ANY] * len(waits),
            out_specs=[pl.BlockSpec(s, lambda i, t, n=len(s): (0,) * n) for s, _ in outs],
            scratch_shapes=scratch,
        ),
        out_shape=like(*outs),
        compiler_params=params(),
        cost_estimate=cost(4),
        name=name,
    )(t, *tables, *[v for v, _ in args], *waits)


def middle(t, st, parts, streams, c1, mt, waits):
    peers, rows, width = parts.shape
    return token_call(
        middle_kernel,
        "middle",
        t,
        (st,),
        (
            (parts, None),
            (streams, (rows, K, width)),
            (c1, (K * rows, 128)),
            (mt, None),
        ),
        (
            ((K, rows, width), F32),
            ((rows, width), F32),
            ((K, rows, 128), F32),
            ((peers, rows, width + 128), BF),
        ),
        [
            pltpu.VMEM((32, width), F32),
            pltpu.VMEM((128, width), BF),
            pltpu.VMEM((2 * K * rows, width), BF),
        ],
        waits,
    )


def feed_kernel(pay_ref, cot_ref, wg_ref, wu_ref, wd_ref, *refs):
    *xy_refs, acts_ref, out_ref, gb_ref, b_ref, l_ref = refs
    step, steps = pl.program_id(0), pl.num_programs(0)
    rows, width = gb_ref.shape
    count = len(xy_refs) // 2
    piece = width // count

    @pl.when(step == 0)
    def _():
        chunk = 32
        row, lane = iota((chunk, K * chunk), 0), iota((chunk, K * chunk), 1)

        def body(i, carry):
            r = pl.multiple_of(i * chunk, chunk)
            give = pay_ref[pl.ds(r, chunk), width:].astype(F32)
            block = cot_ref[pl.ds(r, chunk)].reshape(K * chunk, width)
            total = None
            for n in range(3):
                w = jnp.zeros((chunk, K * chunk), F32)
                for j in range(K):
                    w = jnp.where(lane == K * row + j, give[:, K * n + j : K * n + j + 1], w)
                part = dot(w.astype(BF), block)
                total = part if total is None else total + part
            gb_ref[pl.ds(r, chunk), :] = total.astype(BF)
            return carry

        lax.fori_loop(0, rows // chunk, body, 0, unroll=True)
        for i in range(count):
            at = columns_for(i, count, piece)
            xy_refs[i][...] = pay_ref[:, at]
            xy_refs[count + i][...] = gb_ref[:, at]
        b_ref[...] = jnp.zeros_like(b_ref)
        l_ref[...] = jnp.zeros_like(l_ref)

    normed = pay_ref[:, 0:width]
    gate = dot(normed, wg_ref[...])
    up = dot(normed, wu_ref[...])
    sig = 1.0 / (1.0 + jnp.exp(-gate))
    silu = gate * sig
    hidden = (silu * up).astype(BF)
    grad = dot(gb_ref[...], wd_ref[...], NT)
    grad_gate = (grad * up * (sig * (1.0 + gate * (1.0 - sig)))).astype(BF)
    grad_up = (grad * silu).astype(BF)
    tile = hidden.shape[1]
    acts_ref[:, 0:tile] = grad_gate
    acts_ref[:, tile : 2 * tile] = grad_up
    acts_ref[:, 2 * tile :] = hidden
    b_ref[...] += dot(hidden, wd_ref[...])
    l_ref[...] += dot(grad_gate, wg_ref[...], NT) + dot(grad_up, wu_ref[...], NT)

    @pl.when(step == steps - 1)
    def _():
        out_ref[:, 0:width] = b_ref[...].astype(BF)
        out_ref[:, width:] = l_ref[...].astype(BF)


FEED_TILE = 256


def feed(pay, cotangent, wg, wu, wd, count):
    rows, _, width = cotangent.shape
    hidden = wg.shape[1]
    tile = FEED_TILE
    xy = (rows, width // count)
    return pl.pallas_call(
        feed_kernel,
        grid=(hidden // tile,),
        in_specs=[
            whole(pay.shape),
            whole(cotangent.shape),
            pl.BlockSpec((width, tile), lambda f: (0, f)),
            pl.BlockSpec((width, tile), lambda f: (0, f)),
            pl.BlockSpec((tile, width), lambda f: (f, 0)),
        ],
        out_specs=[
            *[whole(xy)] * (2 * count),
            pl.BlockSpec((rows, 3 * tile), lambda f: (0, f)),
            whole((rows, 2 * width)),
        ],
        out_shape=like(
            *[(xy, BF)] * (2 * count),
            ((rows, 3 * hidden), BF),
            ((rows, 2 * width), BF),
        ),
        scratch_shapes=[
            pltpu.VMEM((rows, width), BF),
            pltpu.VMEM((rows, width), F32),
            pltpu.VMEM((rows, width), F32),
        ],
        compiler_params=params(),
        cost_estimate=cost(14),
        name="feed",
    )(pay, cotangent, wg, wu, wd)


def coef_back(grads, coefs, st_ref, layer, m, xhats, dm_ref, ds_ref, columns):
    rows = xhats[0].shape[0]
    dzs, statics = [], []
    for k in range(K):
        g = lanes(rows, grads[k].items())
        th = coefs[k] - static_row(st_ref, layer, k)
        dzs.append(g * (1.0 - th * th))
        statics.append(jnp.sum(g, 0, keepdims=True))
    ds_ref[layer] = jnp.concatenate(statics + [jnp.zeros((8 - K, 128), F32)], 0)
    for c in range(8):
        if c in columns:
            v = None
            for k in range(K):
                part = dzs[k][:, c : c + 1] * xhats[k]
                v = part if v is None else v + part
            dm_ref[layer, c : c + 1, :] = jnp.sum(v, 0, keepdims=True)
        else:
            dm_ref[layer, c : c + 1, :] = jnp.zeros((1, xhats[0].shape[1]), F32)
    out = []
    for k in range(K):
        v = None
        for c in columns:
            part = dzs[k][:, c : c + 1] * m[c : c + 1, :]
            v = part if v is None else v + part
        out.append(v)
    return out


def turn_kernel(t_ref, st_ref, parts_ref, s1_ref, c2_ref, cot_ref, s_ref, c1_ref, b1_ref, m_ref,
                own_ref, pair_ref, base_ref, gb1_ref, dm_ref, ds_ref):
    rows, width = b1_ref.shape
    both = jnp.sum(parts_ref[...].astype(F32), 0)
    b2, gn = both[:, 0:width], both[:, width:]
    s1 = [s1_ref[k] for k in range(K)]
    c2 = [c2_ref[k] for k in range(K)]
    g2 = planes(cot_ref[...])
    grads = [dict() for _ in range(K)]
    taken, s2 = None, []
    for j in range(K):
        v = c2[j][:, 5:6] * b2
        for k in range(K):
            v = v + c2[k][:, 1 + j : 2 + j] * s1[k]
        s2.append(v.astype(BF))
        grads[j][5] = lsum(g2[j] * b2)
        for k in range(K):
            grads[k][1 + j] = lsum(g2[j] * s1[k])
        part = c2[j][:, 0:1] * s1[j]
        taken = part if taken is None else taken + part
    s2 = unplanes(s2)
    own_ref[...] = s2
    pair_ref[0] = s2
    normed, rstd = norm_parts(taken)
    gt = norm_back(gn, normed, rstd)
    for k in range(K):
        grads[k][0] = lsum(gt * s1[k])
    xhats = [(s1[k] - c2[k][:, 8:9]) * c2[k][:, 9:10] for k in range(K)]
    gx = coef_back(grads, c2, st_ref, 1, m_ref[:, 1, :], xhats, dm_ref, ds_ref, range(6))
    g1 = []
    for k in range(K):
        v = c2[k][:, 0:1] * gt + norm_back(gx[k], xhats[k], c2[k][:, 9:10])
        for j in range(K):
            v = v + c2[k][:, 1 + j : 2 + j] * g2[j]
        g1.append(v)
    c1 = stream_coefs(c1_ref, rows)
    b1 = b1_ref[...]
    s0 = planes(s_ref[...])
    gb1 = None
    grads = [dict() for _ in range(K)]
    for j in range(K):
        part = c1[j][:, 5:6] * g1[j]
        gb1 = part if gb1 is None else gb1 + part
        grads[j][5] = lsum(g1[j] * b1)
        for k in range(K):
            grads[k][1 + j] = lsum(g1[j] * s0[k])
    gb1_ref[0] = gb1.astype(BF)
    copies(gb1_ref)
    xhats = [(s0[k] - c1[k][:, 8:9]) * c1[k][:, 9:10] for k in range(K)]
    gx = coef_back(grads, c1, st_ref, 0, m_ref[:, 0, :], xhats, dm_ref, ds_ref, range(1, 6))
    for k in range(K):
        v = norm_back(gx[k], xhats[k], c1[k][:, 9:10])
        for j in range(K):
            v = v + c1[k][:, 1 + j : 2 + j] * g1[j]
        base_ref[k] = v


def turn_back(t, st, parts, s1, c2, cotangent, streams, c1, b1, mt, waits):
    rows, width = b1.shape
    block = (rows, K, width)
    return token_call(
        turn_kernel,
        "turn",
        t,
        (st,),
        (
            (parts, None),
            (s1, None),
            (c2, None),
            (cotangent, block),
            (streams, block),
            (c1, (K * rows, 128)),
            (b1, None),
            (mt, None),
        ),
        (
            ((K * rows, width), BF),
            ((2, K * rows, width), BF),
            ((K, rows, width), F32),
            ((parts.shape[0], rows, width), BF),
            ((2, 8, width), F32),
            ((2, 8, 128), F32),
        ),
        [],
        waits,
    )


def query_kernel(waits, place_ref, gb_ref, wo_ref, q_ref, own_ref, log_ref, same_ref, other_ref, trig_ref,
                 *refs):
    do_ref, gq_ref = refs[waits:]
    rows, cols = gq_ref.shape
    heads = cols // HEAD
    scale = HEAD ** (-0.5)
    grad = dot(gb_ref[...], wo_ref[...], NT).astype(BF)
    do_ref[0, 0:rows, :] = grad
    blocks = own_blocks(place_ref, own_ref, same_ref, other_ref)
    lag = key_after_query(rows, rows)
    inners, logs = [], []
    for h in range(heads):
        cut, vcut = head_cuts(cols, h)
        q, do = q_ref[:, cut], grad[:, cut]
        log = log_ref[:, cut]
        logs.append(log)
        probs, gps, inner = [], [], None
        for b, reach in blocks:
            s = jnp.where(lag <= reach, dot(b[:, cut], q, NT) * scale, -1e30)
            p = jnp.exp(s - log)
            gp = dot(b[:, vcut], do, NT)
            part = jnp.sum(p * gp, 0, keepdims=True)
            inner = part if inner is None else inner + part
            probs.append(p)
            gps.append(gp)
        gq = None
        for p, gp, (b, _) in zip(probs, gps, blocks):
            part = dot((p * (gp - inner)).astype(BF), b[:, cut], TN)
            gq = part if gq is None else gq + part
        gq_ref[:, cut] = turn(gq * scale, trig_ref[0], -trig_ref[1]).astype(BF)
        inners.append(inner)
    do_ref[0, rows:, :] = jnp.concatenate(
        [vector_rows(i, log) for i, log in zip(inners, logs)], 1
    ).astype(BF)
    copies(do_ref)


def query_back(place, gb1, wo, q, kv, log, same, other, trig, waits):
    rows, cols = q.shape
    args = (gb1, wo, q, kv, log, same, other, trig)
    outs = (((same.shape[0], rows + 16, cols), BF), ((rows, cols), BF))
    specs = [whole(v.shape) for v in args]
    specs[3] = own_block(kv)
    return pl.pallas_call(
        functools.partial(query_kernel, len(waits)),
        grid=(1,),
        out_shape=like(*outs),
        in_specs=[SMEM] + specs + [ANY] * len(waits),
        out_specs=[whole(s) for s, _ in outs],
        compiler_params=params(),
        cost_estimate=cost(5.5),
        name="query_back",
    )(place, *args, *waits)


def key_kernel(waits, place_ref, own_ref, qall_ref, same_ref, other_ref, gq_ref, trig_ref,
               wq_ref, wk_ref, wv_ref, gb_ref, at_ref, *refs):
    part_ref, *ship_refs = refs[waits:]
    rows, cols = gq_ref.shape
    small_ref = ship_refs[0].at[:, cols : 4 * cols]
    ship_refs[0][:, 0:cols] = at_ref[...]
    heads = cols // HEAD
    scale = HEAD ** (-0.5)
    me, core = device_index()
    own = place_ref[me]
    count = place_ref.shape[0]
    prompts = count // 2
    groups = [(g, rel) for g in range(count // 2) for rel in range(2)]
    reach = []
    for g, rel in groups:
        seg = place_ref[2 * g + (core + rel) % 2]
        full = (own < prompts) & (seg > own)
        value = jnp.where(full, 4096, jnp.where(seg == own, 0, -4096))
        reach.append(jnp.zeros((1, rows), jnp.int32) + value)
    reach = jnp.concatenate(reach, 1)
    lag = key_after_query(rows, rows)
    seen = jnp.concatenate([lag] * count, 1) <= reach
    for h in range(heads):
        cut, vcut = head_cuts(cols, h)
        k, v = own_ref[0, :, cut], own_ref[0, :, vcut]
        qs, dos, logs, inners = [], [], [], []
        for g, rel in groups:
            src = same_ref if rel == 0 else other_ref
            qs.append(qall_ref[2 * g + (core + rel) % 2, :, cut])
            dos.append(src[g, 0:rows, cut])
            inners.append(vector_of(src[g, rows:, cut], 0))
            logs.append(vector_of(src[g, rows:, cut], 1))
        qs, dos = jnp.concatenate(qs, 0), jnp.concatenate(dos, 0)
        logs, inners = jnp.concatenate(logs, 1), jnp.concatenate(inners, 1)
        s = jnp.where(seen, dot(k, qs, NT) * scale, -1e30)
        p = jnp.exp(s - logs)
        gp = dot(v, dos, NT)
        ds = (p * (gp - inners)).astype(BF)
        gv = dot(p.astype(BF), dos)
        gk = dot(ds, qs) * scale
        small_ref[:, vcut] = turn(gk, trig_ref[0], -trig_ref[1]).astype(BF)
        small_ref[:, 2 * cols + h * HEAD : 2 * cols + (h + 1) * HEAD] = gv.astype(BF)
    small_ref[:, 0:cols] = gq_ref[...]
    part = dot(gq_ref[...], wq_ref[...], NT)
    part += dot(small_ref[:, cols : 2 * cols], wk_ref[...], NT)
    part += dot(small_ref[:, 2 * cols :], wv_ref[...], NT)
    part_ref[...] = part.astype(BF)
    count = len(ship_refs)
    piece = gb_ref.shape[1] // count
    for i, ref in enumerate(ship_refs):
        if i:
            ref[:, 0 : 4 * cols] = ship_refs[0][:, 0 : 4 * cols]
        ref[:, 4 * cols :] = gb_ref[:, columns_for(i, count, piece)]


def key_back(place, kv, qall, same, other, gq, trig, wq, wk, wv, gb1, attended, count, waits):
    rows, cols = gq.shape
    width = wq.shape[0]
    args = (kv, qall, same, other, gq, trig, wq, wk, wv, gb1, attended)
    specs = [whole(v.shape) for v in args]
    specs[0] = own_block(kv)
    outs = (((rows, width), BF), *[((rows, 4 * cols + width // count), BF)] * count)
    return pl.pallas_call(
        functools.partial(key_kernel, len(waits)),
        grid=(1,),
        out_shape=like(*outs),
        in_specs=[SMEM] + specs + [ANY] * len(waits),
        out_specs=[whole(s) for s, _ in outs],
        compiler_params=params(),
        cost_estimate=cost(6.5),
        name="key_back",
    )(place, *args, *waits)


def last_kernel(t_ref, st_ref, parts_ref, base_ref, s_ref, c_ref, m_ref, dm_ref, ds_ref, out_ref, keep_ref, give_ref):
    gn = jnp.sum(parts_ref[...].astype(F32), 0)
    rows, width = gn.shape
    s0 = planes(s_ref[...])
    c1 = stream_coefs(c_ref, rows)
    taken = None
    for k in range(K):
        part = c1[k][:, 0:1] * s0[k]
        taken = part if taken is None else taken + part
    normed, rstd = norm_parts(taken)
    gt = norm_back(gn, normed, rstd)
    total, statics, out = None, [], []
    lane = iota((1, 128), 1)
    m = m_ref[0:1, 0, :]
    ctr = m - lmean(m)
    for k in range(K):
        g = lsum(gt * s0[k])
        th = c1[k][:, 0:1] - st_ref[0, k, 0]
        dz = g * (1.0 - th * th)
        xhat = (s0[k] - c1[k][:, 8:9]) * c1[k][:, 9:10]
        part = dz * xhat
        total = part if total is None else total + part
        v = base_ref[k] + c1[k][:, 0:1] * gt
        out.append((v + c1[k][:, 9:10] * dz * (ctr - xhat * lmean(m * xhat))).astype(BF))
        statics.append(jnp.where(lane == 0, jnp.sum(g, 0, keepdims=True), 0.0))
    out_ref[0] = unplanes(out)
    copies(out_ref)
    top = dm_ref[0] + jnp.concatenate(
        [jnp.sum(total, 0, keepdims=True), jnp.zeros((7, width), F32)], 0
    )
    statics = ds_ref[0] + jnp.concatenate(statics + [jnp.zeros((8 - K, 128), F32)], 0)
    bottom = dm_ref[1]
    core = lax.axis_index("core")
    blocks = keep_ref.shape[0] - 1
    nz = blocks // 2
    for yh in range(2):
        for z in range(nz):
            pair = []
            for i in range(2):
                at = ((z * 2 + yh) * 2 + i) * 128
                pair.append(jnp.concatenate([top[:, at : at + 128], bottom[:, at : at + 128]], 0))
            keep_ref[yh * nz + z] = jnp.where(core == 0, pair[0], pair[1])
            give_ref[yh * nz + z] = jnp.where(core == 0, pair[1], pair[0])
    both = jnp.concatenate([statics, ds_ref[1]], 0)
    keep_ref[blocks] = both
    give_ref[blocks] = both


def last(t, st, parts, base, streams, c1, mt, dm, ds, waits):
    peers, rows, width = parts.shape
    blocks = ((width // 256 + 1, 16, 128), F32)
    return token_call(
        last_kernel,
        "last",
        t,
        (st,),
        (
            (parts, None),
            (base, None),
            (streams, (rows, K, width)),
            (c1, (K * rows, 128)),
            (mt, None),
            (dm, None),
            (ds, None),
        ),
        (((peers, K * rows, width), BF), blocks, blocks),
        [],
        waits,
    )


def weight_kernel(picks, tile, count, gathered, waits, whole_sums, *refs):
    if whole_sums:
        *lefts, sum_ref = refs
        span = sum_ref.shape[3]
    else:
        *lefts, keep_ref, give_ref, hold_ref = refs
        span = keep_ref.shape[3]
    lefts = lefts[: len(lefts) - waits]
    rights = lefts[-1:] if gathered else lefts[-count:]
    lefts = lefts[: -len(rights)]
    units = len(picks)
    core, z = lax.axis_index("core"), lax.axis_index("z")
    mats = [
        jnp.concatenate([r[...] for r in lefts[i : i + count]], 0).T
        for i in range(0, len(lefts), count)
    ]
    part = 128
    kept = pl.ds(pl.multiple_of(core * part, part), part)
    given = pl.ds(pl.multiple_of((1 - core) * part, part), part)
    for f in range(span // tile):
        for u, pick in enumerate(picks):
            cut = slice((f * units + u) * tile, (f * units + u + 1) * tile)
            if gathered:
                right = [rights[0][lax.rem(z - i + count, count), :, cut] for i in range(count)]
            else:
                right = [r[:, cut] for r in rights]
            v = dot(mats[pick], jnp.concatenate(right, 0))
            to = slice(f * tile, (f + 1) * tile)
            if whole_sums:
                sum_ref[0, u, :, to] = v[0:part].astype(BF)
                sum_ref[1, u, :, to] = v[part:].astype(BF)
            else:
                hold_ref[f % 2] = v
                keep_ref[0, u, :, to] = hold_ref[f % 2, kept, :]
                give_ref[0, u, :, to] = hold_ref[f % 2, given, :].astype(BF)


def weight_part(lefts, right, tiles, picks, tile, name, us, waits=(), whole_sums=False):
    count = len(lefts[0][0])
    rows = lefts[0][0][0].shape[0]
    units = len(picks)
    gathered = not isinstance(right, (list, tuple))
    shape = (2, units, 128, tiles * tile)
    out = pl.BlockSpec((1, *shape[1:]), lambda y: (y, 0, 0, 0))
    outs, shapes = [out, out], like((shape, F32), (shape, BF))
    scratch = [pltpu.VMEM((2, 256, tile), F32)]
    if whole_sums:
        outs = pl.BlockSpec(shape, lambda y: (y, 0, 0, 0))
        shapes = jax.ShapeDtypeStruct((4, *shape[1:]), BF)
        scratch = []
    specs = [
        pl.BlockSpec((rows, 256), lambda y, o=o: (0, o + y)) for pieces, o in lefts for _ in pieces
    ]
    if gathered:
        specs.append(pl.BlockSpec((count, rows, units * tile * tiles), lambda y: (0, 0, 0)))
        right = [right]
    else:
        specs += [pl.BlockSpec((rows, units * tile * tiles), lambda y: (0, 0))] * count
    return pl.pallas_call(
        functools.partial(weight_kernel, picks, tile, count, gathered, len(waits), whole_sums),
        grid=(2,),
        in_specs=specs + [ANY] * len(waits),
        out_specs=outs,
        out_shape=shapes,
        scratch_shapes=scratch,
        compiler_params=params(),
        cost_estimate=cost(us),
        name=name,
    )(*[v for pieces, _ in lefts for v in pieces], *right, *waits)


def exchange(blocks, axes):
    return lax.all_to_all(blocks, axes, 0, 0, tiled=True)


def scatter_parts(partial, axes):
    n = lax.axis_size(axes)
    return exchange(partial.reshape(n, partial.shape[0] // n, partial.shape[1]), axes)


def swap(v, axis):
    return lax.ppermute(v, axis, [(0, 1), (1, 0)])


def along_z(pieces):
    n = lax.axis_size("z")
    return [pieces[0]] + [
        lax.ppermute(pieces[i], "z", [(a, (a + i) % n) for a in range(n)]) for i in range(1, n)
    ]


def pin(v, *waits):
    def body(*refs):
        pass

    return pl.pallas_call(
        body,
        out_shape=jax.ShapeDtypeStruct(v.shape, v.dtype),
        in_specs=[ANY] * (1 + len(waits)),
        out_specs=ANY,
        input_output_aliases={0: 0},
        name="pin",
    )(v, *waits)


def over_tensor(pair):
    half, _, rows, width = pair.shape
    return pl.BlockSpec(
        (half, 1, rows, width), lambda i, t: (0, jnp.abs(i - t[0] // half), 0, 0)
    )


def gathered_rows(blocks, t, *waits):
    rows, width = blocks.shape[-2:]
    half = int(np.prod(blocks.shape[:-2])) // 2
    out = (half * rows // K, K, width)
    spec = pl.BlockSpec((half, rows, width), lambda i, t: (i, 0, 0))
    if blocks.ndim == 4:
        spec = over_tensor(blocks)

    def body(t_ref, in_ref, *refs):
        refs[-1][...] = in_ref[...].reshape(out)

    return pl.pallas_call(
        body,
        grid_spec=pltpu.PrefetchScalarGridSpec(
            num_scalar_prefetch=1,
            grid=(2,),
            in_specs=[spec, *[ANY] * len(waits)],
            out_specs=pl.BlockSpec(out, lambda i, t: (i, 0, 0)),
        ),
        out_shape=jax.ShapeDtypeStruct((2 * out[0], *out[1:]), blocks.dtype),
        compiler_params=params(),
        cost_estimate=cost(2.6),
        name="rows",
    )(t, blocks, *waits)


def to_each(v, axis):
    n = lax.axis_size(axis)
    return v + sum(lax.ppermute(v, axis, [(a, (a + i) % n) for a in range(n)]) for i in range(1, n))


def pick(v, at):
    return lax.dynamic_index_in_dim(v, at, 0, keepdims=False)


def over_core(kept, got):
    yh = lax.axis_index("yh")
    give = pick(kept, 1 - yh) + pick(got, 1 - yh).astype(F32)
    return pick(kept, yh) + pick(got, yh).astype(F32), give.astype(BF)


def per_device(streams, placement, w_query, w_key, w_value, w_output, w_gate, w_up, w_down,
               mix_dynamic, mix_static, cotangent):
    rows, _, width = streams.shape
    groups = placement.shape[0]
    t = lax.axis_index(TP).astype(jnp.int32)[None]
    nz = lax.axis_size("z")
    mt = jnp.transpose(mix_dynamic, (2, 0, 1))

    c1, q, kv, trig, *x_one = first(
        placement, mix_static, streams, mt, w_query, w_key, w_value, groups // 2, nz
    )
    same = exchange(kv, ("z", "yh"))
    other = swap(same, "core")
    attended, log, part_one, q = attend(placement, q, kv, same, other, w_output)
    qall = lax.all_gather(q, DP, axis=0)
    x_one = along_z(x_one)
    s1, b1, c2, pay = middle(
        t, mix_static, scatter_parts(part_one, TP), streams, c1, mt, x_one[1:]
    )
    pay = exchange(pay, TP).reshape(rows, width + 128)
    *xy, acts, part_two = feed(pay, cotangent, w_gate, w_up, w_down, nz)
    acts = lax.all_gather(acts, "z", axis=0)
    x_two = along_z(xy[:nz])
    turned, pair, base, gb1, dm, ds = turn_back(
        t, mix_static, scatter_parts(part_two, TP), s1, c2, cotangent, streams, c1, b1, mt, (qall, *x_two[1:])
    )
    pair = lax.dynamic_update_slice(pair, swap(turned, "yl")[None], (1, 0, 0))
    gb1 = exchange(gb1, TP).reshape(rows, width)
    y_two = along_z(xy[nz:])
    do, gq = query_back(placement, gb1, w_output, q, kv, log, same, other, trig, (pair, *y_two[1:],))
    own_pair = pair
    pair = lax.all_gather(pin(pair, gb1), "x", axis=0)
    tiles = w_gate.shape[1] // FEED_TILE
    do_same = exchange(do, ("z", "yh"))
    do_other = swap(do_same, "core")
    part_three, *ship = key_back(
        placement, kv, qall, do_same, do_other, gq, trig, w_query, w_key, w_value, gb1, attended, nz,
        (),
    )
    ff_keep, ff_give = weight_part(
        ((x_two, 0), (y_two, 0)), acts, tiles, (0, 0, 1), FEED_TILE, "feed_weights", 8, (part_three,)
    )
    ship = along_z(ship)
    gt, mix_keep, mix_give = last(
        t, mix_static, scatter_parts(part_three, TP), base, streams, c1, mt, dm, ds, (ff_keep,)
    )
    ff_keep, ff_give = over_core(ff_keep, swap(ff_give, "core"))
    ff_got = swap(ff_give, "yh")
    ff = ff_keep + ff_got.astype(F32)

    v = mix_keep + swap(mix_give, "core")
    mix_low = v
    yh, z = lax.axis_index("yh"), lax.axis_index("z")

    def half(at):
        return jnp.concatenate([lax.dynamic_slice_in_dim(v, at * nz, nz, 0), v[2 * nz :]], 0)

    v = half(yh) + swap(half(1 - yh), "yh")
    mix_mid = v

    def mine(at):
        return jnp.stack([pick(v, lax.rem(at, nz)), v[nz]])

    v = sum(along_z([mine(z + i) for i in range(nz)]))
    mix_high = v
    v = to_each(to_each(v, "yl"), "x")
    grad_dynamic = jnp.transpose(v[0].reshape(2, 8, -1)[:, :6], (0, 2, 1))
    grad_static = v[1].reshape(2, 8, 128)[:, :4, :6]
    keep, give = weight_part(
        ((ship, 4), (x_one, 0)), ship, 1, (0, 1, 1, 1), 256, "tail_weights", 4, (mix_mid,)
    )
    keep, give = over_core(keep, swap(give, "core"))
    tail = keep + swap(give, "yh").astype(F32)
    streams_out = gathered_rows(pair, t, mix_keep)
    gt = exchange(gt, TP)
    grad_streams = gathered_rows(gt, t, streams_out)
    return (
        streams_out,
        grad_streams,
        tail[1],
        tail[2],
        tail[3],
        jnp.transpose(tail[0]),
        ff[0],
        ff[1],
        jnp.transpose(ff[2]),
        grad_dynamic,
        grad_static,
    )


def solution(mesh):
    fine = Mesh(mesh.devices.reshape(4, 2, 2, 2, 4), ("z", "yh", "core", "yl", "x"))
    placed = (
        P(DP, None, None),
        P(),
        P(None, TP),
        P(None, TP),
        P(None, TP),
        P(TP, None),
        P(None, TP),
        P(None, TP),
        P(TP, None),
        P(),
        P(),
        P(DP, None, None),
    )
    return jax.shard_map(
        per_device,
        mesh=fine,
        in_specs=placed,
        out_specs=(
            P(DP, None, None),
            P(DP, None, None),
            P(DP, TP),
            P(DP, TP),
            P(DP, TP),
            P(TP, DP),
            P(DP, TP),
            P(DP, TP),
            P(TP, DP),
            P(None, DP, None),
            P(),
        ),
        check_vma=False,
    )
```

```python
import functools

import jax
import jax.numpy as jnp
import numpy as np
from jax import lax
from jax.experimental import pallas as pl
from jax.experimental.pallas import tpu as pltpu
from jax.sharding import Mesh
from jax.sharding import PartitionSpec as P

HEAD = 128
EPS = 1e-05
THETA = 10000.0
BF = jnp.bfloat16
F32 = jnp.float32
K = 4
DP = ("z", "yh", "core")
TP = ("yl", "x")
SMEM = pl.BlockSpec(memory_space=pltpu.SMEM)
ANY = pl.BlockSpec(memory_space=pl.ANY)
NT = (((1,), (1,)), ((), ()))
TN = (((0,), (0,)), ((), ()))
NN = (((1,), (0,)), ((), ()))


def dot(a, b, dims=NN):
    return lax.dot_general(a, b, dims, preferred_element_type=F32)


def lmean(v):
    return jnp.mean(v, -1, keepdims=True)


def lsum(v):
    return jnp.sum(v, -1, keepdims=True)


def norm_parts(v):
    ctr = v - lmean(v)
    rstd = lax.rsqrt(lmean(ctr * ctr) + EPS)
    return ctr * rstd, rstd


def norm_back(g, xhat, rstd):
    return rstd * (g - lmean(g) - xhat * lmean(g * xhat))


def three(v):
    hi = v.astype(BF)
    rest = v - hi.astype(F32)
    mid = rest.astype(BF)
    low = (rest - mid.astype(F32)).astype(BF)
    return hi, mid, low


def lanes(rows, pairs, start=None):
    lane = lax.broadcasted_iota(jnp.int32, (rows, 128), 1)
    out = jnp.zeros((rows, 128), F32) if start is None else start
    for at, v in pairs:
        out = jnp.where(lane == at, v, out)
    return out


def fold_parts(z):
    return z + pltpu.roll(z, 120, 1) + pltpu.roll(z, 112, 1)


def turn(v, cos, sin):
    return v * cos + pltpu.roll(v, 64, 1) * sin


def cost(us):
    return pl.CostEstimate(flops=0, bytes_accessed=int(us * 3.69e6), transcendentals=0)


def params():
    return pltpu.CompilerParams(vmem_limit_bytes=60 * 2**20)


def whole(shape):
    n = len(shape)
    return pl.BlockSpec(shape, lambda *_: (0,) * n)


def like(*shapes):
    return tuple(jax.ShapeDtypeStruct(s, d) for s, d in shapes)


def iota(shape, dim):
    return lax.broadcasted_iota(jnp.int32, shape, dim)


def order(rows, to_planes):
    count = rows // K
    a, b = iota((rows, rows), 0), iota((rows, rows), 1)
    if not to_planes:
        a, b = b, a
    return (a == (b % K) * count + b // K).astype(BF)


def planes(block):
    rows, _, width = block.shape
    v = dot(order(K * rows, True), block.reshape(K * rows, width))
    return [v[k * rows : (k + 1) * rows] for k in range(K)]


def unplanes(parts):
    rows = parts[0].shape[0]
    return dot(order(K * rows, False), jnp.concatenate(parts, 0)).astype(BF)


def stream_coefs(ref, rows):
    return [ref[pl.ds(k, rows, stride=K), :] for k in range(K)]


def static_rows(st_ref, layer, rows):
    row, lane = iota((rows, 128), 0) % K, iota((rows, 128), 1)
    out = jnp.zeros((rows, 128), F32)
    for k in range(K):
        for c in range(K + 2):
            out = jnp.where((row == k) & (lane == c), st_ref[layer, k, c], out)
    return out


def static_row(st_ref, layer, k):
    lane = iota((1, 128), 1)
    out = jnp.zeros((1, 128), F32)
    for c in range(K + 2):
        out = jnp.where(lane == c, st_ref[layer, k, c], out)
    return out


def fill_parts(m, wide_ref, mp_ref):
    cols = m.shape[0]
    wide_ref[...] = jnp.zeros_like(wide_ref)
    for i, v in enumerate(three(m)):
        wide_ref[8 * i : 8 * i + cols, :] = v.astype(F32)
    wide_ref[24:25, :] = jnp.ones((1, m.shape[1]), F32)
    mp_ref[...] = jnp.zeros_like(mp_ref)
    mp_ref[0:32, :] = wide_ref[...].astype(BF)


def columns_for(step, count, piece):
    at = lax.rem(lax.axis_index("z") + step, count) * piece
    return pl.ds(pl.multiple_of(at, piece), piece)


def copies(ref):
    for i in range(1, ref.shape[0]):
        ref[i] = ref[0]


def device_index():
    core = lax.axis_index("core")
    return (lax.axis_index("z") * 2 + lax.axis_index("yh")) * 2 + core, core


def first_kernel(place_ref, st_ref, freq_ref, s_ref, m_ref, wq_ref, wk_ref, wv_ref,
                 c_ref, q_ref, kv_ref, trig_ref, *refs):
    *x_refs, n_ref, wide_ref, mp_ref = refs
    rows, _, width = s_ref.shape
    fill_parts(m_ref[:, 0, :], wide_ref, mp_ref)
    sums = fold_parts(dot(jnp.ones((16, width), BF), mp_ref[...], NT))[0:1]
    step = 32
    part = K * step
    static = static_rows(st_ref, 0, part)
    row, lane = iota((part, 128), 0), iota((part, 128), 1)
    mine = (lane % step) == row // K

    def body(i, carry):
        r = pl.multiple_of(i * step, step)
        low = s_ref[pl.ds(r, step)].reshape(part, width)
        z = dot(low, mp_ref[...], NT)
        s = low.astype(F32)
        mean = z[:, 24:25] * (1.0 / width)
        ctr = s - mean
        rstd = lax.rsqrt(lmean(ctr * ctr) + EPS)
        c = static + jnp.tanh(rstd * (fold_parts(z) - mean * sums))
        c_ref[pl.ds(pl.multiple_of(i * part, part), part), :] = lanes(part, ((8, mean), (9, rstd)), c)
        a, b, d = (v.astype(F32) for v in three(c[:, 0:1]))
        take = jnp.where(lane < step, a, jnp.where(lane < 2 * step, b, d))
        take = jnp.where(mine & (lane < 3 * step), take, 0.0).astype(BF)
        w = dot(take, low, TN)
        taken = w[0:step] + w[step : 2 * step] + w[2 * step : 3 * step]
        n_ref[pl.ds(r, step), :] = norm_parts(taken)[0].astype(BF)
        return carry

    lax.fori_loop(0, rows // step, body, 0, unroll=True)
    piece = width // len(x_refs)
    for i, ref in enumerate(x_refs):
        ref[...] = n_ref[:, columns_for(i, len(x_refs), piece)]
    me, _ = device_index()
    prompts = place_ref.shape[0] // 2
    start = jnp.minimum(place_ref[me], prompts) * rows
    angle = (start + iota((rows, HEAD), 0)).astype(F32) * freq_ref[...]
    cos = jnp.cos(angle)
    sin = jnp.where(iota((rows, HEAD), 1) < HEAD // 2, -1.0, 1.0) * jnp.sin(angle)
    trig_ref[0] = cos
    trig_ref[1] = sin
    normed = n_ref[...]
    q = dot(normed, wq_ref[...])
    k = dot(normed, wk_ref[...])
    heads = q.shape[1] // HEAD
    for h in range(heads):
        cut = slice(h * HEAD, (h + 1) * HEAD)
        q_ref[:, cut] = turn(q[:, cut], cos, sin).astype(BF)
        kv_ref[0, :, cut] = turn(k[:, cut], cos, sin).astype(BF)
    kv_ref[0, :, heads * HEAD :] = dot(normed, wv_ref[...]).astype(BF)
    copies(kv_ref)


def first(place, st, streams, mt, wq, wk, wv, chips, count):
    rows, _, width = streams.shape
    cols = wq.shape[1]
    half = HEAD // 2
    freq = np.float32(THETA) ** (-np.arange(half, dtype=np.float32) / np.float32(half))
    freq = jnp.asarray(np.concatenate([freq, freq])[None].astype(np.float32))
    outs = (
        ((K * rows, 128), F32),
        ((rows, cols), BF),
        ((chips, rows, 2 * cols), BF),
        ((2, rows, HEAD), F32),
        *[((rows, width // count), BF)] * count,
    )
    return pl.pallas_call(
        first_kernel,
        grid=(1,),
        out_shape=like(*outs),
        in_specs=[SMEM, SMEM, whole(freq.shape), whole(streams.shape),
                  whole(mt.shape),
                  whole(wq.shape), whole(wk.shape), whole(wv.shape)],
        out_specs=[whole(s) for s, _ in outs],
        scratch_shapes=[
            pltpu.VMEM((rows, width), BF),
            pltpu.VMEM((32, width), F32),
            pltpu.VMEM((128, width), BF),
        ],
        compiler_params=params(),
        cost_estimate=cost(10),
        name="first",
    )(place, st, freq, streams, mt, wq, wk, wv)


def own_blocks(place_ref, own_ref, same_ref, other_ref):
    me, core = device_index()
    own = place_ref[me]
    count = place_ref.shape[0]
    prompts = count // 2
    is_cont = own >= prompts
    blocks = []
    for s in range(prompts):
        d = jnp.int32(0)
        for a in range(count):
            d = jnp.where(place_ref[a] == s, a, d)
        block = jnp.where((d % 2) == core, same_ref[d // 2], other_ref[d // 2])
        reach = jnp.where(is_cont | (s < own), 4096, jnp.where(s == own, 0, -4096))
        blocks.append((block, reach))
    blocks.append((own_ref[0], jnp.where(is_cont, 0, -4096)))
    return blocks


def key_after_query(keys, queries):
    return iota((keys, queries), 0) - iota((keys, queries), 1)


def vector_rows(*vectors):
    row = iota((16, vectors[0].shape[1]), 0)
    out = jnp.zeros(row.shape, F32)
    for i, v in enumerate(vectors):
        for n, p in enumerate(three(v)):
            out = jnp.where(row == 3 * i + n, p.astype(F32), out)
    return out


def vector_of(rows16, i):
    v = rows16.astype(F32)
    return v[3 * i : 3 * i + 1] + v[3 * i + 1 : 3 * i + 2] + v[3 * i + 2 : 3 * i + 3]


def head_cuts(cols, h):
    return [slice(i * cols + h * HEAD, i * cols + (h + 1) * HEAD) for i in (0, 1)]


def attend_kernel(place_ref, q_ref, own_ref, same_ref, other_ref, wo_ref, at_ref, log_ref, part_ref, qcopy_ref):
    rows, cols = at_ref.shape
    heads = cols // HEAD
    scale = HEAD ** (-0.5)
    blocks = own_blocks(place_ref, own_ref, same_ref, other_ref)
    lag = key_after_query(rows, rows)
    logs = []
    for h in range(heads):
        cut, vcut = head_cuts(cols, h)
        q = q_ref[:, cut]
        scores = [
            jnp.where(lag <= reach, dot(b[:, cut], q, NT) * scale, -1e30) for b, reach in blocks
        ]
        top = functools.reduce(jnp.maximum, [jnp.max(s, 0, keepdims=True) for s in scores])
        terms = [jnp.exp(s - top) for s in scores]
        total = functools.reduce(jnp.add, [jnp.sum(e, 0, keepdims=True) for e in terms])
        inv = 1.0 / total
        out = None
        for e, (b, _) in zip(terms, blocks):
            o = dot((e * inv).astype(BF), b[:, vcut], TN)
            out = o if out is None else out + o
        at_ref[:, cut] = out.astype(BF)
        logs.append(top + jnp.log(total))
    log_ref[...] = jnp.concatenate(logs, 1)
    qcopy_ref[...] = q_ref[...]
    part_ref[...] = dot(at_ref[...], wo_ref[...]).astype(BF)


def own_block(kv):
    return pl.BlockSpec((1, *kv.shape[1:]), lambda i: (0, 0, 0))


def attend(place, q, kv, same, other, wo):
    rows, cols = q.shape
    args = (q, kv, same, other, wo)
    outs = (((rows, cols), BF), ((1, cols), F32), ((rows, wo.shape[1]), BF), ((rows, cols), BF))
    return pl.pallas_call(
        attend_kernel,
        grid=(1,),
        out_shape=like(*outs),
        in_specs=[SMEM, whole(q.shape), own_block(kv)] + [whole(v.shape) for v in args[2:]],
        out_specs=[whole(s) for s, _ in outs],
        compiler_params=params(),
        cost_estimate=cost(4.5),
        name="attend",
    )(place, *args)


def middle_kernel(t_ref, st_ref, parts_ref, s_ref, c_ref, m_ref, s1_ref, b1_ref, c2_ref, pay_ref,
                  wide_ref, mp_ref, split_ref):
    fill_parts(m_ref[:, 1, :], wide_ref, mp_ref)
    b1 = jnp.sum(parts_ref[...].astype(F32), 0)
    b1_ref[...] = b1
    rows, width = b1.shape
    s0 = planes(s_ref[...])
    c1 = stream_coefs(c_ref, rows)
    stats = []
    for j in range(K):
        v = c1[j][:, 5:6] * b1
        for k in range(K):
            v = v + c1[k][:, 1 + j : 2 + j] * s0[k]
        s1_ref[j] = v
        mean = lmean(v)
        ctr = v - mean
        stats.append((mean, lax.rsqrt(lmean(ctr * ctr) + EPS)))
        hi = ctr.astype(BF)
        split_ref[j * rows : (j + 1) * rows, :] = hi
        split_ref[(K + j) * rows : (K + j + 1) * rows, :] = (ctr - hi.astype(F32)).astype(BF)
    z = dot(split_ref[...], mp_ref[...], NT)
    taken, gives = None, []
    for j in range(K):
        mean, rstd = stats[j]
        zj = z[j * rows : (j + 1) * rows] + z[(K + j) * rows : (K + j + 1) * rows]
        c = static_row(st_ref, 1, j) + jnp.tanh(rstd * fold_parts(zj))
        c2_ref[j] = lanes(rows, ((8, mean), (9, rstd)), c)
        part = c[:, 0:1] * s1_ref[j]
        taken = part if taken is None else taken + part
        gives += [(4 * i + j, v.astype(F32)) for i, v in enumerate(three(c[:, 5:6]))]
    pay_ref[0, :, 0:width] = norm_parts(taken)[0].astype(BF)
    pay_ref[0, :, width:] = lanes(rows, gives).astype(BF)
    copies(pay_ref)


def token_call(kernel, name, t, tables, args, outs, scratch, waits=()):
    count = 1 + len(tables) + len(args)

    def body(*refs):
        kernel(*refs[:count], *refs[count + len(waits) :])

    in_specs = [SMEM] * len(tables)
    for v, block in args:
        if block is None:
            in_specs.append(pl.BlockSpec(v.shape, lambda i, t, n=v.ndim: (0,) * n))
        else:
            in_specs.append(pl.BlockSpec(block, lambda i, t, n=v.ndim: (t[0],) + (0,) * (n - 1)))
    return pl.pallas_call(
        body,
        grid_spec=pltpu.PrefetchScalarGridSpec(
            num_scalar_prefetch=1,
            grid=(1,),
            in_specs=in_specs + [ANY] * len(waits),
            out_specs=[pl.BlockSpec(s, lambda i, t, n=len(s): (0,) * n) for s, _ in outs],
            scratch_shapes=scratch,
        ),
        out_shape=like(*outs),
        compiler_params=params(),
        cost_estimate=cost(4),
        name=name,
    )(t, *tables, *[v for v, _ in args], *waits)


def middle(t, st, parts, streams, c1, mt, waits):
    peers, rows, width = parts.shape
    return token_call(
        middle_kernel,
        "middle",
        t,
        (st,),
        (
            (parts, None),
            (streams, (rows, K, width)),
            (c1, (K * rows, 128)),
            (mt, None),
        ),
        (
            ((K, rows, width), F32),
            ((rows, width), F32),
            ((K, rows, 128), F32),
            ((peers, rows, width + 128), BF),
        ),
        [
            pltpu.VMEM((32, width), F32),
            pltpu.VMEM((128, width), BF),
            pltpu.VMEM((2 * K * rows, width), BF),
        ],
        waits,
    )


def feed_kernel(pay_ref, cot_ref, wg_ref, wu_ref, wd_ref, *refs):
    *xy_refs, acts_ref, out_ref, gb_ref, b_ref, l_ref = refs
    step, steps = pl.program_id(0), pl.num_programs(0)
    rows, width = gb_ref.shape
    count = len(xy_refs) // 2
    piece = width // count

    @pl.when(step == 0)
    def _():
        chunk = 32
        row, lane = iota((chunk, K * chunk), 0), iota((chunk, K * chunk), 1)

        def body(i, carry):
            r = pl.multiple_of(i * chunk, chunk)
            give = pay_ref[pl.ds(r, chunk), width:].astype(F32)
            block = cot_ref[pl.ds(r, chunk)].reshape(K * chunk, width)
            total = None
            for n in range(3):
                w = jnp.zeros((chunk, K * chunk), F32)
                for j in range(K):
                    w = jnp.where(lane == K * row + j, give[:, K * n + j : K * n + j + 1], w)
                part = dot(w.astype(BF), block)
                total = part if total is None else total + part
            gb_ref[pl.ds(r, chunk), :] = total.astype(BF)
            return carry

        lax.fori_loop(0, rows // chunk, body, 0, unroll=True)
        for i in range(count):
            at = columns_for(i, count, piece)
            xy_refs[i][...] = pay_ref[:, at]
            xy_refs[count + i][...] = gb_ref[:, at]
        b_ref[...] = jnp.zeros_like(b_ref)
        l_ref[...] = jnp.zeros_like(l_ref)

    normed = pay_ref[:, 0:width]
    gate = dot(normed, wg_ref[...])
    up = dot(normed, wu_ref[...])
    sig = 1.0 / (1.0 + jnp.exp(-gate))
    silu = gate * sig
    hidden = (silu * up).astype(BF)
    grad = dot(gb_ref[...], wd_ref[...], NT)
    grad_gate = (grad * up * (sig * (1.0 + gate * (1.0 - sig)))).astype(BF)
    grad_up = (grad * silu).astype(BF)
    tile = hidden.shape[1]
    acts_ref[:, 0:tile] = grad_gate
    acts_ref[:, tile : 2 * tile] = grad_up
    acts_ref[:, 2 * tile :] = hidden
    b_ref[...] += dot(hidden, wd_ref[...])
    l_ref[...] += dot(grad_gate, wg_ref[...], NT) + dot(grad_up, wu_ref[...], NT)

    @pl.when(step == steps - 1)
    def _():
        out_ref[:, 0:width] = b_ref[...].astype(BF)
        out_ref[:, width:] = l_ref[...].astype(BF)


FEED_TILE = 256


def feed(pay, cotangent, wg, wu, wd, count):
    rows, _, width = cotangent.shape
    hidden = wg.shape[1]
    tile = FEED_TILE
    xy = (rows, width // count)
    return pl.pallas_call(
        feed_kernel,
        grid=(hidden // tile,),
        in_specs=[
            whole(pay.shape),
            whole(cotangent.shape),
            pl.BlockSpec((width, tile), lambda f: (0, f)),
            pl.BlockSpec((width, tile), lambda f: (0, f)),
            pl.BlockSpec((tile, width), lambda f: (f, 0)),
        ],
        out_specs=[
            *[whole(xy)] * (2 * count),
            pl.BlockSpec((rows, 3 * tile), lambda f: (0, f)),
            whole((rows, 2 * width)),
        ],
        out_shape=like(
            *[(xy, BF)] * (2 * count),
            ((rows, 3 * hidden), BF),
            ((rows, 2 * width), BF),
        ),
        scratch_shapes=[
            pltpu.VMEM((rows, width), BF),
            pltpu.VMEM((rows, width), F32),
            pltpu.VMEM((rows, width), F32),
        ],
        compiler_params=params(),
        cost_estimate=cost(14),
        name="feed",
    )(pay, cotangent, wg, wu, wd)


def coef_back(grads, coefs, st_ref, layer, m, xhats, dm_ref, ds_ref, columns):
    rows = xhats[0].shape[0]
    dzs, statics = [], []
    for k in range(K):
        g = lanes(rows, grads[k].items())
        th = coefs[k] - static_row(st_ref, layer, k)
        dzs.append(g * (1.0 - th * th))
        statics.append(jnp.sum(g, 0, keepdims=True))
    ds_ref[layer] = jnp.concatenate(statics + [jnp.zeros((8 - K, 128), F32)], 0)
    for c in range(8):
        if c in columns:
            v = None
            for k in range(K):
                part = dzs[k][:, c : c + 1] * xhats[k]
                v = part if v is None else v + part
            dm_ref[layer, c : c + 1, :] = jnp.sum(v, 0, keepdims=True)
        else:
            dm_ref[layer, c : c + 1, :] = jnp.zeros((1, xhats[0].shape[1]), F32)
    out = []
    for k in range(K):
        v = None
        for c in columns:
            part = dzs[k][:, c : c + 1] * m[c : c + 1, :]
            v = part if v is None else v + part
        out.append(v)
    return out


def turn_kernel(t_ref, st_ref, parts_ref, s1_ref, c2_ref, cot_ref, s_ref, c1_ref, b1_ref, m_ref,
                own_ref, pair_ref, base_ref, gb1_ref, dm_ref, ds_ref):
    rows, width = b1_ref.shape
    both = jnp.sum(parts_ref[...].astype(F32), 0)
    b2, gn = both[:, 0:width], both[:, width:]
    s1 = [s1_ref[k] for k in range(K)]
    c2 = [c2_ref[k] for k in range(K)]
    g2 = planes(cot_ref[...])
    grads = [dict() for _ in range(K)]
    taken, s2 = None, []
    for j in range(K):
        v = c2[j][:, 5:6] * b2
        for k in range(K):
            v = v + c2[k][:, 1 + j : 2 + j] * s1[k]
        s2.append(v.astype(BF))
        grads[j][5] = lsum(g2[j] * b2)
        for k in range(K):
            grads[k][1 + j] = lsum(g2[j] * s1[k])
        part = c2[j][:, 0:1] * s1[j]
        taken = part if taken is None else taken + part
    s2 = unplanes(s2)
    own_ref[...] = s2
    pair_ref[0] = s2
    normed, rstd = norm_parts(taken)
    gt = norm_back(gn, normed, rstd)
    for k in range(K):
        grads[k][0] = lsum(gt * s1[k])
    xhats = [(s1[k] - c2[k][:, 8:9]) * c2[k][:, 9:10] for k in range(K)]
    gx = coef_back(grads, c2, st_ref, 1, m_ref[:, 1, :], xhats, dm_ref, ds_ref, range(6))
    g1 = []
    for k in range(K):
        v = c2[k][:, 0:1] * gt + norm_back(gx[k], xhats[k], c2[k][:, 9:10])
        for j in range(K):
            v = v + c2[k][:, 1 + j : 2 + j] * g2[j]
        g1.append(v)
    c1 = stream_coefs(c1_ref, rows)
    b1 = b1_ref[...]
    s0 = planes(s_ref[...])
    gb1 = None
    grads = [dict() for _ in range(K)]
    for j in range(K):
        part = c1[j][:, 5:6] * g1[j]
        gb1 = part if gb1 is None else gb1 + part
        grads[j][5] = lsum(g1[j] * b1)
        for k in range(K):
            grads[k][1 + j] = lsum(g1[j] * s0[k])
    gb1_ref[0] = gb1.astype(BF)
    copies(gb1_ref)
    xhats = [(s0[k] - c1[k][:, 8:9]) * c1[k][:, 9:10] for k in range(K)]
    gx = coef_back(grads, c1, st_ref, 0, m_ref[:, 0, :], xhats, dm_ref, ds_ref, range(1, 6))
    for k in range(K):
        v = norm_back(gx[k], xhats[k], c1[k][:, 9:10])
        for j in range(K):
            v = v + c1[k][:, 1 + j : 2 + j] * g1[j]
        base_ref[k] = v


def turn_back(t, st, parts, s1, c2, cotangent, streams, c1, b1, mt, waits):
    rows, width = b1.shape
    block = (rows, K, width)
    return token_call(
        turn_kernel,
        "turn",
        t,
        (st,),
        (
            (parts, None),
            (s1, None),
            (c2, None),
            (cotangent, block),
            (streams, block),
            (c1, (K * rows, 128)),
            (b1, None),
            (mt, None),
        ),
        (
            ((K * rows, width), BF),
            ((2, K * rows, width), BF),
            ((K, rows, width), F32),
            ((parts.shape[0], rows, width), BF),
            ((2, 8, width), F32),
            ((2, 8, 128), F32),
        ),
        [],
        waits,
    )


def query_kernel(waits, place_ref, gb_ref, wo_ref, q_ref, own_ref, log_ref, same_ref, other_ref, trig_ref,
                 *refs):
    do_ref, gq_ref = refs[waits:]
    rows, cols = gq_ref.shape
    heads = cols // HEAD
    scale = HEAD ** (-0.5)
    grad = dot(gb_ref[...], wo_ref[...], NT).astype(BF)
    do_ref[0, 0:rows, :] = grad
    blocks = own_blocks(place_ref, own_ref, same_ref, other_ref)
    lag = key_after_query(rows, rows)
    inners, logs = [], []
    for h in range(heads):
        cut, vcut = head_cuts(cols, h)
        q, do = q_ref[:, cut], grad[:, cut]
        log = log_ref[:, cut]
        logs.append(log)
        probs, gps, inner = [], [], None
        for b, reach in blocks:
            s = jnp.where(lag <= reach, dot(b[:, cut], q, NT) * scale, -1e30)
            p = jnp.exp(s - log)
            gp = dot(b[:, vcut], do, NT)
            part = jnp.sum(p * gp, 0, keepdims=True)
            inner = part if inner is None else inner + part
            probs.append(p)
            gps.append(gp)
        gq = None
        for p, gp, (b, _) in zip(probs, gps, blocks):
            part = dot((p * (gp - inner)).astype(BF), b[:, cut], TN)
            gq = part if gq is None else gq + part
        gq_ref[:, cut] = turn(gq * scale, trig_ref[0], -trig_ref[1]).astype(BF)
        inners.append(inner)
    do_ref[0, rows:, :] = jnp.concatenate(
        [vector_rows(i, log) for i, log in zip(inners, logs)], 1
    ).astype(BF)
    copies(do_ref)


def query_back(place, gb1, wo, q, kv, log, same, other, trig, waits):
    rows, cols = q.shape
    args = (gb1, wo, q, kv, log, same, other, trig)
    outs = (((same.shape[0], rows + 16, cols), BF), ((rows, cols), BF))
    specs = [whole(v.shape) for v in args]
    specs[3] = own_block(kv)
    return pl.pallas_call(
        functools.partial(query_kernel, len(waits)),
        grid=(1,),
        out_shape=like(*outs),
        in_specs=[SMEM] + specs + [ANY] * len(waits),
        out_specs=[whole(s) for s, _ in outs],
        compiler_params=params(),
        cost_estimate=cost(5.5),
        name="query_back",
    )(place, *args, *waits)


def key_kernel(waits, place_ref, own_ref, qall_ref, same_ref, other_ref, gq_ref, trig_ref,
               wq_ref, wk_ref, wv_ref, gb_ref, at_ref, *refs):
    part_ref, *ship_refs = refs[waits:]
    rows, cols = gq_ref.shape
    small_ref = ship_refs[0].at[:, cols : 4 * cols]
    ship_refs[0][:, 0:cols] = at_ref[...]
    heads = cols // HEAD
    scale = HEAD ** (-0.5)
    me, core = device_index()
    own = place_ref[me]
    count = place_ref.shape[0]
    prompts = count // 2
    groups = [(g, rel) for g in range(count // 2) for rel in range(2)]
    reach = []
    for g, rel in groups:
        seg = place_ref[2 * g + (core + rel) % 2]
        full = (own < prompts) & (seg > own)
        value = jnp.where(full, 4096, jnp.where(seg == own, 0, -4096))
        reach.append(jnp.zeros((1, rows), jnp.int32) + value)
    reach = jnp.concatenate(reach, 1)
    lag = key_after_query(rows, rows)
    seen = jnp.concatenate([lag] * count, 1) <= reach
    for h in range(heads):
        cut, vcut = head_cuts(cols, h)
        k, v = own_ref[0, :, cut], own_ref[0, :, vcut]
        qs, dos, logs, inners = [], [], [], []
        for g, rel in groups:
            src = same_ref if rel == 0 else other_ref
            qs.append(qall_ref[2 * g + (core + rel) % 2, :, cut])
            dos.append(src[g, 0:rows, cut])
            inners.append(vector_of(src[g, rows:, cut], 0))
            logs.append(vector_of(src[g, rows:, cut], 1))
        qs, dos = jnp.concatenate(qs, 0), jnp.concatenate(dos, 0)
        logs, inners = jnp.concatenate(logs, 1), jnp.concatenate(inners, 1)
        s = jnp.where(seen, dot(k, qs, NT) * scale, -1e30)
        p = jnp.exp(s - logs)
        gp = dot(v, dos, NT)
        ds = (p * (gp - inners)).astype(BF)
        gv = dot(p.astype(BF), dos)
        gk = dot(ds, qs) * scale
        small_ref[:, vcut] = turn(gk, trig_ref[0], -trig_ref[1]).astype(BF)
        small_ref[:, 2 * cols + h * HEAD : 2 * cols + (h + 1) * HEAD] = gv.astype(BF)
    small_ref[:, 0:cols] = gq_ref[...]
    part = dot(gq_ref[...], wq_ref[...], NT)
    part += dot(small_ref[:, cols : 2 * cols], wk_ref[...], NT)
    part += dot(small_ref[:, 2 * cols :], wv_ref[...], NT)
    part_ref[...] = part.astype(BF)
    count = len(ship_refs)
    piece = gb_ref.shape[1] // count
    for i, ref in enumerate(ship_refs):
        if i:
            ref[:, 0 : 4 * cols] = ship_refs[0][:, 0 : 4 * cols]
        ref[:, 4 * cols :] = gb_ref[:, columns_for(i, count, piece)]


def key_back(place, kv, qall, same, other, gq, trig, wq, wk, wv, gb1, attended, count, waits):
    rows, cols = gq.shape
    width = wq.shape[0]
    args = (kv, qall, same, other, gq, trig, wq, wk, wv, gb1, attended)
    specs = [whole(v.shape) for v in args]
    specs[0] = own_block(kv)
    outs = (((rows, width), BF), *[((rows, 4 * cols + width // count), BF)] * count)
    return pl.pallas_call(
        functools.partial(key_kernel, len(waits)),
        grid=(1,),
        out_shape=like(*outs),
        in_specs=[SMEM] + specs + [ANY] * len(waits),
        out_specs=[whole(s) for s, _ in outs],
        compiler_params=params(),
        cost_estimate=cost(6.5),
        name="key_back",
    )(place, *args, *waits)


def last_kernel(t_ref, st_ref, parts_ref, base_ref, s_ref, c_ref, m_ref, dm_ref, ds_ref, out_ref, keep_ref, give_ref):
    gn = jnp.sum(parts_ref[...].astype(F32), 0)
    rows, width = gn.shape
    s0 = planes(s_ref[...])
    c1 = stream_coefs(c_ref, rows)
    taken = None
    for k in range(K):
        part = c1[k][:, 0:1] * s0[k]
        taken = part if taken is None else taken + part
    normed, rstd = norm_parts(taken)
    gt = norm_back(gn, normed, rstd)
    total, statics, out = None, [], []
    lane = iota((1, 128), 1)
    m = m_ref[0:1, 0, :]
    ctr = m - lmean(m)
    for k in range(K):
        g = lsum(gt * s0[k])
        th = c1[k][:, 0:1] - st_ref[0, k, 0]
        dz = g * (1.0 - th * th)
        xhat = (s0[k] - c1[k][:, 8:9]) * c1[k][:, 9:10]
        part = dz * xhat
        total = part if total is None else total + part
        v = base_ref[k] + c1[k][:, 0:1] * gt
        out.append((v + c1[k][:, 9:10] * dz * (ctr - xhat * lmean(m * xhat))).astype(BF))
        statics.append(jnp.where(lane == 0, jnp.sum(g, 0, keepdims=True), 0.0))
    out_ref[0] = unplanes(out)
    copies(out_ref)
    top = dm_ref[0] + jnp.concatenate(
        [jnp.sum(total, 0, keepdims=True), jnp.zeros((7, width), F32)], 0
    )
    statics = ds_ref[0] + jnp.concatenate(statics + [jnp.zeros((8 - K, 128), F32)], 0)
    bottom = dm_ref[1]
    core = lax.axis_index("core")
    blocks = keep_ref.shape[0] - 1
    nz = blocks // 2
    for yh in range(2):
        for z in range(nz):
            pair = []
            for i in range(2):
                at = ((z * 2 + yh) * 2 + i) * 128
                pair.append(jnp.concatenate([top[:, at : at + 128], bottom[:, at : at + 128]], 0))
            keep_ref[yh * nz + z] = jnp.where(core == 0, pair[0], pair[1])
            give_ref[yh * nz + z] = jnp.where(core == 0, pair[1], pair[0])
    both = jnp.concatenate([statics, ds_ref[1]], 0)
    keep_ref[blocks] = both
    give_ref[blocks] = both


def last(t, st, parts, base, streams, c1, mt, dm, ds, waits):
    peers, rows, width = parts.shape
    blocks = ((width // 256 + 1, 16, 128), F32)
    return token_call(
        last_kernel,
        "last",
        t,
        (st,),
        (
            (parts, None),
            (base, None),
            (streams, (rows, K, width)),
            (c1, (K * rows, 128)),
            (mt, None),
            (dm, None),
            (ds, None),
        ),
        (((peers, K * rows, width), BF), blocks, blocks),
        [],
        waits,
    )


def weight_kernel(picks, tile, count, gathered, waits, whole_sums, *refs):
    if whole_sums:
        *lefts, sum_ref = refs
        span = sum_ref.shape[3]
    else:
        *lefts, keep_ref, give_ref, hold_ref = refs
        span = keep_ref.shape[3]
    lefts = lefts[: len(lefts) - waits]
    rights = lefts[-1:] if gathered else lefts[-count:]
    lefts = lefts[: -len(rights)]
    units = len(picks)
    core, z = lax.axis_index("core"), lax.axis_index("z")
    mats = [
        jnp.concatenate([r[...] for r in lefts[i : i + count]], 0).T
        for i in range(0, len(lefts), count)
    ]
    part = 128
    kept = pl.ds(pl.multiple_of(core * part, part), part)
    given = pl.ds(pl.multiple_of((1 - core) * part, part), part)
    for f in range(span // tile):
        for u, pick in enumerate(picks):
            cut = slice((f * units + u) * tile, (f * units + u + 1) * tile)
            if gathered:
                right = [rights[0][lax.rem(z - i + count, count), :, cut] for i in range(count)]
            else:
                right = [r[:, cut] for r in rights]
            v = dot(mats[pick], jnp.concatenate(right, 0))
            to = slice(f * tile, (f + 1) * tile)
            if whole_sums:
                sum_ref[0, u, :, to] = v[0:part].astype(BF)
                sum_ref[1, u, :, to] = v[part:].astype(BF)
            else:
                hold_ref[f % 2] = v
                keep_ref[0, u, :, to] = hold_ref[f % 2, kept, :]
                give_ref[0, u, :, to] = hold_ref[f % 2, given, :].astype(BF)


def weight_part(lefts, right, tiles, picks, tile, name, us, waits=(), whole_sums=False):
    count = len(lefts[0][0])
    rows = lefts[0][0][0].shape[0]
    units = len(picks)
    gathered = not isinstance(right, (list, tuple))
    shape = (2, units, 128, tiles * tile)
    out = pl.BlockSpec((1, *shape[1:]), lambda y: (y, 0, 0, 0))
    outs, shapes = [out, out], like((shape, F32), (shape, BF))
    scratch = [pltpu.VMEM((2, 256, tile), F32)]
    if whole_sums:
        outs = pl.BlockSpec(shape, lambda y: (y, 0, 0, 0))
        shapes = jax.ShapeDtypeStruct((4, *shape[1:]), BF)
        scratch = []
    specs = [
        pl.BlockSpec((rows, 256), lambda y, o=o: (0, o + y)) for pieces, o in lefts for _ in pieces
    ]
    if gathered:
        specs.append(pl.BlockSpec((count, rows, units * tile * tiles), lambda y: (0, 0, 0)))
        right = [right]
    else:
        specs += [pl.BlockSpec((rows, units * tile * tiles), lambda y: (0, 0))] * count
    return pl.pallas_call(
        functools.partial(weight_kernel, picks, tile, count, gathered, len(waits), whole_sums),
        grid=(2,),
        in_specs=specs + [ANY] * len(waits),
        out_specs=outs,
        out_shape=shapes,
        scratch_shapes=scratch,
        compiler_params=params(),
        cost_estimate=cost(us),
        name=name,
    )(*[v for pieces, _ in lefts for v in pieces], *right, *waits)


def exchange(blocks, axes):
    return lax.all_to_all(blocks, axes, 0, 0, tiled=True)


def scatter_parts(partial, axes):
    n = lax.axis_size(axes)
    return exchange(partial.reshape(n, partial.shape[0] // n, partial.shape[1]), axes)


def swap(v, axis):
    return lax.ppermute(v, axis, [(0, 1), (1, 0)])


def along_z(pieces):
    n = lax.axis_size("z")
    return [pieces[0]] + [
        lax.ppermute(pieces[i], "z", [(a, (a + i) % n) for a in range(n)]) for i in range(1, n)
    ]


def pin(v, *waits):
    def body(*refs):
        pass

    return pl.pallas_call(
        body,
        out_shape=jax.ShapeDtypeStruct(v.shape, v.dtype),
        in_specs=[ANY] * (1 + len(waits)),
        out_specs=ANY,
        input_output_aliases={0: 0},
        name="pin",
    )(v, *waits)


def over_tensor(pair):
    half, _, rows, width = pair.shape
    return pl.BlockSpec(
        (half, 1, rows, width), lambda i, t: (0, jnp.abs(i - t[0] // half), 0, 0)
    )


def gathered_rows(blocks, t, *waits):
    rows, width = blocks.shape[-2:]
    half = int(np.prod(blocks.shape[:-2])) // 2
    out = (half * rows // K, K, width)
    spec = pl.BlockSpec((half, rows, width), lambda i, t: (i, 0, 0))
    if blocks.ndim == 4:
        spec = over_tensor(blocks)

    def body(t_ref, in_ref, *refs):
        refs[-1][...] = in_ref[...].reshape(out)

    return pl.pallas_call(
        body,
        grid_spec=pltpu.PrefetchScalarGridSpec(
            num_scalar_prefetch=1,
            grid=(2,),
            in_specs=[spec, *[ANY] * len(waits)],
            out_specs=pl.BlockSpec(out, lambda i, t: (i, 0, 0)),
        ),
        out_shape=jax.ShapeDtypeStruct((2 * out[0], *out[1:]), blocks.dtype),
        compiler_params=params(),
        cost_estimate=cost(2.6),
        name="rows",
    )(t, blocks, *waits)


def to_each(v, axis):
    n = lax.axis_size(axis)
    return v + sum(lax.ppermute(v, axis, [(a, (a + i) % n) for a in range(n)]) for i in range(1, n))


def pick(v, at):
    return lax.dynamic_index_in_dim(v, at, 0, keepdims=False)


def over_core(kept, got):
    yh = lax.axis_index("yh")
    give = pick(kept, 1 - yh) + pick(got, 1 - yh).astype(F32)
    return pick(kept, yh) + pick(got, yh).astype(F32), give.astype(BF)


def per_device(streams, placement, w_query, w_key, w_value, w_output, w_gate, w_up, w_down,
               mix_dynamic, mix_static, cotangent):
    rows, _, width = streams.shape
    groups = placement.shape[0]
    t = lax.axis_index(TP).astype(jnp.int32)[None]
    nz = lax.axis_size("z")
    mt = jnp.transpose(mix_dynamic, (2, 0, 1))

    c1, q, kv, trig, *x_one = first(
        placement, mix_static, streams, mt, w_query, w_key, w_value, groups // 2, nz
    )
    same = exchange(kv, ("z", "yh"))
    other = swap(same, "core")
    attended, log, part_one, q = attend(placement, q, kv, same, other, w_output)
    qall = lax.all_gather(q, DP, axis=0)
    x_one = along_z(x_one)
    s1, b1, c2, pay = middle(
        t, mix_static, scatter_parts(part_one, TP), streams, c1, mt, x_one[1:]
    )
    pay = exchange(pay, TP).reshape(rows, width + 128)
    *xy, acts, part_two = feed(pay, cotangent, w_gate, w_up, w_down, nz)
    acts = lax.all_gather(acts, "z", axis=0)
    x_two = along_z(xy[:nz])
    turned, pair, base, gb1, dm, ds = turn_back(
        t, mix_static, scatter_parts(part_two, TP), s1, c2, cotangent, streams, c1, b1, mt, (qall, *x_two[1:])
    )
    pair = lax.dynamic_update_slice(pair, swap(turned, "yl")[None], (1, 0, 0))
    gb1 = exchange(gb1, TP).reshape(rows, width)
    y_two = along_z(xy[nz:])
    do, gq = query_back(placement, gb1, w_output, q, kv, log, same, other, trig, (pair, *y_two[1:],))
    pair = lax.all_gather(pin(pair, gb1), "x", axis=0)
    tiles = w_gate.shape[1] // FEED_TILE
    do_same = exchange(do, ("z", "yh"))
    do_other = swap(do_same, "core")
    part_three, *ship = key_back(
        placement, kv, qall, do_same, do_other, gq, trig, w_query, w_key, w_value, gb1, attended, nz,
        (),
    )
    ff_keep, ff_give = weight_part(
        ((x_two, 0), (y_two, 0)), acts, tiles, (0, 0, 1), FEED_TILE, "feed_weights", 8, (part_three,)
    )
    gt, mix_keep, mix_give = last(
        t, mix_static, scatter_parts(part_three, TP), base, streams, c1, mt, dm, ds, (ff_keep,)
    )
    ship = along_z([pin(v, mix_keep) for v in ship])
    ff_keep, ff_give = over_core(ff_keep, swap(ff_give, "core"))
    ff_got = swap(ff_give, "yh")
    ff = ff_keep + ff_got.astype(F32)

    v = mix_keep + swap(mix_give, "core")
    mix_low = v
    yh, z = lax.axis_index("yh"), lax.axis_index("z")

    def half(at):
        return jnp.concatenate([lax.dynamic_slice_in_dim(v, at * nz, nz, 0), v[2 * nz :]], 0)

    v = half(yh) + swap(half(1 - yh), "yh")

    def mine(at):
        return jnp.stack([pick(v, lax.rem(at, nz)), v[nz]])

    v = sum(along_z([mine(z + i) for i in range(nz)]))
    v = to_each(to_each(v, "yl"), "x")
    grad_dynamic = jnp.transpose(v[0].reshape(2, 8, -1)[:, :6], (0, 2, 1))
    grad_static = v[1].reshape(2, 8, 128)[:, :4, :6]
    keep, give = weight_part(
        ((ship, 4), (x_one, 0)), ship, 1, (0, 1, 1, 1), 256, "tail_weights", 4, (mix_low,)
    )
    keep, give = over_core(keep, swap(give, "core"))
    tail = keep + swap(give, "yh").astype(F32)
    streams_out = gathered_rows(pair, t, mix_keep)
    gt = exchange(gt, TP)
    grad_streams = gathered_rows(gt, t, streams_out)
    return (
        streams_out,
        grad_streams,
        tail[1],
        tail[2],
        tail[3],
        jnp.transpose(tail[0]),
        ff[0],
        ff[1],
        jnp.transpose(ff[2]),
        grad_dynamic,
        grad_static,
    )


def solution(mesh):
    fine = Mesh(mesh.devices.reshape(4, 2, 2, 2, 4), ("z", "yh", "core", "yl", "x"))
    placed = (
        P(DP, None, None),
        P(),
        P(None, TP),
        P(None, TP),
        P(None, TP),
        P(TP, None),
        P(None, TP),
        P(None, TP),
        P(TP, None),
        P(),
        P(),
        P(DP, None, None),
    )
    return jax.shard_map(
        per_device,
        mesh=fine,
        in_specs=placed,
        out_specs=(
            P(DP, None, None),
            P(DP, None, None),
            P(DP, TP),
            P(DP, TP),
            P(DP, TP),
            P(TP, DP),
            P(DP, TP),
            P(DP, TP),
            P(TP, DP),
            P(None, DP, None),
            P(),
        ),
        check_vma=False,
    )
```
